32 devices in a mesh: inp: 2 (over y), pa: 4 (over x, core), pb: 4 (over z).
Axes of the slice: x: 2, y: 2, z: 4, core: 2. Of those that a mesh axis runs over, the one named last changes fastest.
Arguments:
- log_inputs: float32 [2, 256, 256, 256], P('inp', 'pa', 'pb'), may hold values from -6 to 6
- warm_potential: float32 [2, 256, 256, 256], P('inp', 'pa', 'pb'), may hold values from -6 to 6
- bary_weights: float32 [2], P('inp'), may hold values from 0.1 to 0.5
- band_reach: int32 [3], replicated, may hold values from 0 to 2, each once
- bary_cotangent: float32 [256, 256, 256], P('pa', 'pb', 'inp'), may hold values from -6 to 6
Outputs:
- barycenter: float32 [256, 256, 256], P('pa', 'pb', 'inp')
- input_grad: float32 [2, 256, 256, 256], P('inp', 'pa', 'pb')
The draws below stay inside these ranges and needn't reach their ends.
Inputs may be any that keep to these rules, and one draw needn't show every extreme that they name: `band_reach`: a permutation of 0, 1 and 2, one entry a line direction.
All inputs are finite; a program needn't handle non-finite values.
Results may differ from the reference program's by a relative error of at most 0.00022.
Values sent between devices are 32-bit elements; how exact they have to be, the bound alone decides.
No kernel may reach another device: no remote copies, remote signals or barrier semaphores. Data moves between devices by JAX's collectives and lax.ppermute only.
A program may use at most 128 MiB of HBM per device.

```python
import math
import jax
import jax.numpy as jnp
from jax import lax

N = 256
K = 2


def block_scale(stream_key, shape, split, low, top_value):
    gain = 1.0
    for dim, blocks in split:
        steps = jax.random.uniform(jax.random.fold_in(jax.random.fold_in(stream_key, 6), dim), (blocks,), jnp.float32, low / len(split), top_value / len(split))
        gain = gain * jnp.repeat(jnp.exp(steps), shape[dim] // blocks).reshape((-1,) + (1,) * (len(shape) - 1 - dim))
    return gain


def centred(rng, dims, spread, bound, cuts=(), kind=jnp.bfloat16):
    gain = block_scale(rng, dims, cuts, -0.22, 0.18) if cuts else 1.0
    result = jax.random.normal(rng, dims, jnp.float32) * spread * gain
    return jnp.minimum(jnp.maximum(result, -bound), bound).astype(kind)


def setup_inputs(seed: int = 0) -> dict:
    splits = jax.random.split(jax.random.key(seed), 6)
    log_inputs = centred(splits[0], (K, N, N, N), 1.0, 6.0, ((0, 2), (1, 4), (2, 4)), jnp.float32)
    warm_potential = centred(splits[1], (K, N, N, N), 1.0, 6.0, ((0, 2), (1, 4), (2, 4)), jnp.float32)
    bary_weights = jnp.clip(jnp.exp(math.log(0.5) - 1.609438 * jax.random.uniform(splits[2], (K,), jnp.float32) ** block_scale(splits[2], (K,), ((0, 2),), -0.2, 0.2)), 0.1, 0.5)
    band_reach = jax.random.permutation(splits[3], 3).astype(jnp.int32)
    bary_cotangent = centred(splits[4], (N, N, N), 1.0, 6.0, ((0, 4), (1, 4), (2, 2)), jnp.float32)
    return dict(log_inputs=log_inputs, warm_potential=warm_potential, bary_weights=bary_weights, band_reach=band_reach, bary_cotangent=bary_cotangent)


FORMS = ('ij,jbc->ibc', 'ij,ajc->aic', 'ij,abj->abi')

def line_kernel(length, reach):
    index = jnp.arange(length, dtype=jnp.int32)
    block = 4
    sigma = 3.0
    offset = (index[:, None] - index[None, :]).astype(jnp.float32)
    inside = jnp.abs(index[:, None] // block - index[None, :] // block) <= reach
    gauss = jnp.exp(-offset * offset / (2.0 * sigma * sigma)) / (sigma * math.sqrt(2.0 * math.pi))
    return 0.5 * jnp.eye(length, dtype=jnp.float32) + 0.5 * jnp.where(inside, gauss, jnp.zeros_like(gauss))

def reference(log_inputs, warm_potential, bary_weights, band_reach, bary_cotangent):
    length = log_inputs.shape[1]
    kernels = [line_kernel(length, band_reach[line]) for line in range(3)]

    def convolve(field):
        for line in range(3):
            field = jnp.log(jnp.einsum(FORMS[line], kernels[line], jnp.exp(field), precision=lax.Precision.HIGHEST))
        return field

    def conv_all(fields):
        return lax.map(convolve, fields)

    def adjoint(pair):
        value, cotan = pair
        unused, pull = jax.vjp(convolve, value)
        return pull(cotan)[0]
    weights = bary_weights[:, None, None, None]
    dual_one = log_inputs - conv_all(warm_potential)
    part_one = warm_potential + conv_all(dual_one)
    barycenter = lax.optimization_barrier(jnp.sum(weights * part_one, axis=0))
    one_bar = weights * bary_cotangent[None]
    input_grad = lax.map(adjoint, (dual_one, one_bar))
    return (barycenter, input_grad)
```

```python
import functools
import math

import jax
import jax.numpy as jnp
from jax import lax
from jax.experimental import pallas as pl
from jax.experimental.pallas import tpu as pltpu
from jax.sharding import PartitionSpec as P

BLOCK = 4
SIGMA = 3.0
HALO = 2 * BLOCK
XOUT = 16
SUB = 8
F32 = jnp.float32
BF16 = jnp.bfloat16


def weight(i, j, reach):
    offset = (i - j).astype(F32)
    inside = jnp.abs(i // BLOCK - j // BLOCK) <= reach
    gauss = jnp.exp(-offset * offset / (2.0 * SIGMA * SIGMA)) / (SIGMA * math.sqrt(2.0 * math.pi))
    return jnp.where(i == j, 0.5, 0.0) + 0.5 * jnp.where(inside, gauss, 0.0)


def halves(value):
    high = value.astype(BF16)
    return high, (value - high.astype(F32)).astype(BF16)


def dot(a, b):
    return jnp.dot(a, b, preferred_element_type=F32)


def iotas(shape):
    return (lax.broadcasted_iota(jnp.int32, shape, 0), lax.broadcasted_iota(jnp.int32, shape, 1))


def fill_z(ref, reach):
    n = ref.shape[1]
    i, j = iotas((n, n))
    high, low = halves(weight(i, j, reach))
    ref[0:n] = high
    ref[n : 2 * n] = high
    ref[2 * n : 3 * n] = low


def fill_y(ref, reach):
    n = ref.shape[0]
    m = n + 2 * HALO
    i, c = iotas((n, 3 * m))
    part = jnp.where(c >= 2 * m, 2, jnp.where(c >= m, 1, 0))
    c = c - part * m
    j = jnp.where(c < n, c + HALO, jnp.where(c < n + HALO, c - n, c))
    value = weight(i + HALO, j, reach)
    high = value.astype(BF16).astype(F32)
    ref[...] = jnp.where(part == 2, value - high, high).astype(BF16)


def fill_x(ref, reach):
    m = (XOUT + 2 * HALO) * SUB
    r, c = iotas((XOUT * SUB, m))
    value = weight(r // SUB + HALO, c // SUB, reach)
    value = jnp.where(r % SUB == c % SUB, value, 0.0)
    high, low = halves(value)
    ref[:, 0:m] = high
    ref[:, m : 2 * m] = high
    ref[:, 2 * m : 3 * m] = low


def z_product(rows, kz):
    high, low = halves(rows)
    return dot(jnp.concatenate([high, low, high], axis=1), kz[...])


class Copies:
    def __init__(self, sems):
        self.sems = sems
        self.used = 0

    def start(self, src, dst):
        copy = pltpu.make_async_copy(src, dst, self.sems.at[self.used])
        self.used += 1
        copy.start()
        return copy


def strips_out(copies, buf, outs):
    nx, ny, _ = buf.shape
    xs = (pl.ds(0, HALO), pl.ds(nx - HALO, HALO))
    ys = (pl.ds(0, HALO), pl.ds(ny - HALO, HALO))
    started = []
    for n, x in enumerate(xs):
        started.append(copies.start(buf.at[x], outs[n]))
    for n, y in enumerate(ys):
        started.append(copies.start(buf.at[:, y], outs[2 + n]))
    for n, (x, y) in enumerate(((x, y) for x in xs for y in ys)):
        started.append(copies.start(buf.at[x, y], outs[4 + n]))
    return started


def strip_shapes(nx, ny, nz):
    shapes = [(HALO, ny, nz)] * 2 + [(nx, HALO, nz)] * 2 + [(HALO, HALO, nz)] * 4
    return [jax.ShapeDtypeStruct(s, F32) for s in shapes]


def first_kernel(reach, warm, u_out, *rest):
    outs, (buf, ubuf, kz, sems) = rest[:8], rest[8:]
    nx, ny, nz = buf.shape
    step = 8
    copies = Copies(sems)
    loads = [copies.start(warm.at[pl.ds(x, step)], buf.at[pl.ds(x, step)]) for x in range(0, nx, step)]
    fill_z(kz, reach[2])
    started = []
    for n, x in enumerate(range(0, nx, step)):
        loads[n].wait()
        rows = jnp.exp(buf[x : x + step].reshape(step * ny, nz))
        ubuf[x : x + step] = z_product(rows, kz).reshape(step, ny, nz)
        started.append(copies.start(ubuf.at[pl.ds(x, step)], u_out.at[pl.ds(x, step)]))
    started += strips_out(copies, ubuf, outs)
    for copy in started:
        copy.wait()


def load_halo(copies, u, halos, buf):
    nx, ny, _ = u.shape
    own_x, own_y = pl.ds(HALO, nx), pl.ds(0, ny)
    xs = (pl.ds(0, HALO), pl.ds(HALO + nx, HALO))
    ys = (pl.ds(ny, HALO), pl.ds(ny + HALO, HALO))
    loads = [copies.start(u, buf.at[own_x, own_y])]
    for n, x in enumerate(xs):
        loads.append(copies.start(halos[n], buf.at[x, own_y]))
    for n, y in enumerate(ys):
        loads.append(copies.start(halos[2 + n], buf.at[own_x, y]))
    for n, (x, y) in enumerate(((x, y) for x in xs for y in ys)):
        loads.append(copies.start(halos[4 + n], buf.at[x, y]))
    return loads


def y_products(buf, vbuf, ky):
    unroll = 4

    def body(step, carry):
        for n in range(unroll):
            x = step * unroll + n
            high, low = halves(buf[x])
            vbuf[x] = dot(ky[...], jnp.concatenate([high, low, high], axis=0))
        return carry

    lax.fori_loop(0, buf.shape[0] // unroll, body, 0)


def x_products(vbuf, kx, tile, store):
    nz = vbuf.shape[2]
    span = XOUT + 2 * HALO
    for x in range(0, vbuf.shape[0] - 2 * HALO, XOUT):
        window = vbuf[x : x + span, pl.ds(tile * SUB, SUB), :].reshape(span * SUB, nz)
        high, low = halves(window)
        store(x, dot(kx[...], jnp.concatenate([high, low, high], axis=0)))


def second_kernel(reach, u, *rest):
    halos, (log_in, d_out, u_out), outs = rest[:8], rest[8:11], rest[11:19]
    buf, vbuf, lbuf, dbuf, ubuf, kx, ky, kz, sems = rest[19:]
    nx, ny, nz = ubuf.shape
    copies = Copies(sems)
    loads = load_halo(copies, u, halos, buf)
    late = copies.start(log_in, lbuf)
    fill_x(kx, reach[0])
    fill_y(ky, reach[1])
    fill_z(kz, reach[2])
    for copy in loads:
        copy.wait()
    y_products(buf, vbuf, ky)
    late.wait()

    def body(tile, carry):
        rows = pl.ds(pl.multiple_of(tile * SUB, SUB), SUB)

        def store(x, product):
            value = jnp.exp(lbuf[x : x + XOUT, rows, :].reshape(XOUT * SUB, nz)) / product
            dbuf[x : x + XOUT, rows, :] = value.reshape(XOUT, SUB, nz)

        x_products(vbuf, kx, tile, store)
        d = dbuf[:, rows, :].reshape(nx * SUB, nz)
        ubuf[:, rows, :] = z_product(d, kz).reshape(nx, SUB, nz)
        return carry

    lax.fori_loop(0, ny // SUB, body, 0)
    started = strips_out(copies, ubuf, outs)
    started.append(copies.start(ubuf, u_out))
    started.append(copies.start(dbuf, d_out))
    for copy in started:
        copy.wait()


def third_kernel(reach, side, weights, u, *rest):
    halos, (warm, own_cot, far_cot, keep_out, send_out, u_out), outs = rest[:8], rest[8:14], rest[14:22]
    buf, vbuf, wbuf, cbuf, fbuf, kbuf, sbuf, qbuf, ubuf, kx, ky, kz, sems = rest[22:]
    nx, ny, nz = ubuf.shape
    half = nz // 2
    copies = Copies(sems)
    loads = load_halo(copies, u, halos, buf)
    late = [copies.start(warm, wbuf), copies.start(own_cot, cbuf), copies.start(far_cot, fbuf)]
    fill_x(kx, reach[0])
    fill_y(ky, reach[1])
    fill_z(kz, reach[2])
    for copy in loads:
        copy.wait()
    y_products(buf, vbuf, ky)
    for copy in late:
        copy.wait()
    first = side[0] == 0
    scale = weights[0]

    def body(tile, carry):
        rows = pl.ds(pl.multiple_of(tile * SUB, SUB), SUB)

        def store(x, product):
            planes = slice(x, x + XOUT)
            part = scale * (wbuf[planes, rows, :].reshape(XOUT * SUB, nz) + jnp.log(product))
            left, right = part[:, :half], part[:, half:]
            kbuf[planes, rows, :] = jnp.where(first, left, right).reshape(XOUT, SUB, half)
            sbuf[planes, rows, :] = jnp.where(first, right, left).reshape(XOUT, SUB, half)
            own = cbuf[planes, rows, :].reshape(XOUT * SUB, half)
            far = fbuf[planes, rows, :].reshape(XOUT * SUB, half)
            cot = jnp.concatenate([jnp.where(first, own, far), jnp.where(first, far, own)], axis=1)
            qbuf[planes, rows, :] = (scale * cot / product).reshape(XOUT, SUB, nz)

        x_products(vbuf, kx, tile, store)
        q = qbuf[:, rows, :].reshape(nx * SUB, nz)
        ubuf[:, rows, :] = z_product(q, kz).reshape(nx, SUB, nz)
        return carry

    lax.fori_loop(0, ny // SUB, body, 0)
    started = [copies.start(sbuf, send_out)]
    started += strips_out(copies, ubuf, outs)
    started.append(copies.start(ubuf, u_out))
    started.append(copies.start(kbuf, keep_out))
    for copy in started:
        copy.wait()


def last_kernel(reach, u, *rest):
    halos, (d, g_out) = rest[:8], rest[8:10]
    buf, vbuf, dbuf, gbuf, kx, ky, sems = rest[10:]
    nx, ny, nz = gbuf.shape
    copies = Copies(sems)
    loads = load_halo(copies, u, halos, buf)
    late = copies.start(d, dbuf)
    fill_x(kx, reach[0])
    fill_y(ky, reach[1])
    for copy in loads:
        copy.wait()
    y_products(buf, vbuf, ky)
    late.wait()

    def body(tile, carry):
        rows = pl.ds(pl.multiple_of(tile * SUB, SUB), SUB)

        def store(x, product):
            planes = slice(x, x + XOUT)
            gbuf[planes, rows, :] = dbuf[planes, rows, :] * product.reshape(XOUT, SUB, nz)

        x_products(vbuf, kx, tile, store)
        return carry

    lax.fori_loop(0, ny // SUB, body, 0)
    copies.start(gbuf, g_out).wait()


def add_kernel(a, b, out):
    out[...] = a[...] + b[...]


SMEM = pl.BlockSpec(memory_space=pltpu.SMEM)
ANY = pl.BlockSpec(memory_space=pl.ANY)


def call(kernel, name, scalars, arrays, out_shape, scratch, copies, flops):
    moved = sum(math.prod(a.shape) * 4 for a in list(arrays) + list(out_shape))
    return pl.pallas_call(
        kernel,
        name=name,
        out_shape=out_shape,
        in_specs=[SMEM] * len(scalars) + [ANY] * len(arrays),
        out_specs=[ANY] * len(out_shape),
        scratch_shapes=scratch + [pltpu.SemaphoreType.DMA((copies,))],
        compiler_params=pltpu.CompilerParams(vmem_limit_bytes=52 * 2**20),
        cost_estimate=pl.CostEstimate(flops=flops, bytes_accessed=moved, transcendentals=0),
    )(*scalars, *arrays)


def shift(value, sizes, dx, dy):
    na, nb = sizes
    perm = []
    for a in range(na):
        for b in range(nb):
            if 0 <= a + dx < na and 0 <= b + dy < nb:
                perm.append((a * nb + b, (a + dx) * nb + b + dy))
    return lax.ppermute(value, ("pa", "pb"), perm)


def exchange(strips, sizes):
    x0, x1, y0, y1, c00, c01, c10, c11 = strips
    return [
        shift(x1, sizes, 1, 0),
        shift(x0, sizes, -1, 0),
        shift(y1, sizes, 0, 1),
        shift(y0, sizes, 0, -1),
        shift(c11, sizes, 1, 1),
        shift(c10, sizes, 1, -1),
        shift(c01, sizes, -1, 1),
        shift(c00, sizes, -1, -1),
    ]


def per_device(sizes, log_inputs, warm_potential, bary_weights, band_reach, bary_cotangent):
    _, nx, ny, nz = log_inputs.shape
    half = nz // 2
    log_inputs = log_inputs.reshape(nx, ny, nz)
    warm = warm_potential.reshape(nx, ny, nz)
    side = lax.axis_index("inp").astype(jnp.int32).reshape(1)
    swap = [(0, 1), (1, 0)]

    own = (nx, ny, nz)
    wide = (nx + 2 * HALO, ny + 2 * HALO, nz)
    tall = (nx + 2 * HALO, ny, nz)
    half_shape = (nx, ny, half)
    full = jax.ShapeDtypeStruct(own, F32)
    part = jax.ShapeDtypeStruct(half_shape, F32)
    strips_like = strip_shapes(nx, ny, nz)
    vmem = lambda shape: pltpu.VMEM(shape, F32)
    span = (XOUT + 2 * HALO) * SUB
    kx = pltpu.VMEM((XOUT * SUB, 3 * span), BF16)
    ky = pltpu.VMEM((ny, 3 * (ny + 2 * HALO)), BF16)
    kz = pltpu.VMEM((3 * nz, nz), BF16)
    lines = nx * ny * nz
    z_flops = 2 * 3 * lines * nz
    xy_flops = 2 * 3 * lines * (ny + span)

    far_cot = lax.ppermute(bary_cotangent, "inp", swap)
    u, *strips = call(
        first_kernel, "z_lines", (band_reach,), (warm,), [full] + strips_like,
        [vmem(own), vmem(own), kz], 2 * (nx // 8) + 8, z_flops,
    )
    halos = exchange(strips, sizes)
    d, u, *strips = call(
        second_kernel, "dual", (band_reach,), (u, *halos, log_inputs), [full, full] + strips_like,
        [vmem(wide), vmem(tall), vmem(own), vmem(own), vmem(own), kx, ky, kz], 20, z_flops + xy_flops,
    )
    halos = exchange(strips, sizes)
    keep, send, u, *strips = call(
        third_kernel, "partial", (band_reach, side, bary_weights), (u, *halos, warm, bary_cotangent, far_cot),
        [part, part, full] + strips_like,
        [vmem(wide), vmem(tall), vmem(own)] + [vmem(half_shape)] * 4 + [vmem(own), vmem(own), kx, ky, kz],
        23, z_flops + xy_flops,
    )
    arrived = lax.ppermute(send, "inp", swap)
    halos = exchange(strips, sizes)
    (grad,) = call(
        last_kernel, "gradient", (band_reach,), (u, *halos, d), [full],
        [vmem(wide), vmem(tall), vmem(own), vmem(own), kx, ky], 11, xy_flops,
    )
    step = 8
    block = pl.BlockSpec((step, ny, half), lambda n: (n, 0, 0))
    barycenter = pl.pallas_call(
        add_kernel, name="barycenter", out_shape=part, grid=(nx // step,),
        in_specs=[block, block], out_specs=block,
        cost_estimate=pl.CostEstimate(flops=lines // 2, bytes_accessed=6 * lines, transcendentals=0),
    )(keep, arrived)
    return (barycenter, grad.reshape(1, nx, ny, nz))


def solution(mesh):
    sizes = (mesh.shape["pa"], mesh.shape["pb"])
    return jax.shard_map(
        functools.partial(per_device, sizes),
        mesh=mesh,
        in_specs=(
            P("inp", "pa", "pb", None),
            P("inp", "pa", "pb", None),
            P("inp"),
            P(),
            P("pa", "pb", "inp"),
        ),
        out_specs=(P("pa", "pb", "inp"), P("inp", "pa", "pb", None)),
        check_vma=False,
    )
```

```python
import functools
import math

import jax
import jax.numpy as jnp
from jax import lax
from jax.experimental import pallas as pl
from jax.experimental.pallas import tpu as pltpu
from jax.sharding import PartitionSpec as P

BLOCK = 4
SIGMA = 3.0
SUB = 8
GROUP = 8
F32 = jnp.float32
BF16 = jnp.bfloat16


def tap(offset):
    gauss = math.exp(-offset * offset / (2.0 * SIGMA * SIGMA)) / (SIGMA * math.sqrt(2.0 * math.pi))
    return 0.5 * gauss + (0.5 if offset == 0 else 0.0)


def weight(i, j, reach):
    offset = (i - j).astype(F32)
    inside = jnp.abs(i // BLOCK - j // BLOCK) <= reach
    gauss = jnp.exp(-offset * offset / (2.0 * SIGMA * SIGMA)) / (SIGMA * math.sqrt(2.0 * math.pi))
    return jnp.where(i == j, 0.5, 0.0) + 0.5 * jnp.where(inside, gauss, 0.0)


def halves(value):
    high = value.astype(BF16)
    return high, (value - high.astype(F32)).astype(BF16)


def dot(a, b):
    return jnp.dot(a, b, preferred_element_type=F32)


def iotas(shape):
    return (lax.broadcasted_iota(jnp.int32, shape, 0), lax.broadcasted_iota(jnp.int32, shape, 1))


def fill_z(ref, reach):
    n = ref.shape[1]
    i, j = iotas((n, n))
    high, low = halves(weight(i, j, reach))
    ref[0:n] = high
    ref[n : 2 * n] = high
    ref[2 * n : 3 * n] = low


def z_product(rows, kz):
    high, low = halves(rows)
    return dot(jnp.concatenate([high, low, high], axis=1), kz[...])


def y_depth(ny, halo):
    return 3 * ny + (6 * halo + 15) // 16 * 16


def fill_y(ref, reach, halo):
    ny, depth = ref.shape
    i, c = iotas((ny, depth))
    own = c < 3 * ny
    part = c // ny
    j = c - part * ny
    if halo:
        c = c - 3 * ny
        side = c // (2 * halo)
        e = c - side * 2 * halo - halo
        part = jnp.where(own, part, side)
        j = jnp.where(own, j, jnp.where(e < 0, e, e + ny))
    shift = 2 * BLOCK
    value = weight(i + shift, j + shift, reach)
    high = value.astype(BF16).astype(F32)
    value = jnp.where(part == 2, value - high, jnp.where(part < 2, high, 0.0))
    ref[...] = value.astype(BF16)


def y_product(ky, own, halo=None):
    high, low = halves(own)
    pieces = [high, low, high]
    if halo is not None:
        high = halo.astype(BF16).astype(F32)
        low = halo - high
        pad = -3 * halo.shape[0] % 16
        rows = [high, low, high] + ([jnp.zeros((pad, halo.shape[1]), F32)] if pad else [])
        pieces.append(jnp.concatenate(rows, axis=0).astype(BF16))
    return dot(ky[...], jnp.concatenate(pieces, axis=0))


def pack(even, odd, top):
    row = lax.broadcasted_iota(jnp.int32, even.shape, 0)
    if top:
        return jnp.where(row < 4, even, pltpu.roll(odd, 4, 0))
    return jnp.where(row < 4, pltpu.roll(even, 4, 0), odd)


def x_sum(plane, n, reach):
    phase = n % BLOCK
    span = BLOCK * reach
    total = tap(0) * plane(n)
    for d in range(1, span + 1):
        total = total + tap(d) * (plane(n - d) + plane(n + d))
    for d in range(span + 1, span + phase + 1):
        total = total + tap(d) * plane(n - d)
    for d in range(span + 1, span + BLOCK - phase):
        total = total + tap(d) * plane(n + d)
    return total


class Stage:
    def __init__(self, shape, reaches, kind, finish=None, start=(), send=None):
        self.shape = shape
        self.reaches = reaches
        self.kind = kind
        self.finish = finish
        self.start = start
        self.send = send

    def halo(self, line):
        return BLOCK * self.reaches[line]

    def strip_shape(self, line):
        nx, ny, nz = self.shape
        halo = self.halo(line)
        if line == 0:
            return (halo, ny, nz)
        return (nx * halo // SUB, SUB, nz)

    def scratch(self):
        nx, ny, nz = self.shape
        items = {"work": pltpu.VMEM((GROUP, ny, nz), F32)}
        if 2 in self.start:
            items["kz"] = pltpu.VMEM((3 * nz, nz), BF16)
        if self.finish == 1:
            items["ky"] = pltpu.VMEM((ny, y_depth(ny, self.halo(1))), BF16)
        if 1 in self.start:
            items["ky0"] = pltpu.VMEM((ny, y_depth(ny, 0)), BF16)
        if self.kind in ("exp", "grad"):
            items["sems"] = pltpu.SemaphoreType.DMA((nx // GROUP,))
        if self.kind == "grad":
            items["gbuf"] = pltpu.VMEM(self.shape, F32)
        return items

    def step(self, r, x, rows, product):
        kind = self.kind
        at = (x, rows)
        if kind == "exp":
            return jnp.exp(r["warm"][at])
        if kind == "none":
            return product
        if kind == "dual":
            value = jnp.exp(r["log_in"][at]) / product
            r["d"][at] = value
            return value
        if kind == "grad":
            r["gbuf"][at] = r["d"][at] * product
            return None
        scale = r["weights"][0]
        first = r["side"][0] == 0
        half = self.shape[2] // 2
        if kind == "part":
            part = scale * (r["warm"][at] + jnp.log(product))
            left, right = part[:, :half], part[:, half:]
            r["t"][at] = product
            r["keep"][at] = jnp.where(first, left, right)
            r["send"][at] = jnp.where(first, right, left)
            return None
        own, far = r["cot"][at], r["far"][at]
        cot = jnp.concatenate([jnp.where(first, own, far), jnp.where(first, far, own)], axis=1)
        return scale * cot / r["t"][at]

    def plane(self, r, x0, first, last, rows):
        halo = self.halo(0)

        def get(n):
            if n < 0 and first:
                return r["low"][halo + n, rows]
            if n >= GROUP and last:
                return r["high"][n - GROUP, rows]
            return r["u"][x0 + n, rows]

        return get

    def y_halo(self, r, x0, n):
        if self.halo(1) == SUB:
            return jnp.concatenate([r["low"][x0 + n], r["high"][x0 + n]], axis=0)
        pair = x0 // 2 + n // 2
        low, high = r["low"][pair], r["high"][pair]
        row = lax.broadcasted_iota(jnp.int32, low.shape, 0)
        if n % 2 == 0:
            return jnp.where(row < 4, low, pltpu.roll(high, 4, 0))
        return jnp.where(row < 4, pltpu.roll(low, 4, 0), high)

    def group(self, r, x0, first, last):
        nx, ny, nz = self.shape
        work = r["work"]
        keeps = bool(self.start) or self.send is not None
        out = r.get("u_out")

        def put(n, rows, value):
            if value is not None:
                if self.start:
                    work[n, rows] = value
                else:
                    out[x0 + n, rows] = value

        everything = pl.ds(0, ny)
        if self.finish == 0:

            def tile_body(tile, carry):
                rows = pl.ds(pl.multiple_of(tile * SUB, SUB), SUB)
                get = self.plane(r, x0, first, last, rows)
                for n in range(GROUP):
                    put(n, rows, self.step(r, x0 + n, rows, x_sum(get, n, self.reaches[0])))
                return carry

            lax.fori_loop(0, ny // SUB, tile_body, 0)
        else:
            for n in range(GROUP):
                product = None
                if self.finish == 1:
                    product = y_product(r["ky"], r["u"][x0 + n], self.y_halo(r, x0, n))
                put(n, everything, self.step(r, x0 + n, everything, product))
        if not keeps:
            return
        if 0 in self.start:

            def quad_body(tile, carry):
                rows = pl.ds(pl.multiple_of(tile * SUB, SUB), SUB)
                planes = [work[n, rows] for n in range(GROUP)]
                for n in range(GROUP):
                    work[n, rows] = x_sum(lambda m: planes[m], n, 0)
                return carry

            lax.fori_loop(0, ny // SUB, quad_body, 0)
        if 1 in self.start:
            for n in range(GROUP):
                work[n] = y_product(r["ky0"], work[n])
        if 2 in self.start:
            product = z_product(work[...].reshape(GROUP * ny, nz), r["kz"])
            out[pl.ds(x0, GROUP)] = product.reshape(GROUP, ny, nz)
        if self.send == 0:
            halo = self.halo(0)
            if first:
                r["low_out"][...] = out[0:halo]
            if last:
                r["high_out"][...] = out[nx - halo : nx]
        if self.send == 1:
            top, bottom = pl.ds(0, SUB), pl.ds(ny - SUB, SUB)
            if self.halo(1) == SUB:
                r["low_out"][pl.ds(x0, GROUP)] = out[pl.ds(x0, GROUP), top]
                r["high_out"][pl.ds(x0, GROUP)] = out[pl.ds(x0, GROUP), bottom]
            else:
                for n in range(0, GROUP, 2):
                    pair = x0 // 2 + n // 2
                    r["low_out"][pair] = pack(out[x0 + n, top], out[x0 + n + 1, top], True)
                    r["high_out"][pair] = pack(out[x0 + n, bottom], out[x0 + n + 1, bottom], False)

    def body(self, r):
        nx, ny, nz = self.shape
        groups = nx // GROUP
        planes = lambda g: pl.ds(g * GROUP, GROUP)
        if self.kind == "exp":
            load = lambda g: pltpu.make_async_copy(
                r["warm_in"].at[planes(g)], r["warm"].at[planes(g)], r["sems"].at[g]
            )
            for g in range(groups):
                load(g).start()
        if self.kind == "grad":
            save = lambda g: pltpu.make_async_copy(
                r["gbuf"].at[planes(g)], r["grad"].at[planes(g)], r["sems"].at[g]
            )
        if "kz" in r:
            fill_z(r["kz"], self.reaches[2])
        if "ky" in r:
            fill_y(r["ky"], self.reaches[1], self.halo(1))
        if "ky0" in r:
            fill_y(r["ky0"], 0, 0)

        def run(g, first, last):
            if self.kind == "exp":
                load(g).wait()
            x0 = g * GROUP if isinstance(g, int) else pl.multiple_of(g * GROUP, GROUP)
            self.group(r, x0, first, last)
            if self.kind == "grad":
                save(g).start()

        run(0, True, groups == 1)
        if groups > 2:
            lax.fori_loop(1, groups - 1, lambda g, c: (run(g, False, False), c)[1], 0)
        if groups > 1:
            run(groups - 1, False, True)
        if self.kind == "grad":
            for g in range(groups):
                save(g).wait()

    def __call__(self, name, **arrays):
        nx, ny, nz = self.shape
        half = (nx, ny, nz // 2)
        outs = {}
        if self.kind == "exp":
            outs["warm"] = self.shape
        if self.kind == "dual":
            outs["d"] = self.shape
        if self.kind == "part":
            outs.update(send=half, keep=half, t=self.shape)
        if self.kind == "grad":
            outs["grad"] = self.shape
        if self.start or self.send is not None:
            outs["u_out"] = self.shape
        if self.send is not None:
            outs["low_out"] = outs["high_out"] = self.strip_shape(self.send)
        scratch = self.scratch()
        names = list(arrays) + list(outs) + list(scratch)
        operands, in_specs = [], []
        for key, value in arrays.items():
            if key in ("weights", "side"):
                in_specs.append(pl.BlockSpec(memory_space=pltpu.SMEM))
            elif key == "warm_in":
                in_specs.append(pl.BlockSpec(memory_space=pl.ANY))
            else:
                value = pltpu.with_memory_space_constraint(value, pltpu.VMEM)
                in_specs.append(pl.BlockSpec(memory_space=pltpu.VMEM))
            operands.append(value)
        out_shape, out_specs = [], []
        for key, shape in outs.items():
            if key == "grad":
                out_shape.append(jax.ShapeDtypeStruct(shape, F32))
                out_specs.append(pl.BlockSpec(memory_space=pl.ANY))
            else:
                out_shape.append(pltpu.VMEM(shape, F32))
                out_specs.append(pl.BlockSpec(memory_space=pltpu.VMEM))
        lines = nx * ny * nz
        result = pl.pallas_call(
            lambda *refs: self.body(dict(zip(names, refs))),
            name=name,
            out_shape=out_shape,
            in_specs=in_specs,
            out_specs=out_specs,
            scratch_shapes=list(scratch.values()),
            compiler_params=pltpu.CompilerParams(vmem_limit_bytes=14 * 2**20),
            cost_estimate=pl.CostEstimate(flops=6 * lines * nz, bytes_accessed=16 * lines, transcendentals=0),
        )(*operands)
        return dict(zip(outs, result))


def add_body(keep, arrived, out, total, sems):
    parts = sems.shape[0]
    step = total.shape[0] // parts
    copies = []
    for n in range(parts):
        planes = pl.ds(n * step, step)
        total[planes] = keep[planes] + arrived[planes]
        copies.append(pltpu.make_async_copy(total.at[planes], out.at[planes], sems.at[n]))
        copies[-1].start()
    for copy in copies:
        copy.wait()


def add(keep, arrived):
    in_vmem = [pltpu.with_memory_space_constraint(v, pltpu.VMEM) for v in (keep, arrived)]
    return pl.pallas_call(
        add_body,
        name="barycenter",
        out_shape=jax.ShapeDtypeStruct(keep.shape, F32),
        in_specs=[pl.BlockSpec(memory_space=pltpu.VMEM)] * 2,
        out_specs=pl.BlockSpec(memory_space=pl.ANY),
        scratch_shapes=[pltpu.VMEM(keep.shape, F32), pltpu.SemaphoreType.DMA((4,))],
        compiler_params=pltpu.CompilerParams(vmem_limit_bytes=14 * 2**20),
        cost_estimate=pl.CostEstimate(flops=keep.size, bytes_accessed=12 * keep.size, transcendentals=0),
    )(*in_vmem)


AXES = ("pa", "pb")


def exchange(sizes, line, made):
    n = sizes[line]
    up = [(i, i + 1) for i in range(n - 1)]
    down = [(i + 1, i) for i in range(n - 1)]
    low = lax.ppermute(made["high_out"], AXES[line], up)
    high = lax.ppermute(made["low_out"], AXES[line], down)
    return dict(u=made["u_out"], low=low, high=high)


SWAP = [(0, 1), (1, 0)]


def case(sizes, reaches, log_in, warm_in, weights, cotangent):
    shape = log_in.shape
    side = lax.axis_index("inp").astype(jnp.int32).reshape(1)
    far = lax.ppermute(cotangent, "inp", SWAP)
    stage = functools.partial(Stage, shape, reaches)
    if reaches[2] == 0:
        first, last, begin = 0, 1, (2,)
    elif reaches[0] == 0:
        first, last, begin = 1, 1, (0, 2)
    else:
        first, last, begin = 0, 0, (1, 2)

    def halos(made, name):
        arrays = exchange(sizes, first, made)
        if first != last:
            made = stage("none", finish=first, send=last)(name, **arrays)
            arrays = exchange(sizes, last, made)
        return arrays

    made = stage("exp", start=begin, send=first)("scaling", warm_in=warm_in)
    warm = made["warm"]
    arrays = halos(made, "lines_one")
    made = stage("dual", finish=last, start=begin, send=first)("dual", log_in=log_in, **arrays)
    d = made["d"]
    arrays = halos(made, "lines_two")
    part = stage("part", finish=last)("partial", weights=weights, side=side, warm=warm, **arrays)
    arrived = lax.ppermute(part["send"], "inp", SWAP)
    made = stage("cot", start=begin, send=first)(
        "cotangent", weights=weights, side=side, cot=cotangent, far=far, t=part["t"]
    )
    arrays = halos(made, "lines_three")
    grad = stage("grad", finish=last)("gradient", d=d, **arrays)["grad"]
    return add(part["keep"], arrived), grad


ORDERS = ((0, 1, 2), (0, 2, 1), (1, 0, 2), (1, 2, 0), (2, 0, 1), (2, 1, 0))


def per_device(sizes, log_inputs, warm_potential, bary_weights, band_reach, bary_cotangent):
    shape = log_inputs.shape[1:]
    index = 2 * band_reach[0] + (band_reach[1] > band_reach[2]).astype(jnp.int32)
    branches = [functools.partial(case, sizes, reaches) for reaches in ORDERS]
    barycenter, grad = lax.switch(
        index, branches, log_inputs.reshape(shape), warm_potential.reshape(shape), bary_weights, bary_cotangent
    )
    return (barycenter, grad[None])


def solution(mesh):
    sizes = (mesh.shape["pa"], mesh.shape["pb"])
    return jax.shard_map(
        functools.partial(per_device, sizes),
        mesh=mesh,
        in_specs=(
            P("inp", "pa", "pb", None),
            P("inp", "pa", "pb", None),
            P("inp"),
            P(),
            P("pa", "pb", "inp"),
        ),
        out_specs=(P("pa", "pb", "inp"), P("inp", "pa", "pb", None)),
        check_vma=False,
    )
```

```python
import functools
import math

import jax
import jax.numpy as jnp
from jax import lax
from jax.experimental import pallas as pl
from jax.experimental.pallas import tpu as pltpu
from jax.sharding import PartitionSpec as P

BLOCK = 4
SIGMA = 3.0
SUB = 8
GROUP = 8
F32 = jnp.float32
BF16 = jnp.bfloat16


def tap(offset):
    gauss = math.exp(-offset * offset / (2.0 * SIGMA * SIGMA)) / (SIGMA * math.sqrt(2.0 * math.pi))
    return 0.5 * gauss + (0.5 if offset == 0 else 0.0)


def weight(i, j, reach):
    offset = (i - j).astype(F32)
    inside = jnp.abs(i // BLOCK - j // BLOCK) <= reach
    gauss = jnp.exp(-offset * offset / (2.0 * SIGMA * SIGMA)) / (SIGMA * math.sqrt(2.0 * math.pi))
    return jnp.where(i == j, 0.5, 0.0) + 0.5 * jnp.where(inside, gauss, 0.0)


def halves(value):
    high = value.astype(BF16)
    return high, (value - high.astype(F32)).astype(BF16)


def dot(a, b):
    return jnp.dot(a, b, preferred_element_type=F32)


def iotas(shape):
    return (lax.broadcasted_iota(jnp.int32, shape, 0), lax.broadcasted_iota(jnp.int32, shape, 1))


def fill_z(ref, reach):
    n = ref.shape[1]
    i, j = iotas((n, n))
    high, low = halves(weight(i, j, reach))
    ref[0:n] = high
    ref[n : 2 * n] = high
    ref[2 * n : 3 * n] = low


def z_product(rows, kz):
    high, low = halves(rows)
    return dot(jnp.concatenate([high, low, high], axis=1), kz[...])


def y_depth(ny, halo):
    return 3 * ny + (6 * halo + 15) // 16 * 16


def fill_y(ref, reach, halo):
    ny, depth = ref.shape
    i, c = iotas((ny, depth))
    own = c < 3 * ny
    part = c // ny
    j = c - part * ny
    if halo:
        c = c - 3 * ny
        side = c // (2 * halo)
        e = c - side * 2 * halo - halo
        part = jnp.where(own, part, side)
        j = jnp.where(own, j, jnp.where(e < 0, e, e + ny))
    shift = 2 * BLOCK
    value = weight(i + shift, j + shift, reach)
    high = value.astype(BF16).astype(F32)
    value = jnp.where(part == 2, value - high, jnp.where(part < 2, high, 0.0))
    ref[...] = value.astype(BF16)


def y_product(ky, own, halo=None):
    high, low = halves(own)
    pieces = [high, low, high]
    if halo is not None:
        high = halo.astype(BF16).astype(F32)
        low = halo - high
        pad = -3 * halo.shape[0] % 16
        rows = [high, low, high] + ([jnp.zeros((pad, halo.shape[1]), F32)] if pad else [])
        pieces.append(jnp.concatenate(rows, axis=0).astype(BF16))
    return dot(ky[...], jnp.concatenate(pieces, axis=0))


def pack(even, odd, top):
    row = lax.broadcasted_iota(jnp.int32, even.shape, 0)
    if top:
        return jnp.where(row < 4, even, pltpu.roll(odd, 4, 0))
    return jnp.where(row < 4, pltpu.roll(even, 4, 0), odd)


def x_sum(plane, n, reach):
    phase = n % BLOCK
    span = BLOCK * reach
    total = tap(0) * plane(n)
    for d in range(1, span + 1):
        total = total + tap(d) * (plane(n - d) + plane(n + d))
    for d in range(span + 1, span + phase + 1):
        total = total + tap(d) * plane(n - d)
    for d in range(span + 1, span + BLOCK - phase):
        total = total + tap(d) * plane(n + d)
    return total


READS = {"exp": ("warm",), "dual": ("log_in",), "part": ("warm",), "cot": ("cot", "far")}


COST = pl.CostEstimate(flops=1, bytes_accessed=1, transcendentals=0)


class Stage:
    def __init__(self, shape, reaches, kind, finish=None, start=(), send=None):
        self.shape = shape
        self.reaches = reaches
        self.kind = kind
        self.finish = finish
        self.start = start
        self.send = send

    def halo(self, line):
        return BLOCK * self.reaches[line]

    def strip_shape(self, line):
        nx, ny, nz = self.shape
        halo = self.halo(line)
        if line == 0:
            return (halo, ny, nz)
        return (nx * halo // SUB, SUB, nz)

    def scratch(self):
        nx, ny, nz = self.shape
        items = {"work": pltpu.VMEM((GROUP, ny, nz), F32)}
        if 2 in self.start:
            items["kz"] = pltpu.VMEM((3 * nz, nz), BF16)
        if self.finish == 1:
            items["ky"] = pltpu.VMEM((ny, y_depth(ny, self.halo(1))), BF16)
        if 1 in self.start:
            items["ky0"] = pltpu.VMEM((ny, y_depth(ny, 0)), BF16)
        if self.kind == "grad":
            items["gbuf"] = pltpu.VMEM((2, GROUP, ny, nz), F32)
            items["sems"] = pltpu.SemaphoreType.DMA((2,))
        for key in READS.get(self.kind, ()):
            width = nz // 2 if key in ("cot", "far") else nz
            items[key] = pltpu.VMEM((nx, ny, width), F32)
        if self.kind in READS:
            items["sems"] = pltpu.SemaphoreType.DMA((len(READS[self.kind]), nx // GROUP))
        return items

    def step(self, r, x, n, rows, product):
        kind = self.kind
        at = (x, rows)
        if kind == "exp":
            return jnp.exp(r["warm"][at])
        if kind == "none":
            return product
        if kind == "dual":
            value = jnp.exp(r["log_in"][at]) / product
            r["d"][at] = value
            return value
        if kind == "grad":
            r["gbuf"][r["slot"], n, rows] = r["d"][at] * product
            return None
        scale = r["weights"][0]
        first = r["side"][0] == 0
        half = self.shape[2] // 2
        if kind == "part":
            part = scale * (r["warm"][at] + jnp.log(product))
            left, right = part[:, :half], part[:, half:]
            r["t"][at] = product
            r["keep"][at] = jnp.where(first, left, right)
            r["send"][at] = jnp.where(first, right, left)
            return None
        own, far = r["cot"][at], r["far"][at]
        cot = jnp.concatenate([jnp.where(first, own, far), jnp.where(first, far, own)], axis=1)
        return scale * cot / r["t"][at]

    def plane(self, r, x0, first, last, rows):
        halo = self.halo(0)

        def get(n):
            if n < 0 and first:
                return r["low"][halo + n, rows]
            if n >= GROUP and last:
                return r["high"][n - GROUP, rows]
            return r["u"][x0 + n, rows]

        return get

    def y_halo(self, r, x0, n):
        if self.halo(1) == SUB:
            return jnp.concatenate([r["low"][x0 + n], r["high"][x0 + n]], axis=0)
        pair = x0 // 2 + n // 2
        low, high = r["low"][pair], r["high"][pair]
        row = lax.broadcasted_iota(jnp.int32, low.shape, 0)
        if n % 2 == 0:
            return jnp.where(row < 4, low, pltpu.roll(high, 4, 0))
        return jnp.where(row < 4, pltpu.roll(low, 4, 0), high)

    def tiles(self, body):
        def tile_body(tile, carry):
            body(pl.ds(pl.multiple_of(tile * SUB, SUB), SUB))
            return carry

        lax.fori_loop(0, self.shape[1] // SUB, tile_body, 0)

    def finish_x(self, r, x0, first, last):
        def body(rows):
            get = self.plane(r, x0, first, last, rows)
            for n in range(GROUP):
                value = self.step(r, x0 + n, n, rows, x_sum(get, n, self.reaches[0]))
                if value is not None:
                    if self.start:
                        r["work"][n, rows] = value
                    else:
                        r["u_out"][x0 + n, rows] = value

        self.tiles(body)

    def group(self, r, g):
        nx, ny, nz = self.shape
        groups = nx // GROUP
        work, out = r["work"], r.get("u_out")
        x0 = pl.multiple_of(g * GROUP, GROUP)
        everything = pl.ds(0, ny)
        if self.finish == 0:
            pl.when(g == 0)(lambda: self.finish_x(r, x0, True, groups == 1))
            if groups > 2:
                pl.when((g > 0) & (g < groups - 1))(lambda: self.finish_x(r, x0, False, False))
            if groups > 1:
                pl.when(g == groups - 1)(lambda: self.finish_x(r, x0, False, True))
            if 1 in self.start:
                for n in range(GROUP):
                    work[n] = y_product(r["ky0"], work[n])
        elif 0 in self.start:
            if self.finish == 1:
                for n in range(GROUP):
                    work[n] = y_product(r["ky"], r["u"][x0 + n], self.y_halo(r, x0, n))

            def body(rows):
                planes = []
                for n in range(GROUP):
                    product = work[n, rows] if self.finish == 1 else None
                    planes.append(self.step(r, x0 + n, n, rows, product))
                for n in range(GROUP):
                    work[n, rows] = x_sum(lambda m: planes[m], n, 0)

            self.tiles(body)
        else:
            for n in range(GROUP):
                product = None
                if self.finish == 1:
                    product = y_product(r["ky"], r["u"][x0 + n], self.y_halo(r, x0, n))
                value = self.step(r, x0 + n, n, everything, product)
                if value is not None:
                    work[n] = y_product(r["ky0"], value) if 1 in self.start else value
        if 2 in self.start:
            product = z_product(work[...].reshape(GROUP * ny, nz), r["kz"])
            out[pl.ds(x0, GROUP)] = product.reshape(GROUP, ny, nz)
        if self.send == 0:
            halo = self.halo(0)

            def put_low():
                r["low_out"][...] = out[0:halo]

            def put_high():
                r["high_out"][...] = out[nx - halo : nx]

            pl.when(g == 0)(put_low)
            pl.when(g == groups - 1)(put_high)
        if self.send == 1:
            top, bottom = pl.ds(0, SUB), pl.ds(ny - SUB, SUB)
            if self.halo(1) == SUB:
                r["low_out"][pl.ds(x0, GROUP)] = out[pl.ds(x0, GROUP), top]
                r["high_out"][pl.ds(x0, GROUP)] = out[pl.ds(x0, GROUP), bottom]
            else:
                for n in range(0, GROUP, 2):
                    pair = x0 // 2 + n // 2
                    r["low_out"][pair] = pack(out[x0 + n, top], out[x0 + n + 1, top], True)
                    r["high_out"][pair] = pack(out[x0 + n, bottom], out[x0 + n + 1, bottom], False)

    def body(self, r):
        groups = self.shape[0] // GROUP
        planes = lambda g: pl.ds(pl.multiple_of(g * GROUP, GROUP), GROUP)
        reads = READS.get(self.kind, ())

        def loads(g):
            for n, key in enumerate(reads):
                yield pltpu.make_async_copy(
                    r[key + "_in"].at[planes(g)], r[key].at[planes(g)], r["sems"].at[n, g]
                )

        def save(g):
            slot = g % 2
            return pltpu.make_async_copy(r["gbuf"].at[slot], r["grad"].at[planes(g)], r["sems"].at[slot])

        for g in range(groups):
            for copy in loads(g):
                copy.start()
        if "kz" in r:
            fill_z(r["kz"], self.reaches[2])
        if "ky" in r:
            fill_y(r["ky"], self.reaches[1], self.halo(1))
        if "ky0" in r:
            fill_y(r["ky0"], 0, 0)

        def run(g, carry):
            for copy in loads(g):
                copy.wait()
            if self.kind == "grad":
                pl.when(g >= 2)(lambda: save(g - 2).wait())
                self.group(dict(r, slot=g % 2), g)
                save(g).start()
            else:
                self.group(r, g)
            return carry

        lax.fori_loop(0, groups, run, 0)
        if self.kind == "grad":
            for g in range(max(groups - 2, 0), groups):
                save(g).wait()

    def __call__(self, name, **arrays):
        nx, ny, nz = self.shape
        half = (nx, ny, nz // 2)
        outs = {}
        if self.kind == "dual":
            outs["d"] = self.shape
        if self.kind == "part":
            outs.update(send=half, keep=half, t=self.shape)
        if self.kind == "grad":
            outs["grad"] = self.shape
        if self.start or self.send is not None:
            outs["u_out"] = self.shape
        if self.send is not None:
            outs["low_out"] = outs["high_out"] = self.strip_shape(self.send)
        scratch = self.scratch()
        names = list(arrays) + list(outs) + list(scratch)
        operands, in_specs = [], []
        for key, value in arrays.items():
            if key in ("weights", "side"):
                in_specs.append(pl.BlockSpec(memory_space=pltpu.SMEM))
            elif key.endswith("_in"):
                in_specs.append(pl.BlockSpec(memory_space=pl.ANY))
            else:
                value = pltpu.with_memory_space_constraint(value, pltpu.VMEM)
                in_specs.append(pl.BlockSpec(memory_space=pltpu.VMEM))
            operands.append(value)
        out_shape, out_specs = [], []
        for key, shape in outs.items():
            if key == "grad":
                out_shape.append(jax.ShapeDtypeStruct(shape, F32))
                out_specs.append(pl.BlockSpec(memory_space=pl.ANY))
            else:
                out_shape.append(pltpu.VMEM(shape, F32))
                out_specs.append(pl.BlockSpec(memory_space=pltpu.VMEM))
        result = pl.pallas_call(
            lambda *refs: self.body(dict(zip(names, refs))),
            name=name,
            out_shape=out_shape,
            in_specs=in_specs,
            out_specs=out_specs,
            scratch_shapes=list(scratch.values()),
            compiler_params=pltpu.CompilerParams(vmem_limit_bytes=(10 if self.kind in READS else 6) * 2**20),
            cost_estimate=COST,
        )(*operands)
        return dict(zip(outs, result))


def add_body(keep, arrived, out, total, sems):
    parts = sems.shape[0]
    step = total.shape[0] // parts
    copies = []
    for n in range(parts):
        planes = pl.ds(n * step, step)
        total[planes] = keep[planes] + arrived[planes]
        copies.append(pltpu.make_async_copy(total.at[planes], out.at[planes], sems.at[n]))
        copies[-1].start()
    for copy in copies:
        copy.wait()


def add(keep, arrived):
    in_vmem = [pltpu.with_memory_space_constraint(v, pltpu.VMEM) for v in (keep, arrived)]
    return pl.pallas_call(
        add_body,
        name="barycenter",
        out_shape=jax.ShapeDtypeStruct(keep.shape, F32),
        in_specs=[pl.BlockSpec(memory_space=pltpu.VMEM)] * 2,
        out_specs=pl.BlockSpec(memory_space=pl.ANY),
        scratch_shapes=[pltpu.VMEM(keep.shape, F32), pltpu.SemaphoreType.DMA((4,))],
        compiler_params=pltpu.CompilerParams(vmem_limit_bytes=4 * 2**20),
        cost_estimate=COST,
    )(*in_vmem)


AXES = ("pa", "pb")


def exchange(sizes, line, made):
    n = sizes[line]
    up = [(i, i + 1) for i in range(n - 1)]
    down = [(i + 1, i) for i in range(n - 1)]
    low = lax.ppermute(made["high_out"], AXES[line], up)
    high = lax.ppermute(made["low_out"], AXES[line], down)
    return dict(u=made["u_out"], low=low, high=high)


SWAP = [(0, 1), (1, 0)]


def plan(reaches):
    if reaches[2] == 0:
        return 0, 1, (2,)
    if reaches[0] == 0:
        return 1, 1, (0, 2)
    return 0, 0, (1, 2)


def halos(sizes, reaches, made, name):
    first, last, _ = plan(reaches)
    arrays = exchange(sizes, first, made)
    if first != last:
        made = Stage(made["u_out"].shape, reaches, "none", finish=first, send=last)(name, **arrays)
        arrays = exchange(sizes, last, made)
    return arrays


def scalings(sizes, reaches, log_in, warm, weights, side):
    stage = functools.partial(Stage, log_in.shape, reaches)
    first, last, begin = plan(reaches)
    made = stage("exp", start=begin, send=first)("scaling", warm_in=warm)
    arrays = halos(sizes, reaches, made, "lines_one")
    made = stage("dual", finish=last, start=begin, send=first)("dual", log_in_in=log_in, **arrays)
    arrays = halos(sizes, reaches, made, "lines_two")
    part = stage("part", finish=last)("partial", weights=weights, side=side, warm_in=warm, **arrays)
    return part["send"], part["keep"], part["t"], made["d"]


def gradient(sizes, reaches, cotangent, far, weights, side, t, d):
    stage = functools.partial(Stage, t.shape, reaches)
    first, last, begin = plan(reaches)
    made = stage("cot", start=begin, send=first)(
        "cotangent", weights=weights, side=side, cot_in=cotangent, far_in=far, t=t
    )
    arrays = halos(sizes, reaches, made, "lines_three")
    return stage("grad", finish=last)("gradient", d=d, **arrays)["grad"]


ORDERS = ((0, 1, 2), (0, 2, 1), (1, 0, 2), (1, 2, 0), (2, 0, 1), (2, 1, 0))


def per_device(sizes, log_inputs, warm_potential, bary_weights, band_reach, bary_cotangent):
    shape = log_inputs.shape[1:]
    index = 2 * band_reach[0] + (band_reach[1] > band_reach[2]).astype(jnp.int32)
    side = lax.axis_index("inp").astype(jnp.int32).reshape(1)
    far = lax.ppermute(bary_cotangent, "inp", SWAP)
    send, keep, t, d = lax.switch(
        index,
        [functools.partial(scalings, sizes, reaches) for reaches in ORDERS],
        log_inputs.reshape(shape), warm_potential.reshape(shape), bary_weights, side,
    )
    arrived = lax.ppermute(send, "inp", SWAP)
    grad = lax.switch(
        index,
        [functools.partial(gradient, sizes, reaches) for reaches in ORDERS],
        bary_cotangent, far, bary_weights, side, t, d,
    )
    return (add(keep, arrived), grad[None])


def solution(mesh):
    sizes = (mesh.shape["pa"], mesh.shape["pb"])
    return jax.shard_map(
        functools.partial(per_device, sizes),
        mesh=mesh,
        in_specs=(
            P("inp", "pa", "pb", None),
            P("inp", "pa", "pb", None),
            P("inp"),
            P(),
            P("pa", "pb", "inp"),
        ),
        out_specs=(P("pa", "pb", "inp"), P("inp", "pa", "pb", None)),
        check_vma=False,
    )
```

```python
import functools
import math

import jax
import jax.numpy as jnp
from jax import lax
from jax.experimental import pallas as pl
from jax.experimental.pallas import tpu as pltpu
from jax.sharding import PartitionSpec as P

BLOCK = 4
SIGMA = 3.0
SUB = 8
GROUP = 8
F32 = jnp.float32
BF16 = jnp.bfloat16


def tap(offset):
    gauss = math.exp(-offset * offset / (2.0 * SIGMA * SIGMA)) / (SIGMA * math.sqrt(2.0 * math.pi))
    return 0.5 * gauss + (0.5 if offset == 0 else 0.0)


def weight(i, j, reach):
    offset = (i - j).astype(F32)
    inside = jnp.abs(i // BLOCK - j // BLOCK) <= reach
    gauss = jnp.exp(-offset * offset / (2.0 * SIGMA * SIGMA)) / (SIGMA * math.sqrt(2.0 * math.pi))
    return jnp.where(i == j, 0.5, 0.0) + 0.5 * jnp.where(inside, gauss, 0.0)


def halves(value):
    high = value.astype(BF16)
    return high, (value - high.astype(F32)).astype(BF16)


def dot(a, b):
    return jnp.dot(a, b, preferred_element_type=F32)


def iotas(shape):
    return (lax.broadcasted_iota(jnp.int32, shape, 0), lax.broadcasted_iota(jnp.int32, shape, 1))


def fill_z(ref, reach):
    n = ref.shape[1]
    i, j = iotas((n, n))
    high, low = halves(weight(i, j, reach))
    ref[0:n] = high
    ref[n : 2 * n] = high
    ref[2 * n : 3 * n] = low


def z_product(rows, kz):
    high, low = halves(rows)
    return dot(jnp.concatenate([high, low, high], axis=1), kz[...])


def y_depth(ny, halo):
    return 3 * ny + (6 * halo + 15) // 16 * 16


def fill_y(ref, reach, halo):
    ny, depth = ref.shape
    i, c = iotas((ny, depth))
    own = c < 3 * ny
    part = c // ny
    j = c - part * ny
    if halo:
        c = c - 3 * ny
        side = c // (2 * halo)
        e = c - side * 2 * halo - halo
        part = jnp.where(own, part, side)
        j = jnp.where(own, j, jnp.where(e < 0, e, e + ny))
    shift = 2 * BLOCK
    value = weight(i + shift, j + shift, reach)
    high = value.astype(BF16).astype(F32)
    value = jnp.where(part == 2, value - high, jnp.where(part < 2, high, 0.0))
    ref[...] = value.astype(BF16)


def y_product(ky, own, halo=None):
    high, low = halves(own)
    pieces = [high, low, high]
    if halo is not None:
        high = halo.astype(BF16).astype(F32)
        low = halo - high
        pad = -3 * halo.shape[0] % 16
        rows = [high, low, high] + ([jnp.zeros((pad, halo.shape[1]), F32)] if pad else [])
        pieces.append(jnp.concatenate(rows, axis=0).astype(BF16))
    return dot(ky[...], jnp.concatenate(pieces, axis=0))


def pack(even, odd, top):
    row = lax.broadcasted_iota(jnp.int32, even.shape, 0)
    if top:
        return jnp.where(row < 4, even, pltpu.roll(odd, 4, 0))
    return jnp.where(row < 4, pltpu.roll(even, 4, 0), odd)


def x_sum(plane, n, reach):
    phase = n % BLOCK
    span = BLOCK * reach
    total = tap(0) * plane(n)
    for d in range(1, span + 1):
        total = total + tap(d) * (plane(n - d) + plane(n + d))
    for d in range(span + 1, span + phase + 1):
        total = total + tap(d) * plane(n - d)
    for d in range(span + 1, span + BLOCK - phase):
        total = total + tap(d) * plane(n + d)
    return total


COST = pl.CostEstimate(flops=1, bytes_accessed=1, transcendentals=0)


class Stage:
    def __init__(self, shape, reaches, cut, piece, kind, finish=None, start=(), send=None):
        self.cut = cut
        self.piece = piece
        self.shape = tuple(n // 2 if line == cut else n for line, n in enumerate(shape))
        self.reaches = reaches
        self.kind = kind
        self.finish = finish
        self.start = start
        self.send = send

    def halo(self, line):
        return BLOCK * self.reaches[line]

    def strip_shape(self, line):
        nx, ny, nz = self.shape
        halo = self.halo(line)
        if line == 0:
            return (halo, ny, nz)
        return (nx * halo // SUB, SUB, nz)

    def scratch(self):
        nx, ny, nz = self.shape
        items = {"work": pltpu.VMEM((GROUP, ny, nz), F32)}
        if 2 in self.start:
            items["kz"] = pltpu.VMEM((3 * nz, nz), BF16)
        if self.finish == 1:
            items["ky"] = pltpu.VMEM((ny, y_depth(ny, self.halo(1))), BF16)
        if 1 in self.start:
            items["ky0"] = pltpu.VMEM((ny, y_depth(ny, 0)), BF16)
        for key in self.reads() + self.writes():
            halved = key in ("cot", "far", "send", "keep") and self.cut != 2
            items[key + "_here"] = pltpu.VMEM((nx, ny, nz // 2 if halved else nz), F32)
        streams = len(self.reads() + self.writes())
        if streams:
            items["sems"] = pltpu.SemaphoreType.DMA((streams, nx // GROUP))
        return items

    def reads(self):
        if self.kind == "cot":
            return ("t",) + (("far", "cot") if self.cut != 2 else ("cot" if self.piece else "far",))
        return {"exp": ("warm",), "dual": ("inputs",), "part": ("warm",), "grad": ("d",)}.get(self.kind, ())

    def writes(self):
        if self.kind == "part":
            return (("send", "keep") if self.cut != 2 else ("keep" if self.piece else "send",)) + ("t",)
        return {"dual": ("d",), "grad": ("grad",)}.get(self.kind, ())

    def place(self, r, ref, x, rows):
        nx, ny, nz = self.shape
        if self.cut == 0 and ref.shape[0] != nx:
            if isinstance(x, pl.Slice):
                x = pl.ds(self.piece * nx + x.start, x.size)
            else:
                x = self.piece * nx + x
        if self.cut == 1 and ref.shape[1] != ny:
            rows = pl.ds(self.piece * ny + rows.start, rows.size)
        if self.cut == 2 and ref.shape[2] != nz:
            side = r["side"][0]
            z = (side if self.piece else 1 - side) * nz
            return (x, rows, pl.ds(pl.multiple_of(z, nz), nz))
        return (x, rows)

    def step(self, r, x, n, rows, product):
        kind = self.kind
        at = (x, rows)

        def get(key):
            return r[key + "_here"][at]

        def put(key, value):
            r[key + "_here"][at] = value

        if kind == "exp":
            return jnp.exp(get("warm"))
        if kind == "none":
            return product
        if kind == "dual":
            value = jnp.exp(get("inputs")) / product
            put("d", value)
            return value
        if kind == "grad":
            put("grad", get("d") * product)
            return None
        scale = r["weights"][0]
        half = self.shape[2] // 2
        first = r["side"][0] == 0
        if kind == "part":
            part = scale * (get("warm") + jnp.log(product))
            put("t", product)
            if self.cut == 2:
                put("keep" if self.piece else "send", part)
                return None
            left, right = part[:, :half], part[:, half:]
            put("keep", jnp.where(first, left, right))
            put("send", jnp.where(first, right, left))
            return None
        if self.cut == 2:
            return scale * get("cot" if self.piece else "far") / get("t")
        own, far = get("cot"), get("far")
        cot = jnp.concatenate([jnp.where(first, own, far), jnp.where(first, far, own)], axis=1)
        return scale * cot / get("t")

    def plane(self, r, x0, first, last, rows):
        halo = self.halo(0)

        def get(n):
            if n < 0 and first:
                return r["low"][halo + n, rows]
            if n >= GROUP and last:
                return r["high"][n - GROUP, rows]
            return r["u"][x0 + n, rows]

        return get

    def y_halo(self, r, x0, n):
        if self.halo(1) == SUB:
            return jnp.concatenate([r["low"][x0 + n], r["high"][x0 + n]], axis=0)
        pair = x0 // 2 + n // 2
        low, high = r["low"][pair], r["high"][pair]
        row = lax.broadcasted_iota(jnp.int32, low.shape, 0)
        if n % 2 == 0:
            return jnp.where(row < 4, low, pltpu.roll(high, 4, 0))
        return jnp.where(row < 4, pltpu.roll(low, 4, 0), high)

    def tiles(self, body):
        def tile_body(tile, carry):
            body(pl.ds(pl.multiple_of(tile * SUB, SUB), SUB))
            return carry

        lax.fori_loop(0, self.shape[1] // SUB, tile_body, 0)

    def finish_x(self, r, x0, first, last):
        def body(rows):
            get = self.plane(r, x0, first, last, rows)
            for n in range(GROUP):
                value = self.step(r, x0 + n, n, rows, x_sum(get, n, self.reaches[0]))
                if value is not None:
                    if self.start:
                        r["work"][n, rows] = value
                    else:
                        r["u_out"][x0 + n, rows] = value

        self.tiles(body)

    def group(self, r, g):
        nx, ny, nz = self.shape
        groups = nx // GROUP
        work, out = r["work"], r.get("u_out")
        x0 = pl.multiple_of(g * GROUP, GROUP)
        everything = pl.ds(0, ny)
        if self.finish == 0:
            pl.when(g == 0)(lambda: self.finish_x(r, x0, True, groups == 1))
            if groups > 2:
                pl.when((g > 0) & (g < groups - 1))(lambda: self.finish_x(r, x0, False, False))
            if groups > 1:
                pl.when(g == groups - 1)(lambda: self.finish_x(r, x0, False, True))
            if 1 in self.start:
                for n in range(GROUP):
                    work[n] = y_product(r["ky0"], work[n])
        elif 0 in self.start:
            if self.finish == 1:
                for n in range(GROUP):
                    work[n] = y_product(r["ky"], r["u"][x0 + n], self.y_halo(r, x0, n))

            def body(rows):
                planes = []
                for n in range(GROUP):
                    product = work[n, rows] if self.finish == 1 else None
                    planes.append(self.step(r, x0 + n, n, rows, product))
                for n in range(GROUP):
                    work[n, rows] = x_sum(lambda m: planes[m], n, 0)

            self.tiles(body)
        else:
            for n in range(GROUP):
                product = None
                if self.finish == 1:
                    product = y_product(r["ky"], r["u"][x0 + n], self.y_halo(r, x0, n))
                value = self.step(r, x0 + n, n, everything, product)
                if value is not None:
                    work[n] = y_product(r["ky0"], value) if 1 in self.start else value
        if 2 in self.start:
            product = z_product(work[...].reshape(GROUP * ny, nz), r["kz"])
            out[pl.ds(x0, GROUP)] = product.reshape(GROUP, ny, nz)
        if self.send == 0:
            halo = self.halo(0)

            def put_low():
                r["low_out"][...] = out[0:halo]

            def put_high():
                r["high_out"][...] = out[nx - halo : nx]

            pl.when(g == 0)(put_low)
            pl.when(g == groups - 1)(put_high)
        if self.send == 1:
            top, bottom = pl.ds(0, SUB), pl.ds(ny - SUB, SUB)
            if self.halo(1) == SUB:
                r["low_out"][pl.ds(x0, GROUP)] = out[pl.ds(x0, GROUP), top]
                r["high_out"][pl.ds(x0, GROUP)] = out[pl.ds(x0, GROUP), bottom]
            else:
                for n in range(0, GROUP, 2):
                    pair = x0 // 2 + n // 2
                    r["low_out"][pair] = pack(out[x0 + n, top], out[x0 + n + 1, top], True)
                    r["high_out"][pair] = pack(out[x0 + n, bottom], out[x0 + n + 1, bottom], False)

    def body(self, r):
        groups = self.shape[0] // GROUP
        planes = lambda g: pl.ds(pl.multiple_of(g * GROUP, GROUP), GROUP)

        everything = pl.ds(0, self.shape[1])
        reads, writes = self.reads(), self.writes()

        def load(n, g):
            source = r[reads[n]]
            source = source.at[self.place(r, source, planes(g), everything)]
            return pltpu.make_async_copy(source, r[reads[n] + "_here"].at[planes(g)], r["sems"].at[n, g])

        def save(n, g):
            target = r[writes[n]]
            target = target.at[self.place(r, target, planes(g), everything)]
            sem = r["sems"].at[len(reads) + n, g]
            return pltpu.make_async_copy(r[writes[n] + "_here"].at[planes(g)], target, sem)

        for g in range(groups):
            for n in range(len(reads)):
                load(n, g).start()
        if "kz" in r:
            fill_z(r["kz"], self.reaches[2])
        if "ky" in r:
            fill_y(r["ky"], self.reaches[1], self.halo(1))
        if "ky0" in r:
            fill_y(r["ky0"], 0, 0)

        def run(g, carry):
            for n in range(len(reads)):
                load(n, g).wait()
            self.group(r, g)
            for n in range(len(writes)):
                save(n, g).start()
            return carry

        lax.fori_loop(0, groups, run, 0)
        for g in range(groups):
            for n in range(len(writes)):
                save(n, g).wait()

    def __call__(self, name, **arrays):
        nx, ny, nz = self.shape
        whole = tuple(n * 2 if line == self.cut else n for line, n in enumerate(self.shape))
        outs = {}
        aliases = {}
        alone = self.cut == 2 and self.piece == 1
        if self.kind == "dual":
            outs["d"] = self.shape if alone else whole
        if self.kind == "part":
            kept = (*whole[:2], whole[2] // 2)
            outs["t"] = self.shape if alone else whole
            outs.update(dict(keep=kept) if alone else dict(send=kept, keep=kept))
        if self.kind == "grad":
            outs["grad"] = whole
        for n, key in enumerate(arrays):
            if key.endswith("_in"):
                aliases[n] = list(outs).index(key[:-3])
        if self.start or self.send is not None:
            outs["u_out"] = self.shape
        if self.send is not None:
            outs["low_out"] = outs["high_out"] = self.strip_shape(self.send)
        scratch = self.scratch()
        names = list(arrays) + list(outs) + list(scratch)
        operands, in_specs = [], []
        for key, value in arrays.items():
            if key in ("weights", "side"):
                in_specs.append(pl.BlockSpec(memory_space=pltpu.SMEM))
            elif key in ("u", "low", "high"):
                value = pltpu.with_memory_space_constraint(value, pltpu.VMEM)
                in_specs.append(pl.BlockSpec(memory_space=pltpu.VMEM))
            else:
                in_specs.append(pl.BlockSpec(memory_space=pl.ANY))
            operands.append(value)
        out_shape, out_specs = [], []
        for key, shape in outs.items():
            space = pltpu.VMEM if key in ("u_out", "low_out", "high_out") else pltpu.HBM
            out_shape.append(space(shape, F32))
            out_specs.append(pl.BlockSpec(memory_space=space))
        result = pl.pallas_call(
            lambda *refs: self.body(dict(zip(names, refs))),
            name=name,
            out_shape=out_shape,
            in_specs=in_specs,
            out_specs=out_specs,
            input_output_aliases=aliases,
            scratch_shapes=list(scratch.values()),
            compiler_params=pltpu.CompilerParams(vmem_limit_bytes=16 * 2**20),
            cost_estimate=COST,
        )(*operands)
        return dict(zip(outs, result))


def add_body(keep, arrived, after, out, left, right, total, sems):
    parts = sems.shape[1]
    step = total.shape[0] // parts
    planes = [pl.ds(n * step, step) for n in range(parts)]
    loads = [
        pltpu.make_async_copy(source.at[p], target.at[p], sems.at[m, n])
        for n, p in enumerate(planes)
        for m, (source, target) in enumerate(((keep, left), (arrived, right)))
    ]
    saves = [pltpu.make_async_copy(total.at[p], out.at[p], sems.at[2, n]) for n, p in enumerate(planes)]
    for copy in loads:
        copy.start()
    for n, p in enumerate(planes):
        loads[2 * n].wait()
        loads[2 * n + 1].wait()
        total[p] = left[p] + right[p]
        saves[n].start()
    for copy in saves:
        copy.wait()


def add(keep, arrived, after):
    return pl.pallas_call(
        add_body,
        name="barycenter",
        out_shape=pltpu.HBM(keep.shape, F32),
        in_specs=[pl.BlockSpec(memory_space=pl.ANY)] * 3,
        out_specs=pl.BlockSpec(memory_space=pltpu.HBM),
        scratch_shapes=[pltpu.VMEM(keep.shape, F32)] * 3 + [pltpu.SemaphoreType.DMA((3, 4))],
        compiler_params=pltpu.CompilerParams(vmem_limit_bytes=10 * 2**20),
        cost_estimate=COST,
    )(keep, arrived, after)


AXES = ("pa", "pb")


def exchange(sizes, line, made):
    n = sizes[line]
    up = [(i, i + 1) for i in range(n - 1)]
    down = [(i + 1, i) for i in range(n - 1)]
    low = lax.ppermute(made["high_out"], AXES[line], up)
    high = lax.ppermute(made["low_out"], AXES[line], down)
    return dict(u=made["u_out"], low=low, high=high)


SWAP = [(0, 1), (1, 0)]


def plan(reaches):
    if reaches[2] == 0:
        return 0, 1, (2,)
    if reaches[0] == 0:
        return 1, 1, (0, 2)
    return 0, 0, (1, 2)


class Case:
    def __init__(self, sizes, reaches, shape):
        self.sizes = sizes
        self.reaches = reaches
        self.shape = shape
        self.first, self.last, self.begin = plan(reaches)
        self.cut = reaches.index(0)

    def stage(self, n, *args, **kwargs):
        return Stage(self.shape, self.reaches, self.cut, n, *args, **kwargs)

    def halos(self, made, name):
        arrays = {n: exchange(self.sizes, self.first, made[n]) for n in made}
        if self.first != self.last:
            for n in made:
                arrays[n] = self.stage(n, "none", finish=self.first, send=self.last)(f"{name}_{n}", **arrays[n])
            arrays = {n: exchange(self.sizes, self.last, arrays[n]) for n in made}
        return arrays

    def chain(self, pieces, inputs, warm, weights, side):
        made = {
            n: self.stage(n, "exp", start=self.begin, send=self.first)(f"scaling_{n}", warm=warm, side=side)
            for n in pieces
        }
        arrays = self.halos(made, "lines_one")
        made, whole = {}, {}
        for n in pieces:
            maker = self.stage(n, "dual", finish=self.last, start=self.begin, send=self.first)
            made[n] = maker(f"dual_{n}", inputs=inputs, side=side, **arrays[n], **whole)
            whole = dict(d_in=made[n]["d"])
        d = whole["d_in"]
        arrays = self.halos(made, "lines_two")
        whole = {}
        for n in pieces:
            part = self.stage(n, "part", finish=self.last)(
                f"partial_{n}", warm=warm, weights=weights, side=side, **arrays[n], **whole
            )
            whole = {key + "_in": value for key, value in part.items()}
        return dict(part, d=d)

    def scalings(self, inputs, warm, weights, side):
        pieces = (0,) if self.cut == 2 else (0, 1)
        done = self.chain(pieces, inputs, warm, weights, side)
        return tuple(done[key] for key in ("send", "keep", "t", "d"))

    def gradient(self, inputs, warm, weights, side, cotangent, far, keep, t, d):
        t, d = [t, t], [d, d]
        if self.cut == 2:
            done = self.chain((1,), inputs, warm, weights, side)
            keep, t[1], d[1] = done["keep"], done["t"], done["d"]
        made = {}
        for n in (0, 1):
            reads = dict(far=far, cot=cotangent)
            if self.cut == 2:
                reads.pop(("cot", "far")[n])
            made[n] = self.stage(n, "cot", start=self.begin, send=self.first)(
                f"cotangent_{n}", t=t[n], weights=weights, side=side, **reads
            )
        arrays = self.halos(made, "lines_three")
        whole = {}
        for n in (0, 1):
            grad = self.stage(n, "grad", finish=self.last)(
                f"gradient_{n}", d=d[n], side=side, **arrays[n], **whole
            )["grad"]
            whole = dict(grad_in=grad)
        return grad, keep


ORDERS = ((0, 1, 2), (0, 2, 1), (1, 0, 2), (1, 2, 0), (2, 0, 1), (2, 1, 0))


def per_device(sizes, log_inputs, warm_potential, bary_weights, band_reach, bary_cotangent):
    shape = log_inputs.shape[1:]
    index = 2 * band_reach[0] + (band_reach[1] > band_reach[2]).astype(jnp.int32)
    side = lax.axis_index("inp").astype(jnp.int32).reshape(1)
    cases = [Case(sizes, reaches, shape) for reaches in ORDERS]
    inputs, warm = log_inputs.reshape(shape), warm_potential.reshape(shape)
    common = (inputs, warm, bary_weights, side)
    far = lax.ppermute(bary_cotangent, "inp", SWAP)
    send, keep, t, d = lax.switch(index, [case.scalings for case in cases], *common)
    arrived = lax.ppermute(send, "inp", SWAP)
    grad, keep = lax.switch(
        index, [case.gradient for case in cases], *common, bary_cotangent, far, keep, t, d
    )
    return (add(keep, arrived, grad), grad[None])


def solution(mesh):
    sizes = (mesh.shape["pa"], mesh.shape["pb"])
    return jax.shard_map(
        functools.partial(per_device, sizes),
        mesh=mesh,
        in_specs=(
            P("inp", "pa", "pb", None),
            P("inp", "pa", "pb", None),
            P("inp"),
            P(),
            P("pa", "pb", "inp"),
        ),
        out_specs=(P("pa", "pb", "inp"), P("inp", "pa", "pb", None)),
        check_vma=False,
    )
```

```python
import functools
import math

import jax
import jax.numpy as jnp
from jax import lax
from jax.experimental import pallas as pl
from jax.experimental.pallas import tpu as pltpu
from jax.sharding import PartitionSpec as P

BLOCK = 4
BLOCK_BITS = 2
HALO = 2 * BLOCK
SIGMA = 3.0
SUB = 8
GROUP = 8
F32 = jnp.float32
BF16 = jnp.bfloat16


def tap(offset):
    gauss = math.exp(-offset * offset / (2.0 * SIGMA * SIGMA)) / (SIGMA * math.sqrt(2.0 * math.pi))
    return 0.5 * gauss + (0.5 if offset == 0 else 0.0)


def weight(i, j, reach):
    offset = (i - j).astype(F32)
    inside = jnp.abs((i >> BLOCK_BITS) - (j >> BLOCK_BITS)) <= reach
    gauss = jnp.exp(-offset * offset / (2.0 * SIGMA * SIGMA)) / (SIGMA * math.sqrt(2.0 * math.pi))
    return jnp.where(i == j, 0.5, 0.0) + 0.5 * jnp.where(inside, gauss, 0.0)


def halves(value):
    high = value.astype(BF16)
    return high, (value - high.astype(F32)).astype(BF16)


def dot(a, b):
    return jnp.dot(a, b, preferred_element_type=F32)


def iotas(shape):
    return (lax.broadcasted_iota(jnp.int32, shape, 0), lax.broadcasted_iota(jnp.int32, shape, 1))


def fill_z(ref, reach):
    n = ref.shape[1]
    i, j = iotas((n, n))
    high, low = halves(weight(i, j, reach))
    ref[0:n] = high
    ref[n : 2 * n] = high
    ref[2 * n : 3 * n] = low


def z_product(rows, kz):
    high, low = halves(rows)
    return dot(jnp.concatenate([high, low, high], axis=1), kz[...])


def y_depth(ny, halo):
    return 3 * (ny + 2 * halo)


def fill_y(ref, reach, halo):
    ny, depth = ref.shape
    i, c = iotas((ny, depth))
    wide = 2 * halo
    own = c < 3 * ny
    size = jnp.where(own, ny, max(wide, 1))
    c = jnp.where(own, c, c - 3 * ny)
    part = jnp.where(c >= 2 * size, 2, jnp.where(c >= size, 1, 0))
    j = c - part * size
    j = jnp.where(own, j, jnp.where(j < halo, j - halo, j - halo + ny))
    value = weight(i + HALO, j + HALO, reach)
    high = value.astype(BF16).astype(F32)
    ref[...] = jnp.where(part == 2, value - high, high).astype(BF16)


def y_product(ky, own, halo=None):
    high, low = halves(own)
    pieces = [high, low, high]
    if halo is not None:
        high, low = halves(halo)
        pieces += [high, low, high]
    return dot(ky[...], jnp.concatenate(pieces, axis=0))


def x_sum(plane, n, reach):
    phase = n % BLOCK
    span = BLOCK * reach
    total = tap(0) * plane(n)
    for d in range(1, span + 1):
        total = total + tap(d) * (plane(n - d) + plane(n + d))
    for d in range(span + 1, span + phase + 1):
        total = total + tap(d) * plane(n - d)
    for d in range(span + 1, span + BLOCK - phase):
        total = total + tap(d) * plane(n + d)
    return total


MATRICES = ("kz", "ky", "ky0")
COST = pl.CostEstimate(flops=1, bytes_accessed=1, transcendentals=0)


class Stage:
    def __init__(self, shape, cut, piece, kind, finish=None, start=(), send=None, fills=False):
        self.cut = cut
        self.piece = piece
        self.shape = tuple(n // 2 if line == cut else n for line, n in enumerate(shape))
        self.kind = kind
        self.finish = finish
        self.start = start
        self.send = send
        self.fills = fills

    def matrices(self):
        nx, ny, nz = self.shape
        shapes = {"kz": (3 * nz, nz)}
        if self.cut == 1:
            shapes["ky0"] = (ny, y_depth(ny, 0))
        else:
            shapes["ky"] = (ny, y_depth(ny, HALO))
        return shapes

    def needs(self):
        if self.fills:
            return ()
        wanted = {"kz": 2 in self.start, "ky": self.finish == 1, "ky0": 1 in self.start}
        return tuple(key for key in self.matrices() if wanted[key])

    def scratch(self):
        nx, ny, nz = self.shape
        items = {"work": pltpu.VMEM((GROUP, ny, nz), F32)}
        for key in self.reads() + self.writes():
            halved = key in ("cot", "far", "send", "keep") and self.cut != 2
            items[key + "_here"] = pltpu.VMEM((nx, ny, nz // 2 if halved else nz), F32)
        streams = len(self.reads() + self.writes())
        if streams:
            items["sems"] = pltpu.SemaphoreType.DMA((streams, nx // GROUP))
        return items

    def reads(self):
        if self.kind == "cot":
            return ("t",) + (("far", "cot") if self.cut != 2 else ("cot" if self.piece else "far",))
        return {"exp": ("warm",), "dual": ("inputs",), "part": ("warm",), "grad": ("d",)}.get(self.kind, ())

    def writes(self):
        if self.kind == "part":
            return (("send", "keep") if self.cut != 2 else ("keep" if self.piece else "send",)) + ("t",)
        return {"dual": ("d",), "grad": ("grad",)}.get(self.kind, ())

    def place(self, r, ref, x, rows):
        nx, ny, nz = self.shape
        if self.cut == 0 and ref.shape[0] != nx:
            if isinstance(x, pl.Slice):
                x = pl.ds(self.piece * nx + x.start, x.size)
            else:
                x = self.piece * nx + x
        if self.cut == 1 and ref.shape[1] != ny:
            rows = pl.ds(self.piece * ny + rows.start, rows.size)
        if self.cut == 2 and ref.shape[2] != nz:
            side = r["side"][0]
            z = (side if self.piece else 1 - side) * nz
            return (x, rows, pl.ds(pl.multiple_of(z, nz), nz))
        return (x, rows)

    def step(self, r, x, n, rows, product):
        kind = self.kind
        at = (x, rows)

        def get(key):
            return r[key + "_here"][at]

        def put(key, value):
            r[key + "_here"][at] = value

        if kind == "exp":
            return jnp.exp(get("warm"))
        if kind == "none":
            return product
        if kind == "dual":
            value = jnp.exp(get("inputs")) / product
            put("d", value)
            return value
        if kind == "grad":
            put("grad", get("d") * product)
            return None
        scale = r["weights"][0]
        half = self.shape[2] // 2
        first = r["side"][0] == 0
        if kind == "part":
            part = scale * (get("warm") + jnp.log(product))
            put("t", product)
            if self.cut == 2:
                put("keep" if self.piece else "send", part)
                return None
            left, right = part[:, :half], part[:, half:]
            put("keep", jnp.where(first, left, right))
            put("send", jnp.where(first, right, left))
            return None
        if self.cut == 2:
            return scale * get("cot" if self.piece else "far") / get("t")
        own, far = get("cot"), get("far")
        cot = jnp.concatenate([jnp.where(first, own, far), jnp.where(first, far, own)], axis=1)
        return scale * cot / get("t")

    def tiles(self, body):
        def tile_body(tile, carry):
            body(pl.ds(pl.multiple_of(tile * SUB, SUB), SUB))
            return carry

        lax.fori_loop(0, self.shape[1] // SUB, tile_body, 0)

    def planes(self, body):
        def pair_body(pair, carry):
            body(2 * pair)
            body(2 * pair + 1)
            return carry

        lax.fori_loop(0, GROUP // 2, pair_body, 0)

    def finish_x(self, r, x0, reach):
        u = r["u_ext"]

        def body(rows):
            for q in range(0, GROUP, BLOCK):
                span = BLOCK * reach
                window = {m: u[HALO + x0 + m, rows] for m in range(q - span, q + BLOCK + span)}
                for n in range(q, q + BLOCK):
                    value = self.step(r, x0 + n, n, rows, x_sum(window.get, n, reach))
                    if value is not None:
                        if self.start:
                            r["work"][n, rows] = value
                        else:
                            r["u_out"][x0 + n, rows] = value

        self.tiles(body)

    def group(self, r, g):
        nx, ny, nz = self.shape
        groups = nx // GROUP
        work, out = r["work"], r.get("u_out")
        x0 = pl.multiple_of(g * GROUP, GROUP)
        everything = pl.ds(0, ny)

        def finish_y(n):
            x = x0 + n
            return y_product(r["ky"], r["u"][x], jnp.concatenate([r["low"][x], r["high"][x]], axis=0))

        if self.finish == 0:
            for reach in (1, 2):
                pl.when(r["reach"][0] == reach)(lambda: self.finish_x(r, x0, reach))
            if 1 in self.start:

                def local_y(n):
                    work[n] = y_product(r["ky0"], work[n])

                self.planes(local_y)
        elif 0 in self.start:
            if self.finish == 1:

                def keep_product(n):
                    work[n] = finish_y(n)

                self.planes(keep_product)

            def body(rows):
                for q in range(0, GROUP, BLOCK):
                    planes = {}
                    for n in range(q, q + BLOCK):
                        product = work[n, rows] if self.finish == 1 else None
                        planes[n] = self.step(r, x0 + n, n, rows, product)
                    for n in range(q, q + BLOCK):
                        work[n, rows] = x_sum(planes.get, n, 0)

            self.tiles(body)
        else:

            def whole_plane(n):
                product = finish_y(n) if self.finish == 1 else None
                value = self.step(r, x0 + n, n, everything, product)
                if value is not None:
                    work[n] = y_product(r["ky0"], value) if 1 in self.start else value

            self.planes(whole_plane)
        shift = HALO if self.send == 0 else 0
        if 2 in self.start:
            product = z_product(work[...].reshape(GROUP * ny, nz), r["kz"])
            out[pl.ds(x0 + shift, GROUP)] = product.reshape(GROUP, ny, nz)
        if self.send == 0:

            def put_low():
                r["low_out"][...] = out[HALO : 2 * HALO]

            def put_high():
                r["high_out"][...] = out[nx : nx + HALO]

            pl.when(g == 0)(put_low)
            pl.when(g == groups - 1)(put_high)
        if self.send == 1:
            r["low_out"][pl.ds(x0, GROUP)] = out[pl.ds(x0, GROUP), pl.ds(0, HALO)]
            r["high_out"][pl.ds(x0, GROUP)] = out[pl.ds(x0, GROUP), pl.ds(ny - HALO, HALO)]

    def body(self, r):
        groups = self.shape[0] // GROUP
        planes = lambda g: pl.ds(pl.multiple_of(g * GROUP, GROUP), GROUP)

        everything = pl.ds(0, self.shape[1])
        reads, writes = self.reads(), self.writes()

        def load(n, g):
            source = r[reads[n]]
            source = source.at[self.place(r, source, planes(g), everything)]
            return pltpu.make_async_copy(source, r[reads[n] + "_here"].at[planes(g)], r["sems"].at[n, g])

        def save(n, g):
            target = r[writes[n]]
            target = target.at[self.place(r, target, planes(g), everything)]
            sem = r["sems"].at[len(reads) + n, g]
            return pltpu.make_async_copy(r[writes[n] + "_here"].at[planes(g)], target, sem)

        for g in range(groups):
            for n in range(len(reads)):
                load(n, g).start()
        if self.fills:
            fill_z(r["kz"], r["reach"][2])
            if "ky" in r:
                fill_y(r["ky"], r["reach"][1], HALO)
            if "ky0" in r:
                fill_y(r["ky0"], 0, 0)
        if self.finish == 0:
            nx = self.shape[0]
            r["u_ext"][0:HALO] = r["low"][...]
            r["u_ext"][HALO + nx : 2 * HALO + nx] = r["high"][...]

        def run(g, carry):
            for n in range(len(reads)):
                load(n, g).wait()
            self.group(r, g)
            for n in range(len(writes)):
                save(n, g).start()
            return carry

        lax.fori_loop(0, groups, run, 0)
        for g in range(groups):
            for n in range(len(writes)):
                save(n, g).wait()

    def __call__(self, name, **arrays):
        nx, ny, nz = self.shape
        whole = tuple(n * 2 if line == self.cut else n for line, n in enumerate(self.shape))
        outs = {}
        aliases = {}
        alone = self.cut == 2 and self.piece == 1
        if self.kind == "dual":
            outs["d"] = self.shape if alone else whole
        if self.kind == "part":
            kept = (*whole[:2], whole[2] // 2)
            outs["t"] = self.shape if alone else whole
            outs.update(dict(keep=kept) if alone else dict(send=kept, keep=kept))
        if self.kind == "grad":
            outs["grad"] = whole
        for n, key in enumerate(arrays):
            if key.endswith("_in"):
                aliases[n] = list(outs).index(key[:-3])
        if self.start or self.send is not None:
            outs["u_out"] = (nx + 2 * HALO, ny, nz) if self.send == 0 else self.shape
        if self.send is not None:
            outs["low_out"] = outs["high_out"] = (HALO, ny, nz) if self.send == 0 else (nx, HALO, nz)
        if self.finish == 0:
            outs["u_ext"] = arrays["u"].shape
            aliases[list(arrays).index("u")] = list(outs).index("u_ext")
        if self.fills:
            outs.update(self.matrices())
        scratch = self.scratch()
        names = list(arrays) + list(outs) + list(scratch)
        operands, in_specs = [], []
        for key, value in arrays.items():
            if key in ("weights", "side", "reach"):
                in_specs.append(pl.BlockSpec(memory_space=pltpu.SMEM))
            elif key in ("u", "low", "high", "kz", "ky", "ky0"):
                value = pltpu.with_memory_space_constraint(value, pltpu.VMEM)
                in_specs.append(pl.BlockSpec(memory_space=pltpu.VMEM))
            else:
                in_specs.append(pl.BlockSpec(memory_space=pl.ANY))
            operands.append(value)
        out_shape, out_specs = [], []
        for key, shape in outs.items():
            inside = ("u_out", "low_out", "high_out", "u_ext", *MATRICES)
            space = pltpu.VMEM if key in inside else pltpu.HBM
            out_shape.append(space(shape, BF16 if key in MATRICES else F32))
            out_specs.append(pl.BlockSpec(memory_space=space))
        result = pl.pallas_call(
            lambda *refs: self.body(dict(zip(names, refs))),
            name=name,
            out_shape=out_shape,
            in_specs=in_specs,
            out_specs=out_specs,
            input_output_aliases=aliases,
            scratch_shapes=list(scratch.values()),
            compiler_params=pltpu.CompilerParams(vmem_limit_bytes=16 * 2**20),
            cost_estimate=COST,
        )(*operands)
        return dict(zip(outs, result))


def add_body(keep, arrived, after, out, left, right, total, sems):
    parts = sems.shape[1]
    step = total.shape[0] // parts
    planes = [pl.ds(n * step, step) for n in range(parts)]
    loads = [
        pltpu.make_async_copy(source.at[p], target.at[p], sems.at[m, n])
        for n, p in enumerate(planes)
        for m, (source, target) in enumerate(((keep, left), (arrived, right)))
    ]
    saves = [pltpu.make_async_copy(total.at[p], out.at[p], sems.at[2, n]) for n, p in enumerate(planes)]
    for copy in loads:
        copy.start()
    for n, p in enumerate(planes):
        loads[2 * n].wait()
        loads[2 * n + 1].wait()
        total[p] = left[p] + right[p]
        saves[n].start()
    for copy in saves:
        copy.wait()


def add(keep, arrived, after):
    return pl.pallas_call(
        add_body,
        name="barycenter",
        out_shape=pltpu.HBM(keep.shape, F32),
        in_specs=[pl.BlockSpec(memory_space=pl.ANY)] * 3,
        out_specs=pl.BlockSpec(memory_space=pltpu.HBM),
        scratch_shapes=[pltpu.VMEM(keep.shape, F32)] * 3 + [pltpu.SemaphoreType.DMA((3, 4))],
        compiler_params=pltpu.CompilerParams(vmem_limit_bytes=10 * 2**20),
        cost_estimate=COST,
    )(keep, arrived, after)


AXES = ("pa", "pb")


def exchange(sizes, line, made):
    n = sizes[line]
    up = [(i, i + 1) for i in range(n - 1)]
    down = [(i + 1, i) for i in range(n - 1)]
    low = lax.ppermute(made["high_out"], AXES[line], up)
    high = lax.ppermute(made["low_out"], AXES[line], down)
    return dict(u=made["u_out"], low=low, high=high)


SWAP = [(0, 1), (1, 0)]


def plan(cut):
    return ((1, 1, (0, 2)), (0, 0, (1, 2)), (0, 1, (2,)))[cut]


class Case:
    def __init__(self, sizes, cut, shape):
        self.sizes = sizes
        self.cut = cut
        self.shape = shape
        self.first, self.last, self.begin = plan(cut)

    def run(self, matrices, n, name, kind, arrays, fills=False, **form):
        stage = Stage(self.shape, self.cut, n, kind, fills=fills, **form)
        made = stage(f"{name}_{n}", **arrays, **{key: matrices[key] for key in stage.needs()})
        if fills:
            matrices.update({key: made.pop(key) for key in stage.matrices()})
        return made

    def halos(self, matrices, made, name, scalars):
        arrays = {n: exchange(self.sizes, self.first, made[n]) for n in made}
        if self.first != self.last:
            for n in made:
                arrays[n] = self.run(
                    matrices, n, name, "none", dict(**scalars, **arrays[n]), finish=self.first, send=self.last
                )
            arrays = {n: exchange(self.sizes, self.last, arrays[n]) for n in made}
        return arrays

    def chain(self, matrices, pieces, inputs, warm, weights, side, reach):
        scalars = dict(side=side, reach=reach)
        begin = dict(start=self.begin, send=self.first)
        made = {
            n: self.run(matrices, n, "scaling", "exp", dict(warm=warm, **scalars), fills=n == pieces[0], **begin)
            for n in pieces
        }
        arrays = self.halos(matrices, made, "lines_one", scalars)
        made, whole = {}, {}
        for n in pieces:
            given = dict(inputs=inputs, **scalars, **arrays[n], **whole)
            made[n] = self.run(matrices, n, "dual", "dual", given, finish=self.last, **begin)
            whole = dict(d_in=made[n]["d"])
        d = whole["d_in"]
        arrays = self.halos(matrices, made, "lines_two", scalars)
        whole = {}
        for n in pieces:
            given = dict(warm=warm, weights=weights, **scalars, **arrays[n], **whole)
            part = self.run(matrices, n, "partial", "part", given, finish=self.last)
            whole = {key + "_in": part[key] for key in ("send", "keep", "t") if key in part}
        return dict(part, d=d)

    def scalings(self, *common):
        done = self.chain({}, (0,) if self.cut == 2 else (0, 1), *common)
        return tuple(done[key] for key in ("send", "keep", "t", "d"))

    def gradient(self, inputs, warm, weights, side, reach, cotangent, far, keep, t, d):
        t, d, matrices = [t, t], [d, d], {}
        if self.cut == 2:
            done = self.chain(matrices, (1,), inputs, warm, weights, side, reach)
            keep, t[1], d[1] = done["keep"], done["t"], done["d"]
        made = {}
        scalars = dict(side=side, reach=reach)
        for n in (0, 1):
            given = dict(t=t[n], weights=weights, far=far, cot=cotangent, **scalars)
            if self.cut == 2:
                given.pop(("cot", "far")[n])
            form = dict(start=self.begin, send=self.first, fills=not matrices)
            made[n] = self.run(matrices, n, "cotangent", "cot", given, **form)
        arrays = self.halos(matrices, made, "lines_three", scalars)
        whole = {}
        for n in (0, 1):
            given = dict(d=d[n], **scalars, **arrays[n], **whole)
            whole = dict(grad_in=self.run(matrices, n, "gradient", "grad", given, finish=self.last)["grad"])
        return whole["grad_in"], keep


def per_device(sizes, log_inputs, warm_potential, bary_weights, band_reach, bary_cotangent):
    shape = log_inputs.shape[1:]
    index = (band_reach[0] != 0).astype(jnp.int32) + (band_reach[2] == 0).astype(jnp.int32)
    side = lax.axis_index("inp").astype(jnp.int32).reshape(1)
    cases = [Case(sizes, cut, shape) for cut in range(3)]
    inputs, warm = log_inputs.reshape(shape), warm_potential.reshape(shape)
    common = (inputs, warm, bary_weights, side, band_reach)
    far = lax.ppermute(bary_cotangent, "inp", SWAP)
    send, keep, t, d = lax.switch(index, [case.scalings for case in cases], *common)
    arrived = lax.ppermute(send, "inp", SWAP)
    grad, keep = lax.switch(
        index, [case.gradient for case in cases], *common, bary_cotangent, far, keep, t, d
    )
    return (add(keep, arrived, grad), grad[None])


def solution(mesh):
    sizes = (mesh.shape["pa"], mesh.shape["pb"])
    return jax.shard_map(
        functools.partial(per_device, sizes),
        mesh=mesh,
        in_specs=(
            P("inp", "pa", "pb", None),
            P("inp", "pa", "pb", None),
            P("inp"),
            P(),
            P("pa", "pb", "inp"),
        ),
        out_specs=(P("pa", "pb", "inp"), P("inp", "pa", "pb", None)),
        check_vma=False,
    )
```

```python
import functools
import math

import jax
import jax.numpy as jnp
from jax import lax
from jax.experimental import pallas as pl
from jax.experimental.pallas import tpu as pltpu
from jax.sharding import PartitionSpec as P

BLOCK = 4
BLOCK_BITS = 2
HALO = 2 * BLOCK
SIGMA = 3.0
SUB = 8
GROUP = 8
F32 = jnp.float32
BF16 = jnp.bfloat16


def tap(offset):
    gauss = math.exp(-offset * offset / (2.0 * SIGMA * SIGMA)) / (SIGMA * math.sqrt(2.0 * math.pi))
    return 0.5 * gauss + (0.5 if offset == 0 else 0.0)


def weight(i, j, reach):
    offset = (i - j).astype(F32)
    inside = jnp.abs((i >> BLOCK_BITS) - (j >> BLOCK_BITS)) <= reach
    gauss = jnp.exp(-offset * offset / (2.0 * SIGMA * SIGMA)) / (SIGMA * math.sqrt(2.0 * math.pi))
    return jnp.where(i == j, 0.5, 0.0) + 0.5 * jnp.where(inside, gauss, 0.0)


def halves(value):
    high = value.astype(BF16)
    return high, (value - high.astype(F32)).astype(BF16)


def dot(a, b):
    return jnp.dot(a, b, preferred_element_type=F32)


def iotas(shape):
    return (lax.broadcasted_iota(jnp.int32, shape, 0), lax.broadcasted_iota(jnp.int32, shape, 1))


def fill_z(ref, reach):
    n = ref.shape[1]
    i, j = iotas((n, n))
    high, low = halves(weight(i, j, reach))
    ref[0:n] = high
    ref[n : 2 * n] = high
    ref[2 * n : 3 * n] = low


def z_product(rows, kz):
    high, low = halves(rows)
    return dot(jnp.concatenate([high, low, high], axis=1), kz[...])


def y_depth(ny, halo):
    return 3 * (ny + 2 * halo)


def fill_y(ref, reach, halo):
    ny, depth = ref.shape
    i, c = iotas((ny, depth))
    wide = 2 * halo
    own = c < 3 * ny
    size = jnp.where(own, ny, max(wide, 1))
    c = jnp.where(own, c, c - 3 * ny)
    part = jnp.where(c >= 2 * size, 2, jnp.where(c >= size, 1, 0))
    j = c - part * size
    j = jnp.where(own, j, jnp.where(j < halo, j - halo, j - halo + ny))
    value = weight(i + HALO, j + HALO, reach)
    high = value.astype(BF16).astype(F32)
    ref[...] = jnp.where(part == 2, value - high, high).astype(BF16)


def y_product(ky, own, halo=None):
    high, low = halves(own)
    pieces = [high, low, high]
    if halo is not None:
        high, low = halves(halo)
        pieces += [high, low, high]
    return dot(ky[...], jnp.concatenate(pieces, axis=0))


def x_sum(plane, n, reach):
    phase = n % BLOCK
    span = BLOCK * reach
    total = tap(0) * plane(n)
    for d in range(1, span + 1):
        total = total + tap(d) * (plane(n - d) + plane(n + d))
    for d in range(span + 1, span + phase + 1):
        total = total + tap(d) * plane(n - d)
    for d in range(span + 1, span + BLOCK - phase):
        total = total + tap(d) * plane(n + d)
    return total


MATRICES = ("kz", "ky", "ky0")
EDGES = ("low", "high", "y_low", "y_high", "corner_low", "corner_high")
INSIDE = ("u", "u_out", "u_ext", *EDGES, *(edge + "_out" for edge in EDGES), *MATRICES)
BOTH = (0, 1)
COST = pl.CostEstimate(flops=1, bytes_accessed=1, transcendentals=0)


class Stage:
    def __init__(self, shape, cut, piece, kind, finish=None, start=(), send=None, fills=False):
        self.cut = cut
        self.piece = piece
        self.shape = tuple(n // 2 if line == cut else n for line, n in enumerate(shape))
        self.kind = kind
        self.finish = finish
        self.start = start
        self.send = send
        self.fills = fills

    def matrices(self):
        nx, ny, nz = self.shape
        shapes = {"kz": (3 * nz, nz)}
        if 1 in self.start:
            shapes["ky0"] = (ny, y_depth(ny, 0))
        else:
            shapes["ky"] = (ny, y_depth(ny, HALO))
        return shapes

    def needs(self):
        if self.fills:
            return ()
        wanted = {"kz": 2 in self.start, "ky": self.finish in (1, BOTH), "ky0": 1 in self.start}
        return tuple(key for key in wanted if wanted[key])

    def scratch(self):
        nx, ny, nz = self.shape
        items = {"work": pltpu.VMEM((GROUP, ny, nz), F32)}
        if self.finish == BOTH:
            items["edge"] = pltpu.VMEM((GROUP, 2 * HALO, nz), F32)
            items["y_ext"] = pltpu.VMEM((nx + 2 * HALO, 2 * HALO, nz), F32)
        for key in self.reads() + self.writes():
            halved = key in ("cot", "far", "send", "keep")
            items[key + "_here"] = pltpu.VMEM((nx, ny, nz // 2 if halved else nz), F32)
        streams = len(self.reads() + self.writes())
        if streams:
            items["sems"] = pltpu.SemaphoreType.DMA((streams, nx // GROUP))
        return items

    def reads(self):
        if self.kind == "cot":
            return ("t", "far", "cot")
        return {"exp": ("warm",), "dual": ("inputs",), "part": ("warm",), "grad": ("d",)}.get(self.kind, ())

    def writes(self):
        if self.kind == "part":
            return ("send", "keep", "t")
        return {"dual": ("d",), "grad": ("grad",)}.get(self.kind, ())

    def place(self, g):
        nx, ny, _ = self.shape
        x, y = (self.piece * n if self.cut == line else 0 for line, n in enumerate((nx, ny)))
        return (pl.ds(pl.multiple_of(x + g * GROUP, GROUP), GROUP), pl.ds(y, ny))

    def step(self, r, x, n, rows, product):
        kind = self.kind
        at = (x, rows)

        def get(key):
            return r[key + "_here"][at]

        def put(key, value):
            r[key + "_here"][at] = value

        if kind == "exp":
            return jnp.exp(get("warm"))
        if kind == "none":
            return product
        if kind == "dual":
            value = jnp.exp(get("inputs")) / product
            put("d", value)
            return value
        if kind == "grad":
            put("grad", get("d") * product)
            return None
        scale = r["weights"][0]
        half = self.shape[2] // 2
        first = lax.axis_index("inp") == 0
        if kind == "part":
            part = scale * (get("warm") + jnp.log(product))
            put("t", product)
            left, right = part[:, :half], part[:, half:]
            put("keep", jnp.where(first, left, right))
            put("send", jnp.where(first, right, left))
            return None
        own, far = get("cot"), get("far")
        cot = jnp.concatenate([jnp.where(first, own, far), jnp.where(first, far, own)], axis=1)
        return scale * cot / get("t")

    def tiles(self, body):
        def tile_body(tile, carry):
            body(pl.ds(pl.multiple_of(tile * SUB, SUB), SUB))
            return carry

        lax.fori_loop(0, self.shape[1] // SUB, tile_body, 0)

    def finish_x(self, r, x0, reach):
        span = BLOCK * reach

        def sums(ref, rows, put):
            for q in range(0, GROUP, BLOCK):
                window = {m: ref[HALO + x0 + m, rows] for m in range(q - span, q + BLOCK + span)}
                for n in range(q, q + BLOCK):
                    put(n, x_sum(window.get, n, reach))

        def body(rows):
            def put(n, product):
                if self.finish == BOTH:
                    r["work"][n, rows] = product
                    return
                value = self.step(r, x0 + n, n, rows, product)
                if value is not None:
                    r["work"][n, rows] = value

            sums(r["u_ext"], rows, put)

        self.tiles(body)
        if self.finish == BOTH:
            for edge in range(2):
                rows = pl.ds(edge * HALO, HALO)

                def put_edge(n, product):
                    r["edge"][n, rows] = product

                sums(r["y_ext"], rows, put_edge)

    def group(self, r, g):
        nx, ny, nz = self.shape
        groups = nx // GROUP
        work, out = r["work"], r.get("u_out")
        x0 = pl.multiple_of(g * GROUP, GROUP)
        everything = pl.ds(0, ny)

        def finish_y(n):
            if self.finish == BOTH:
                return y_product(r["ky"], work[n], r["edge"][n])
            x = x0 + n
            return y_product(r["ky"], r["u"][x], jnp.concatenate([r["low"][x], r["high"][x]], axis=0))

        if self.finish in (0, BOTH):
            for reach in (1, 2):
                pl.when(r["reach"][0] == reach)(lambda: self.finish_x(r, x0, reach))
        if self.finish == 0:
            if 1 in self.start:
                for n in range(GROUP):
                    work[n] = y_product(r["ky0"], work[n])
        elif 0 in self.start:
            if self.finish == 1:
                for n in range(GROUP):
                    work[n] = finish_y(n)

            def body(rows):
                for q in range(0, GROUP, BLOCK):
                    planes = {}
                    for n in range(q, q + BLOCK):
                        product = work[n, rows] if self.finish == 1 else None
                        planes[n] = self.step(r, x0 + n, n, rows, product)
                    for n in range(q, q + BLOCK):
                        work[n, rows] = x_sum(planes.get, n, 0)

            self.tiles(body)
        else:
            for n in range(GROUP):
                product = finish_y(n) if self.finish in (1, BOTH) else None
                value = self.step(r, x0 + n, n, everything, product)
                if value is not None:
                    work[n] = y_product(r["ky0"], value) if 1 in self.start else value
        shift = HALO if self.send in (0, BOTH) else 0
        if 2 in self.start:
            product = z_product(work[...].reshape(GROUP * ny, nz), r["kz"])
            out[pl.ds(x0 + shift, GROUP)] = product.reshape(GROUP, ny, nz)
        if self.send in (0, BOTH):

            def put_low():
                r["low_out"][...] = out[HALO : 2 * HALO]

            def put_high():
                r["high_out"][...] = out[nx : nx + HALO]

            pl.when(g == 0)(put_low)
            pl.when(g == groups - 1)(put_high)
        if self.send in (1, BOTH):
            low, high = ("y_low_out", "y_high_out") if self.send == BOTH else ("low_out", "high_out")
            r[low][pl.ds(x0, GROUP)] = out[pl.ds(x0 + shift, GROUP), pl.ds(0, HALO)]
            r[high][pl.ds(x0, GROUP)] = out[pl.ds(x0 + shift, GROUP), pl.ds(ny - HALO, HALO)]

    def body(self, r):
        groups = self.shape[0] // GROUP
        planes = lambda g: pl.ds(pl.multiple_of(g * GROUP, GROUP), GROUP)

        reads, writes = self.reads(), self.writes()

        def load(n, g):
            source = r[reads[n]]
            source = source.at[self.place(g)]
            return pltpu.make_async_copy(source, r[reads[n] + "_here"].at[planes(g)], r["sems"].at[n, g])

        def save(n, g):
            target = r[writes[n]]
            target = target.at[self.place(g)]
            sem = r["sems"].at[len(reads) + n, g]
            return pltpu.make_async_copy(r[writes[n] + "_here"].at[planes(g)], target, sem)

        for g in range(groups):
            for n in range(len(reads)):
                load(n, g).start()
        if self.fills:
            fill_z(r["kz"], r["reach"][2])
            if "ky" in r:
                fill_y(r["ky"], r["reach"][1], HALO)
            if "ky0" in r:
                fill_y(r["ky0"], 0, 0)
        if self.finish in (0, BOTH):
            nx = self.shape[0]
            r["u_ext"][0:HALO] = r["low"][...]
            r["u_ext"][HALO + nx : 2 * HALO + nx] = r["high"][...]
        if self.finish == BOTH:
            for n, side in enumerate(("low", "high")):
                rows = pl.ds(n * HALO, HALO)
                r["y_ext"][0:HALO, rows] = r["corner_" + side][0:HALO]
                r["y_ext"][HALO : HALO + nx, rows] = r["y_" + side][...]
                r["y_ext"][HALO + nx : 2 * HALO + nx, rows] = r["corner_" + side][HALO : 2 * HALO]

        def run(g, carry):
            for n in range(len(reads)):
                load(n, g).wait()
            self.group(r, g)
            for n in range(len(writes)):
                save(n, g).start()
            return carry

        lax.fori_loop(0, groups, run, 0)
        for g in range(groups):
            for n in range(len(writes)):
                save(n, g).wait()

    def __call__(self, name, **arrays):
        nx, ny, nz = self.shape
        whole = tuple(n * 2 if line == self.cut else n for line, n in enumerate(self.shape))
        outs = {}
        aliases = {}
        if self.kind == "dual":
            outs["d"] = whole
        if self.kind == "part":
            outs.update(send=(*whole[:2], nz // 2), keep=(*whole[:2], nz // 2), t=whole)
        if self.kind == "grad":
            outs["grad"] = whole
        for n, key in enumerate(arrays):
            if key.endswith("_in"):
                aliases[n] = list(outs).index(key[:-3])
        if self.start:
            outs["u_out"] = self.shape if self.send == 1 else (nx + 2 * HALO, ny, nz)
        if self.send in (0, BOTH):
            outs["low_out"] = outs["high_out"] = (HALO, ny, nz)
        if self.send == 1:
            outs["low_out"] = outs["high_out"] = (nx, HALO, nz)
        if self.send == BOTH:
            outs["y_low_out"] = outs["y_high_out"] = (nx, HALO, nz)
        if self.finish in (0, BOTH):
            outs["u_ext"] = arrays["u"].shape
            aliases[list(arrays).index("u")] = list(outs).index("u_ext")
        if self.fills:
            outs.update(self.matrices())
        scratch = self.scratch()
        names = list(arrays) + list(outs) + list(scratch)
        operands, in_specs = [], []
        for key, value in arrays.items():
            if key in ("weights", "reach"):
                in_specs.append(pl.BlockSpec(memory_space=pltpu.SMEM))
            elif key in INSIDE:
                value = pltpu.with_memory_space_constraint(value, pltpu.VMEM)
                in_specs.append(pl.BlockSpec(memory_space=pltpu.VMEM))
            else:
                in_specs.append(pl.BlockSpec(memory_space=pl.ANY))
            operands.append(value)
        out_shape, out_specs = [], []
        for key, shape in outs.items():
            space = pltpu.VMEM if key in INSIDE else pltpu.HBM
            out_shape.append(space(shape, BF16 if key in MATRICES else F32))
            out_specs.append(pl.BlockSpec(memory_space=space))
        result = pl.pallas_call(
            lambda *refs: self.body(dict(zip(names, refs))),
            name=name,
            out_shape=out_shape,
            in_specs=in_specs,
            out_specs=out_specs,
            input_output_aliases=aliases,
            scratch_shapes=list(scratch.values()),
            compiler_params=pltpu.CompilerParams(vmem_limit_bytes=(16 if self.cut is not None else 20) * 2**20),
            cost_estimate=COST,
        )(*operands)
        return dict(zip(outs, result))


def add_body(keep, arrived, after, out, left, total, sems):
    parts = sems.shape[1]
    step = total.shape[0] // parts
    planes = [pl.ds(n * step, step) for n in range(parts)]
    loads = [pltpu.make_async_copy(keep.at[p], left.at[p], sems.at[0, n]) for n, p in enumerate(planes)]
    saves = [pltpu.make_async_copy(total.at[p], out.at[p], sems.at[1, n]) for n, p in enumerate(planes)]
    for copy in loads:
        copy.start()
    for n, p in enumerate(planes):
        loads[n].wait()
        total[p] = left[p] + arrived[p]
        saves[n].start()
    for copy in saves:
        copy.wait()


def add(keep, arrived, after):
    return pl.pallas_call(
        add_body,
        name="barycenter",
        out_shape=pltpu.HBM(keep.shape, F32),
        in_specs=[pl.BlockSpec(memory_space=space) for space in (pl.ANY, pltpu.VMEM, pl.ANY)],
        out_specs=pl.BlockSpec(memory_space=pltpu.HBM),
        scratch_shapes=[pltpu.VMEM(keep.shape, F32)] * 2 + [pltpu.SemaphoreType.DMA((2, 4))],
        compiler_params=pltpu.CompilerParams(vmem_limit_bytes=10 * 2**20),
        cost_estimate=COST,
    )(keep, pltpu.with_memory_space_constraint(arrived, pltpu.VMEM), after)


AXES = ("pa", "pb")


def neighbours(sizes, line, low, high):
    n = sizes[line]
    up = [(i, i + 1) for i in range(n - 1)]
    down = [(i + 1, i) for i in range(n - 1)]
    return lax.ppermute(high, AXES[line], up), lax.ppermute(low, AXES[line], down)


def corner_body(low, high, top, bottom):
    ny = low.shape[1]
    for n, ref in enumerate((low, high)):
        planes = pl.ds(n * HALO, HALO)
        top[planes] = ref[:, 0:HALO]
        bottom[planes] = ref[:, ny - HALO : ny]


def corners(low, high):
    inside = pl.BlockSpec(memory_space=pltpu.VMEM)
    shape = (2 * HALO, HALO, low.shape[2])
    return pl.pallas_call(
        corner_body,
        name="corners",
        out_shape=[pltpu.VMEM(shape, F32)] * 2,
        in_specs=[inside] * 2,
        out_specs=[inside] * 2,
        compiler_params=pltpu.CompilerParams(vmem_limit_bytes=4 * 2**20),
        cost_estimate=COST,
    )(*(pltpu.with_memory_space_constraint(v, pltpu.VMEM) for v in (low, high)))


def exchange(sizes, line, made):
    if line != BOTH:
        low, high = neighbours(sizes, line, made["low_out"], made["high_out"])
        return dict(u=made["u_out"], low=low, high=high)
    low, high = neighbours(sizes, 0, made["low_out"], made["high_out"])
    y_low, y_high = neighbours(sizes, 1, made["y_low_out"], made["y_high_out"])
    corner_low, corner_high = neighbours(sizes, 1, *corners(low, high))
    halos = (low, high, y_low, y_high, corner_low, corner_high)
    return dict(zip(EDGES, halos), u=made["u_out"])


SWAP = [(0, 1), (1, 0)]


class Case:
    def __init__(self, sizes, line, shape):
        self.sizes = sizes
        self.cut = line if line < 2 else None
        self.pieces = (0, 1) if line < 2 else (0,)
        self.shape = shape
        self.sent, self.begin = ((1, (0, 2)), (0, (1, 2)), (BOTH, (2,)))[line]

    def run(self, matrices, n, name, kind, arrays, fills=False, **form):
        stage = Stage(self.shape, self.cut, n, kind, fills=fills, **form)
        made = stage(f"{name}_{n}", **arrays, **{key: matrices[key] for key in stage.needs()})
        if fills:
            matrices.update({key: made.pop(key) for key in stage.matrices()})
        return made

    def scalings(self, inputs, warm, weights, reach):
        matrices = {}
        begin = dict(start=self.begin, send=self.sent)
        made = {
            n: self.run(matrices, n, "scaling", "exp", dict(warm=warm, reach=reach), fills=n == 0, **begin)
            for n in self.pieces
        }
        arrays = {n: exchange(self.sizes, self.sent, made[n]) for n in made}
        whole = {}
        for n in self.pieces:
            given = dict(inputs=inputs, reach=reach, **arrays[n], **whole)
            made[n] = self.run(matrices, n, "dual", "dual", given, finish=self.sent, **begin)
            whole = dict(d_in=made[n]["d"])
        d = whole["d_in"]
        arrays = {n: exchange(self.sizes, self.sent, made[n]) for n in made}
        whole = {}
        for n in self.pieces:
            given = dict(warm=warm, weights=weights, reach=reach, **arrays[n], **whole)
            part = self.run(matrices, n, "partial", "part", given, finish=self.sent)
            whole = {key + "_in": part[key] for key in ("send", "keep", "t")}
        return part["send"], part["keep"], part["t"], d

    def gradient(self, weights, reach, cotangent, far, t, d):
        matrices, made = {}, {}
        for n in self.pieces:
            given = dict(t=t, weights=weights, far=far, cot=cotangent, reach=reach)
            form = dict(start=self.begin, send=self.sent, fills=n == 0)
            made[n] = self.run(matrices, n, "cotangent", "cot", given, **form)
        arrays = {n: exchange(self.sizes, self.sent, made[n]) for n in made}
        whole = {}
        for n in self.pieces:
            given = dict(d=d, reach=reach, **arrays[n], **whole)
            whole = dict(grad_in=self.run(matrices, n, "gradient", "grad", given, finish=self.sent)["grad"])
        return whole["grad_in"]


def per_device(sizes, log_inputs, warm_potential, bary_weights, band_reach, bary_cotangent):
    shape = log_inputs.shape[1:]
    line = jnp.sum(jnp.where(band_reach == 0, jnp.arange(3, dtype=jnp.int32), 0))
    cases = [Case(sizes, n, shape) for n in range(3)]
    inputs, warm = log_inputs.reshape(shape), warm_potential.reshape(shape)
    far = lax.ppermute(bary_cotangent, "inp", SWAP)
    send, keep, t, d = lax.switch(
        line, [case.scalings for case in cases], inputs, warm, bary_weights, band_reach
    )
    arrived = lax.ppermute(send, "inp", SWAP)
    grad = lax.switch(
        line, [case.gradient for case in cases], bary_weights, band_reach, bary_cotangent, far, t, d
    )
    return (add(keep, arrived, grad), grad[None])


def solution(mesh):
    sizes = (mesh.shape["pa"], mesh.shape["pb"])
    return jax.shard_map(
        functools.partial(per_device, sizes),
        mesh=mesh,
        in_specs=(
            P("inp", "pa", "pb", None),
            P("inp", "pa", "pb", None),
            P("inp"),
            P(),
            P("pa", "pb", "inp"),
        ),
        out_specs=(P("pa", "pb", "inp"), P("inp", "pa", "pb", None)),
        check_vma=False,
    )
```

```python
import functools
import math

import jax
import jax.numpy as jnp
from jax import lax
from jax.experimental import pallas as pl
from jax.experimental.pallas import tpu as pltpu
from jax.sharding import PartitionSpec as P

BLOCK = 4
BLOCK_BITS = 2
HALO = 2 * BLOCK
SIGMA = 3.0
SUB = 8
GROUP = 8
F32 = jnp.float32
BF16 = jnp.bfloat16


def tap(offset):
    gauss = math.exp(-offset * offset / (2.0 * SIGMA * SIGMA)) / (SIGMA * math.sqrt(2.0 * math.pi))
    return 0.5 * gauss + (0.5 if offset == 0 else 0.0)


def weight(i, j, reach):
    offset = (i - j).astype(F32)
    inside = jnp.abs((i >> BLOCK_BITS) - (j >> BLOCK_BITS)) <= reach
    gauss = jnp.exp(-offset * offset / (2.0 * SIGMA * SIGMA)) / (SIGMA * math.sqrt(2.0 * math.pi))
    return jnp.where(i == j, 0.5, 0.0) + 0.5 * jnp.where(inside, gauss, 0.0)


def halves(value):
    high = value.astype(BF16)
    return high, (value - high.astype(F32)).astype(BF16)


def dot(a, b):
    return jnp.dot(a, b, preferred_element_type=F32)


def iotas(shape):
    return (lax.broadcasted_iota(jnp.int32, shape, 0), lax.broadcasted_iota(jnp.int32, shape, 1))


def fill_z(ref, reach):
    n = ref.shape[1]
    i, j = iotas((n, n))
    high, low = halves(weight(i, j, reach))
    ref[0:n] = high
    ref[n : 2 * n] = high
    ref[2 * n : 3 * n] = low


def z_product(rows, kz):
    high, low = halves(rows)
    return dot(jnp.concatenate([high, low, high], axis=1), kz[...])


def y_depth(ny, halo):
    return 3 * (ny + 2 * halo)


def fill_y(ref, reach, halo):
    ny, depth = ref.shape
    i, c = iotas((ny, depth))
    wide = 2 * halo
    own = c < 3 * ny
    size = jnp.where(own, ny, max(wide, 1))
    c = jnp.where(own, c, c - 3 * ny)
    part = jnp.where(c >= 2 * size, 2, jnp.where(c >= size, 1, 0))
    j = c - part * size
    j = jnp.where(own, j, jnp.where(j < halo, j - halo, j - halo + ny))
    value = weight(i + HALO, j + HALO, reach)
    high = value.astype(BF16).astype(F32)
    ref[...] = jnp.where(part == 2, value - high, high).astype(BF16)


def y_product(ky, own, halo=None):
    high, low = halves(own)
    pieces = [high, low, high]
    if halo is not None:
        high, low = halves(halo)
        pieces += [high, low, high]
    return dot(ky[...], jnp.concatenate(pieces, axis=0))


def x_sum(plane, n, reach):
    phase = n % BLOCK
    span = BLOCK * reach
    total = tap(0) * plane(n)
    for d in range(1, span + 1):
        total = total + tap(d) * (plane(n - d) + plane(n + d))
    for d in range(span + 1, span + phase + 1):
        total = total + tap(d) * plane(n - d)
    for d in range(span + 1, span + BLOCK - phase):
        total = total + tap(d) * plane(n + d)
    return total


MATRICES = ("kz", "ky", "ky0")
EDGES = ("low", "high", "y_low", "y_high", "corner_low", "corner_high")
INSIDE = ("warm", "inputs", "t", "d", "t_in", "d_in", "far", "cot", "u", "u_out", "u_ext", *EDGES, *(edge + "_out" for edge in EDGES), *MATRICES)
BOTH = (0, 1)
COST = pl.CostEstimate(flops=1, bytes_accessed=1, transcendentals=0)


class Stage:
    def __init__(self, shape, cut, piece, kind, finish=None, start=(), send=None, fills=False):
        self.cut = cut
        self.piece = piece
        self.shape = tuple(n // 2 if line == cut else n for line, n in enumerate(shape))
        self.kind = kind
        self.finish = finish
        self.start = start
        self.send = send
        self.fills = fills

    def matrices(self):
        nx, ny, nz = self.shape
        shapes = {"kz": (3 * nz, nz)}
        if 1 in self.start:
            shapes["ky0"] = (ny, y_depth(ny, 0))
        else:
            shapes["ky"] = (ny, y_depth(ny, HALO))
        return shapes

    def needs(self):
        if self.fills:
            return ()
        wanted = {"kz": 2 in self.start, "ky": self.finish in (1, BOTH), "ky0": 1 in self.start}
        return tuple(key for key in wanted if wanted[key])

    def scratch(self):
        nx, ny, nz = self.shape
        items = {"work": pltpu.VMEM((GROUP, ny, nz), F32)}
        if self.finish == BOTH:
            items["edge"] = pltpu.VMEM((GROUP, 2 * HALO, nz), F32)
            items["y_ext"] = pltpu.VMEM((nx + 2 * HALO, 2 * HALO, nz), F32)
        for key in self.reads() + self.writes():
            halved = key in ("cot", "far", "send", "keep")
            items[key + "_here"] = pltpu.VMEM((nx, ny, nz // 2 if halved else nz), F32)
        streams = len(self.reads() + self.writes())
        if streams:
            items["sems"] = pltpu.SemaphoreType.DMA((streams, nx // GROUP))
        return items

    def reads(self):
        return ("warm",) if self.kind == "exp" and self.piece == 0 else ()

    def writes(self):
        return {"part": ("send", "keep"), "grad": ("grad",)}.get(self.kind, ())

    def place(self, g):
        nx, ny, _ = self.shape
        x, y = (self.piece * n if self.cut == line else 0 for line, n in enumerate((nx, ny)))
        return (pl.ds(pl.multiple_of(x + g * GROUP, GROUP), GROUP), pl.ds(y, ny))

    def step(self, r, x, n, rows, product):
        kind = self.kind
        at = (x, rows)

        there = (self.piece * self.shape[0] + x if self.cut == 0 else x, rows)

        def get(key):
            return r[key + "_here"][at] if key in self.reads() else r[key][there]

        def put(key, value):
            if key in self.writes():
                r[key + "_here"][at] = value
            else:
                r[key][there] = value

        if kind == "exp":
            return jnp.exp(get("warm"))
        if kind == "none":
            return product
        if kind == "dual":
            value = jnp.exp(get("inputs")) / product
            put("d", value)
            return value
        if kind == "grad":
            put("grad", get("d") * product)
            return None
        scale = r["weights"][0]
        half = self.shape[2] // 2
        first = lax.axis_index("inp") == 0
        if kind == "part":
            part = scale * (get("warm") + jnp.log(product))
            put("t", product)
            left, right = part[:, :half], part[:, half:]
            put("keep", jnp.where(first, left, right))
            put("send", jnp.where(first, right, left))
            return None
        own, far = get("cot"), get("far")
        cot = jnp.concatenate([jnp.where(first, own, far), jnp.where(first, far, own)], axis=1)
        return scale * cot / get("t")

    def tiles(self, body):
        def tile_body(tile, carry):
            body(pl.ds(pl.multiple_of(tile * SUB, SUB), SUB))
            return carry

        lax.fori_loop(0, self.shape[1] // SUB, tile_body, 0)

    def finish_x(self, r, x0, reach):
        span = BLOCK * reach

        def sums(ref, rows, put):
            for q in range(0, GROUP, BLOCK):
                window = {m: ref[HALO + x0 + m, rows] for m in range(q - span, q + BLOCK + span)}
                for n in range(q, q + BLOCK):
                    put(n, x_sum(window.get, n, reach))

        def body(rows):
            def put(n, product):
                if self.finish == BOTH:
                    r["work"][n, rows] = product
                    return
                value = self.step(r, x0 + n, n, rows, product)
                if value is not None:
                    r["work"][n, rows] = value

            sums(r["u_ext"], rows, put)

        self.tiles(body)
        if self.finish == BOTH:
            for edge in range(2):
                rows = pl.ds(edge * HALO, HALO)

                def put_edge(n, product):
                    r["edge"][n, rows] = product

                sums(r["y_ext"], rows, put_edge)

    def group(self, r, g):
        nx, ny, nz = self.shape
        groups = nx // GROUP
        work, out = r["work"], r.get("u_out")
        x0 = pl.multiple_of(g * GROUP, GROUP)
        everything = pl.ds(0, ny)

        def finish_y(n):
            if self.finish == BOTH:
                return y_product(r["ky"], work[n], r["edge"][n])
            x = x0 + n
            return y_product(r["ky"], r["u"][x], jnp.concatenate([r["low"][x], r["high"][x]], axis=0))

        if self.finish in (0, BOTH):
            for reach in (1, 2):
                pl.when(r["reach"][0] == reach)(lambda: self.finish_x(r, x0, reach))
        if self.finish == 0:
            if 1 in self.start:
                for n in range(GROUP):
                    work[n] = y_product(r["ky0"], work[n])
        elif 0 in self.start:
            if self.finish == 1:
                for n in range(GROUP):
                    work[n] = finish_y(n)

            def body(rows):
                for q in range(0, GROUP, BLOCK):
                    planes = {}
                    for n in range(q, q + BLOCK):
                        product = work[n, rows] if self.finish == 1 else None
                        planes[n] = self.step(r, x0 + n, n, rows, product)
                    for n in range(q, q + BLOCK):
                        work[n, rows] = x_sum(planes.get, n, 0)

            self.tiles(body)
        else:
            for n in range(GROUP):
                product = finish_y(n) if self.finish in (1, BOTH) else None
                value = self.step(r, x0 + n, n, everything, product)
                if value is not None:
                    work[n] = y_product(r["ky0"], value) if 1 in self.start else value
        shift = HALO if self.send in (0, BOTH) else 0
        if 2 in self.start:
            product = z_product(work[...].reshape(GROUP * ny, nz), r["kz"])
            out[pl.ds(x0 + shift, GROUP)] = product.reshape(GROUP, ny, nz)
        if self.send in (0, BOTH):

            def put_low():
                r["low_out"][...] = out[HALO : 2 * HALO]

            def put_high():
                r["high_out"][...] = out[nx : nx + HALO]

            pl.when(g == 0)(put_low)
            pl.when(g == groups - 1)(put_high)
        if self.send in (1, BOTH):
            low, high = ("y_low_out", "y_high_out") if self.send == BOTH else ("low_out", "high_out")
            r[low][pl.ds(x0, GROUP)] = out[pl.ds(x0 + shift, GROUP), pl.ds(0, HALO)]
            r[high][pl.ds(x0, GROUP)] = out[pl.ds(x0 + shift, GROUP), pl.ds(ny - HALO, HALO)]

    def body(self, r):
        groups = self.shape[0] // GROUP
        planes = lambda g: pl.ds(pl.multiple_of(g * GROUP, GROUP), GROUP)

        reads, writes = self.reads(), self.writes()

        def load(n, g):
            source = r[reads[n]]
            source = source.at[self.place(g)]
            return pltpu.make_async_copy(source, r[reads[n] + "_here"].at[planes(g)], r["sems"].at[n, g])

        def save(n, g):
            target = r[writes[n]]
            target = target.at[self.place(g)]
            sem = r["sems"].at[len(reads) + n, g]
            return pltpu.make_async_copy(r[writes[n] + "_here"].at[planes(g)], target, sem)

        for g in range(groups):
            for n in range(len(reads)):
                load(n, g).start()
        if self.fills:
            fill_z(r["kz"], r["reach"][2])
            if "ky" in r:
                fill_y(r["ky"], r["reach"][1], HALO)
            if "ky0" in r:
                fill_y(r["ky0"], 0, 0)
        if self.finish in (0, BOTH):
            nx = self.shape[0]
            r["u_ext"][0:HALO] = r["low"][...]
            r["u_ext"][HALO + nx : 2 * HALO + nx] = r["high"][...]
        if self.finish == BOTH:
            for n, side in enumerate(("low", "high")):
                rows = pl.ds(n * HALO, HALO)
                r["y_ext"][0:HALO, rows] = r["corner_" + side][0:HALO]
                r["y_ext"][HALO : HALO + nx, rows] = r["y_" + side][...]
                r["y_ext"][HALO + nx : 2 * HALO + nx, rows] = r["corner_" + side][HALO : 2 * HALO]

        def run(g, carry):
            for n in range(len(reads)):
                load(n, g).wait()
            self.group(r, g)
            for n in range(len(writes)):
                save(n, g).start()
            return carry

        lax.fori_loop(0, groups, run, 0)
        for g in range(groups):
            for n in range(len(writes)):
                save(n, g).wait()

    def __call__(self, name, **arrays):
        nx, ny, nz = self.shape
        whole = tuple(n * 2 if line == self.cut else n for line, n in enumerate(self.shape))
        outs = {}
        aliases = {}
        if self.kind == "dual":
            outs["d"] = whole
        if self.kind == "part":
            outs.update(send=(*whole[:2], nz // 2), keep=(*whole[:2], nz // 2), t=whole)
        if self.kind == "grad":
            outs["grad"] = whole
        for n, key in enumerate(arrays):
            if key.endswith("_in"):
                aliases[n] = list(outs).index(key[:-3])
        if self.start:
            outs["u_out"] = self.shape if self.send == 1 else (nx + 2 * HALO, ny, nz)
        if self.send in (0, BOTH):
            outs["low_out"] = outs["high_out"] = (HALO, ny, nz)
        if self.send == 1:
            outs["low_out"] = outs["high_out"] = (nx, HALO, nz)
        if self.send == BOTH:
            outs["y_low_out"] = outs["y_high_out"] = (nx, HALO, nz)
        if self.finish in (0, BOTH):
            outs["u_ext"] = arrays["u"].shape
            aliases[list(arrays).index("u")] = list(outs).index("u_ext")
        if self.fills:
            outs.update(self.matrices())
        scratch = self.scratch()
        names = list(arrays) + list(outs) + list(scratch)
        operands, in_specs = [], []
        stage_reads = self.reads()
        for key, value in arrays.items():
            if key in ("weights", "reach"):
                in_specs.append(pl.BlockSpec(memory_space=pltpu.SMEM))
            elif key in INSIDE and key not in stage_reads:
                value = pltpu.with_memory_space_constraint(value, pltpu.VMEM)
                in_specs.append(pl.BlockSpec(memory_space=pltpu.VMEM))
            else:
                in_specs.append(pl.BlockSpec(memory_space=pl.ANY))
            operands.append(value)
        out_shape, out_specs = [], []
        for key, shape in outs.items():
            space = pltpu.VMEM if key in INSIDE else pltpu.HBM
            out_shape.append(space(shape, BF16 if key in MATRICES else F32))
            out_specs.append(pl.BlockSpec(memory_space=space))
        result = pl.pallas_call(
            lambda *refs: self.body(dict(zip(names, refs))),
            name=name,
            out_shape=out_shape,
            in_specs=in_specs,
            out_specs=out_specs,
            input_output_aliases=aliases,
            scratch_shapes=list(scratch.values()),
            compiler_params=pltpu.CompilerParams(vmem_limit_bytes=16 * 2**20),
            cost_estimate=COST,
        )(*operands)
        return dict(zip(outs, result))


def add_body(keep, arrived, after, out, total, sems):
    parts = sems.shape[0]
    step = total.shape[0] // parts
    copies = []
    for n in range(parts):
        planes = pl.ds(n * step, step)
        total[planes] = keep[planes] + arrived[planes]
        copies.append(pltpu.make_async_copy(total.at[planes], out.at[planes], sems.at[n]))
        copies[-1].start()
    for copy in copies:
        copy.wait()


def add(keep, arrived, after):
    in_vmem = [pltpu.with_memory_space_constraint(v, pltpu.VMEM) for v in (keep, arrived)]
    return pl.pallas_call(
        add_body,
        name="barycenter",
        out_shape=pltpu.HBM(keep.shape, F32),
        in_specs=[pl.BlockSpec(memory_space=space) for space in (pltpu.VMEM, pltpu.VMEM, pl.ANY)],
        out_specs=pl.BlockSpec(memory_space=pltpu.HBM),
        scratch_shapes=[pltpu.VMEM(keep.shape, F32), pltpu.SemaphoreType.DMA((4,))],
        compiler_params=pltpu.CompilerParams(vmem_limit_bytes=10 * 2**20),
        cost_estimate=COST,
    )(*in_vmem, after)


AXES = ("pa", "pb")


def neighbours(sizes, line, low, high):
    n = sizes[line]
    up = [(i, i + 1) for i in range(n - 1)]
    down = [(i + 1, i) for i in range(n - 1)]
    return lax.ppermute(high, AXES[line], up), lax.ppermute(low, AXES[line], down)


def corner_body(low, high, top, bottom):
    ny = low.shape[1]
    for n, ref in enumerate((low, high)):
        planes = pl.ds(n * HALO, HALO)
        top[planes] = ref[:, 0:HALO]
        bottom[planes] = ref[:, ny - HALO : ny]


def corners(low, high):
    inside = pl.BlockSpec(memory_space=pltpu.VMEM)
    shape = (2 * HALO, HALO, low.shape[2])
    return pl.pallas_call(
        corner_body,
        name="corners",
        out_shape=[pltpu.VMEM(shape, F32)] * 2,
        in_specs=[inside] * 2,
        out_specs=[inside] * 2,
        compiler_params=pltpu.CompilerParams(vmem_limit_bytes=4 * 2**20),
        cost_estimate=COST,
    )(*(pltpu.with_memory_space_constraint(v, pltpu.VMEM) for v in (low, high)))


def exchange(sizes, line, made):
    if line != BOTH:
        low, high = neighbours(sizes, line, made["low_out"], made["high_out"])
        return dict(u=made["u_out"], low=low, high=high)
    low, high = neighbours(sizes, 0, made["low_out"], made["high_out"])
    y_low, y_high = neighbours(sizes, 1, made["y_low_out"], made["y_high_out"])
    corner_low, corner_high = neighbours(sizes, 1, *corners(low, high))
    halos = (low, high, y_low, y_high, corner_low, corner_high)
    return dict(zip(EDGES, halos), u=made["u_out"])


SWAP = [(0, 1), (1, 0)]


class Case:
    def __init__(self, sizes, line, shape):
        self.sizes = sizes
        self.cut = 0 if line == 0 else None
        self.pieces = (0, 1) if line == 0 else (0,)
        self.shape = shape
        self.sent, self.begin = ((1, (0, 2)), (0, (1, 2)), (BOTH, (2,)))[line]

    def run(self, matrices, n, name, kind, arrays, fills=False, **form):
        stage = Stage(self.shape, self.cut, n, kind, fills=fills, **form)
        made = stage(f"{name}_{n}", **arrays, **{key: matrices[key] for key in stage.needs()})
        if fills:
            matrices.update({key: made.pop(key) for key in stage.matrices()})
        return made

    def scalings(self, inputs, warm, weights, reach):
        matrices = {}
        begin = dict(start=self.begin, send=self.sent)
        made = {
            n: self.run(matrices, n, "scaling", "exp", dict(warm=warm, reach=reach), fills=n == 0, **begin)
            for n in self.pieces
        }
        arrays = {n: exchange(self.sizes, self.sent, made[n]) for n in made}
        whole = {}
        for n in self.pieces:
            given = dict(inputs=inputs, reach=reach, **arrays[n], **whole)
            made[n] = self.run(matrices, n, "dual", "dual", given, finish=self.sent, **begin)
            whole = dict(d_in=made[n]["d"])
        d = whole["d_in"]
        arrays = {n: exchange(self.sizes, self.sent, made[n]) for n in made}
        whole = {}
        for n in self.pieces:
            given = dict(warm=warm, weights=weights, reach=reach, **arrays[n], **whole)
            part = self.run(matrices, n, "partial", "part", given, finish=self.sent)
            whole = {key + "_in": part[key] for key in ("send", "keep", "t")}
        return part["send"], part["keep"], part["t"], d

    def gradient(self, weights, reach, cotangent, far, t, d):
        matrices, made = {}, {}
        for n in self.pieces:
            given = dict(t=t, weights=weights, far=far, cot=cotangent, reach=reach)
            form = dict(start=self.begin, send=self.sent, fills=n == 0)
            made[n] = self.run(matrices, n, "cotangent", "cot", given, **form)
        arrays = {n: exchange(self.sizes, self.sent, made[n]) for n in made}
        whole = {}
        for n in self.pieces:
            given = dict(d=d, reach=reach, **arrays[n], **whole)
            whole = dict(grad_in=self.run(matrices, n, "gradient", "grad", given, finish=self.sent)["grad"])
        return whole["grad_in"]


def per_device(sizes, log_inputs, warm_potential, bary_weights, band_reach, bary_cotangent):
    shape = log_inputs.shape[1:]
    line = jnp.sum(jnp.where(band_reach == 0, jnp.arange(3, dtype=jnp.int32), 0))
    cases = [Case(sizes, n, shape) for n in range(3)]
    inputs, warm = log_inputs.reshape(shape), warm_potential.reshape(shape)
    far = lax.ppermute(bary_cotangent, "inp", SWAP)
    send, keep, t, d = lax.switch(
        line, [case.scalings for case in cases], inputs, warm, bary_weights, band_reach
    )
    arrived = lax.ppermute(send, "inp", SWAP)
    grad = lax.switch(
        line, [case.gradient for case in cases], bary_weights, band_reach, bary_cotangent, far, t, d
    )
    return (add(keep, arrived, grad), grad[None])


def solution(mesh):
    sizes = (mesh.shape["pa"], mesh.shape["pb"])
    return jax.shard_map(
        functools.partial(per_device, sizes),
        mesh=mesh,
        in_specs=(
            P("inp", "pa", "pb", None),
            P("inp", "pa", "pb", None),
            P("inp"),
            P(),
            P("pa", "pb", "inp"),
        ),
        out_specs=(P("pa", "pb", "inp"), P("inp", "pa", "pb", None)),
        check_vma=False,
    )
```

```python
import functools
import math

import jax
import jax.numpy as jnp
from jax import lax
from jax.experimental import pallas as pl
from jax.experimental.pallas import tpu as pltpu
from jax.sharding import PartitionSpec as P

BLOCK = 4
BLOCK_BITS = 2
HALO = 2 * BLOCK
SIGMA = 3.0
SUB = 8
GROUP = 8
F32 = jnp.float32
BF16 = jnp.bfloat16


def tap(offset):
    gauss = math.exp(-offset * offset / (2.0 * SIGMA * SIGMA)) / (SIGMA * math.sqrt(2.0 * math.pi))
    return 0.5 * gauss + (0.5 if offset == 0 else 0.0)


def weight(i, j, reach):
    offset = (i - j).astype(F32)
    inside = jnp.abs((i >> BLOCK_BITS) - (j >> BLOCK_BITS)) <= reach
    gauss = jnp.exp(-offset * offset / (2.0 * SIGMA * SIGMA)) / (SIGMA * math.sqrt(2.0 * math.pi))
    return jnp.where(i == j, 0.5, 0.0) + 0.5 * jnp.where(inside, gauss, 0.0)


def halves(value):
    high = value.astype(BF16)
    return high, (value - high.astype(F32)).astype(BF16)


def dot(a, b):
    return jnp.dot(a, b, preferred_element_type=F32)


AXES = ("pa", "pb")


def parity(line):
    return lax.rem(lax.axis_index(AXES[line]), 2)


def edge(line, swap, size, first=0):
    return pl.ds(pl.multiple_of(first + jnp.where(parity(line) == swap, size - HALO, 0), HALO), HALO)


def iotas(shape):
    return (lax.broadcasted_iota(jnp.int32, shape, 0), lax.broadcasted_iota(jnp.int32, shape, 1))


def fill_z(ref, reach):
    n = ref.shape[1]
    i, j = iotas((n, n))
    high, low = halves(weight(i, j, reach))
    ref[0:n] = high
    ref[n : 2 * n] = high
    ref[2 * n : 3 * n] = low


def z_product(rows, kz):
    high, low = halves(rows)
    return dot(jnp.concatenate([high, low, high], axis=1), kz[...])


def y_depth(ny, halo):
    return 3 * (ny + 2 * halo)


def fill_y(ref, reach, halo):
    ny, depth = ref.shape
    i, c = iotas((ny, depth))
    wide = 2 * halo
    own = c < 3 * ny
    size = jnp.where(own, ny, max(wide, 1))
    c = jnp.where(own, c, c - 3 * ny)
    part = jnp.where(c >= 2 * size, 2, jnp.where(c >= size, 1, 0))
    j = c - part * size
    if halo:
        swap = jnp.where(j >= halo, 1, 0)
        e = j - swap * halo
        j = jnp.where(own, j, jnp.where(swap == parity(1), ny + e, e - halo))
    value = weight(i + HALO, j + HALO, reach)
    high = value.astype(BF16).astype(F32)
    ref[...] = jnp.where(part == 2, value - high, high).astype(BF16)


def y_product(ky, own, halo=None):
    high, low = halves(own)
    pieces = [high, low, high]
    if halo is not None:
        high, low = halves(halo)
        pieces += [high, low, high]
    return dot(ky[...], jnp.concatenate(pieces, axis=0))


def x_sum(plane, n, reach):
    phase = n % BLOCK
    span = BLOCK * reach
    total = tap(0) * plane(n)
    for d in range(1, span + 1):
        total = total + tap(d) * (plane(n - d) + plane(n + d))
    for d in range(span + 1, span + phase + 1):
        total = total + tap(d) * plane(n - d)
    for d in range(span + 1, span + BLOCK - phase):
        total = total + tap(d) * plane(n + d)
    return total


MATRICES = ("kz", "ky", "ky0")
EDGES = ("even", "odd", "y_even", "y_odd", "corner_even", "corner_odd")
INSIDE = ("warm", "inputs", "t", "d", "t_in", "d_in", "far", "cot", "u", "u_out", "u_ext", *EDGES, *(edge + "_out" for edge in EDGES), *MATRICES)
BOTH = (0, 1)
COST = pl.CostEstimate(flops=1, bytes_accessed=1, transcendentals=0)


class Stage:
    def __init__(self, shape, cut, piece, kind, finish=None, start=(), send=None, fills=False):
        self.cut = cut
        self.piece = piece
        self.shape = tuple(n // 2 if line == cut else n for line, n in enumerate(shape))
        self.kind = kind
        self.finish = finish
        self.start = start
        self.send = send
        self.fills = fills

    def matrices(self):
        nx, ny, nz = self.shape
        shapes = {"kz": (3 * nz, nz)}
        if 1 in self.start:
            shapes["ky0"] = (ny, y_depth(ny, 0))
        else:
            shapes["ky"] = (ny, y_depth(ny, HALO))
        return shapes

    def needs(self):
        if self.fills:
            return ()
        wanted = {"kz": 2 in self.start, "ky": self.finish in (1, BOTH), "ky0": 1 in self.start}
        return tuple(key for key in wanted if wanted[key])

    def scratch(self):
        nx, ny, nz = self.shape
        items = {"work": pltpu.VMEM((GROUP, ny, nz), F32)}
        if self.finish == BOTH:
            items["edge"] = pltpu.VMEM((GROUP, 2 * HALO, nz), F32)
            items["y_ext"] = pltpu.VMEM((nx + 2 * HALO, 2 * HALO, nz), F32)
        for key in self.reads() + self.writes():
            halved = key in ("cot", "far", "send", "keep")
            items[key + "_here"] = pltpu.VMEM((nx, ny, nz // 2 if halved else nz), F32)
        streams = len(self.reads() + self.writes())
        if streams:
            items["sems"] = pltpu.SemaphoreType.DMA((streams, nx // GROUP))
        return items

    def reads(self):
        return ("warm",) if self.kind == "exp" and self.piece == 0 else ()

    def writes(self):
        return {"part": ("send", "keep"), "grad": ("grad",)}.get(self.kind, ())

    def place(self, g):
        nx, ny, _ = self.shape
        x, y = (self.piece * n if self.cut == line else 0 for line, n in enumerate((nx, ny)))
        return (pl.ds(pl.multiple_of(x + g * GROUP, GROUP), GROUP), pl.ds(y, ny))

    def step(self, r, x, n, rows, product):
        kind = self.kind
        at = (x, rows)

        there = (self.piece * self.shape[0] + x if self.cut == 0 else x, rows)

        def get(key):
            return r[key + "_here"][at] if key in self.reads() else r[key][there]

        def put(key, value):
            if key in self.writes():
                r[key + "_here"][at] = value
            else:
                r[key][there] = value

        if kind == "exp":
            return jnp.exp(get("warm"))
        if kind == "none":
            return product
        if kind == "dual":
            value = jnp.exp(get("inputs")) / product
            put("d", value)
            return value
        if kind == "grad":
            put("grad", get("d") * product)
            return None
        scale = r["weights"][0]
        half = self.shape[2] // 2
        first = lax.axis_index("inp") == 0
        if kind == "part":
            part = scale * (get("warm") + jnp.log(product))
            put("t", product)
            left, right = part[:, :half], part[:, half:]
            put("keep", jnp.where(first, left, right))
            put("send", jnp.where(first, right, left))
            return None
        own, far = get("cot"), get("far")
        cot = jnp.concatenate([jnp.where(first, own, far), jnp.where(first, far, own)], axis=1)
        return scale * cot / get("t")

    def tiles(self, body):
        def tile_body(tile, carry):
            body(pl.ds(pl.multiple_of(tile * SUB, SUB), SUB))
            return carry

        lax.fori_loop(0, self.shape[1] // SUB, tile_body, 0)

    def finish_x(self, r, x0, reach):
        span = BLOCK * reach

        def sums(ref, rows, put):
            for q in range(0, GROUP, BLOCK):
                window = {m: ref[HALO + x0 + m, rows] for m in range(q - span, q + BLOCK + span)}
                for n in range(q, q + BLOCK):
                    put(n, x_sum(window.get, n, reach))

        def body(rows):
            def put(n, product):
                if self.finish == BOTH:
                    r["work"][n, rows] = product
                    return
                value = self.step(r, x0 + n, n, rows, product)
                if value is not None:
                    r["work"][n, rows] = value

            sums(r["u_ext"], rows, put)

        self.tiles(body)
        if self.finish == BOTH:
            for swap in range(2):
                rows = pl.ds(swap * HALO, HALO)

                def put_edge(n, product):
                    r["edge"][n, rows] = product

                sums(r["y_ext"], rows, put_edge)

    def group(self, r, g):
        nx, ny, nz = self.shape
        groups = nx // GROUP
        work, out = r["work"], r.get("u_out")
        x0 = pl.multiple_of(g * GROUP, GROUP)
        everything = pl.ds(0, ny)

        def finish_y(n):
            if self.finish == BOTH:
                return y_product(r["ky"], work[n], r["edge"][n])
            x = x0 + n
            return y_product(r["ky"], r["u"][x], jnp.concatenate([r["even"][x], r["odd"][x]], axis=0))

        if self.finish in (0, BOTH):
            for reach in (1, 2):
                pl.when(r["reach"][0] == reach)(lambda: self.finish_x(r, x0, reach))
        if self.finish == 0:
            if 1 in self.start:
                for n in range(GROUP):
                    work[n] = y_product(r["ky0"], work[n])
        elif 0 in self.start:
            if self.finish == 1:
                for n in range(GROUP):
                    work[n] = finish_y(n)

            def body(rows):
                for q in range(0, GROUP, BLOCK):
                    planes = {}
                    for n in range(q, q + BLOCK):
                        product = work[n, rows] if self.finish == 1 else None
                        planes[n] = self.step(r, x0 + n, n, rows, product)
                    for n in range(q, q + BLOCK):
                        work[n, rows] = x_sum(planes.get, n, 0)

            self.tiles(body)
        else:
            for n in range(GROUP):
                product = finish_y(n) if self.finish in (1, BOTH) else None
                value = self.step(r, x0 + n, n, everything, product)
                if value is not None:
                    work[n] = y_product(r["ky0"], value) if 1 in self.start else value
        shift = HALO if self.send in (0, BOTH) else 0
        if 2 in self.start:
            product = z_product(work[...].reshape(GROUP * ny, nz), r["kz"])
            out[pl.ds(x0 + shift, GROUP)] = product.reshape(GROUP, ny, nz)
        if self.send in (1, BOTH):
            names = ("y_even_out", "y_odd_out") if self.send == BOTH else ("even_out", "odd_out")
            for swap, name in enumerate(names):
                r[name][pl.ds(x0, GROUP)] = out[pl.ds(x0 + shift, GROUP), edge(1, swap, ny)]

    def body(self, r):
        groups = self.shape[0] // GROUP
        planes = lambda g: pl.ds(pl.multiple_of(g * GROUP, GROUP), GROUP)

        reads, writes = self.reads(), self.writes()

        def load(n, g):
            source = r[reads[n]]
            source = source.at[self.place(g)]
            return pltpu.make_async_copy(source, r[reads[n] + "_here"].at[planes(g)], r["sems"].at[n, g])

        def save(n, g):
            target = r[writes[n]]
            target = target.at[self.place(g)]
            sem = r["sems"].at[len(reads) + n, g]
            return pltpu.make_async_copy(r[writes[n] + "_here"].at[planes(g)], target, sem)

        for g in range(groups):
            for n in range(len(reads)):
                load(n, g).start()
        if self.fills:
            fill_z(r["kz"], r["reach"][2])
            if "ky" in r:
                fill_y(r["ky"], r["reach"][1], HALO)
            if "ky0" in r:
                fill_y(r["ky0"], 0, 0)
        if self.finish in (0, BOTH):
            nx = self.shape[0]
            ends = [edge(0, swap, nx + 2 * HALO) for swap in range(2)]
            for end, name in zip(ends, ("even", "odd")):
                r["u_ext"][end] = r[name][...]
            if self.finish == BOTH:
                for swap, name in enumerate(("even", "odd")):
                    rows = pl.ds(swap * HALO, HALO)
                    r["y_ext"][HALO : HALO + nx, rows] = r["y_" + name][...]
                    for n, end in enumerate(ends):
                        r["y_ext"][end, rows] = r["corner_" + name][n * HALO : (n + 1) * HALO]

        def run(g, carry):
            for n in range(len(reads)):
                load(n, g).wait()
            self.group(r, g)
            for n in range(len(writes)):
                save(n, g).start()
            return carry

        lax.fori_loop(0, groups, run, 0)
        if self.send in (0, BOTH):
            for swap, name in enumerate(("even_out", "odd_out")):
                r[name][...] = r["u_out"][edge(0, swap, self.shape[0], HALO)]
        for g in range(groups):
            for n in range(len(writes)):
                save(n, g).wait()

    def __call__(self, name, **arrays):
        nx, ny, nz = self.shape
        whole = tuple(n * 2 if line == self.cut else n for line, n in enumerate(self.shape))
        outs = {}
        aliases = {}
        if self.kind == "dual":
            outs["d"] = whole
        if self.kind == "part":
            outs.update(send=(*whole[:2], nz // 2), keep=(*whole[:2], nz // 2), t=whole)
        if self.kind == "grad":
            outs["grad"] = whole
        for n, key in enumerate(arrays):
            if key.endswith("_in"):
                aliases[n] = list(outs).index(key[:-3])
        if self.start:
            outs["u_out"] = self.shape if self.send == 1 else (nx + 2 * HALO, ny, nz)
        if self.send in (0, BOTH):
            outs["even_out"] = outs["odd_out"] = (HALO, ny, nz)
        if self.send == 1:
            outs["even_out"] = outs["odd_out"] = (nx, HALO, nz)
        if self.send == BOTH:
            outs["y_even_out"] = outs["y_odd_out"] = (nx, HALO, nz)
        if self.finish in (0, BOTH):
            outs["u_ext"] = arrays["u"].shape
            aliases[list(arrays).index("u")] = list(outs).index("u_ext")
        if self.fills:
            outs.update(self.matrices())
        scratch = self.scratch()
        names = list(arrays) + list(outs) + list(scratch)
        operands, in_specs = [], []
        stage_reads = self.reads()
        for key, value in arrays.items():
            if key in ("weights", "reach"):
                in_specs.append(pl.BlockSpec(memory_space=pltpu.SMEM))
            elif key in INSIDE and key not in stage_reads:
                value = pltpu.with_memory_space_constraint(value, pltpu.VMEM)
                in_specs.append(pl.BlockSpec(memory_space=pltpu.VMEM))
            else:
                in_specs.append(pl.BlockSpec(memory_space=pl.ANY))
            operands.append(value)
        out_shape, out_specs = [], []
        for key, shape in outs.items():
            space = pltpu.VMEM if key in INSIDE else pltpu.HBM
            out_shape.append(space(shape, BF16 if key in MATRICES else F32))
            out_specs.append(pl.BlockSpec(memory_space=space))
        result = pl.pallas_call(
            lambda *refs: self.body(dict(zip(names, refs))),
            name=name,
            out_shape=out_shape,
            in_specs=in_specs,
            out_specs=out_specs,
            input_output_aliases=aliases,
            scratch_shapes=list(scratch.values()),
            compiler_params=pltpu.CompilerParams(vmem_limit_bytes=(10 if "sems" in scratch else 6) * 2**20),
            cost_estimate=COST,
        )(*operands)
        return dict(zip(outs, result))


def add_body(keep, arrived, after, out, total, sems):
    parts = sems.shape[0]
    step = total.shape[0] // parts
    copies = []
    for n in range(parts):
        planes = pl.ds(n * step, step)
        total[planes] = keep[planes] + arrived[planes]
        copies.append(pltpu.make_async_copy(total.at[planes], out.at[planes], sems.at[n]))
        copies[-1].start()
    for copy in copies:
        copy.wait()


def add(keep, arrived, after):
    in_vmem = [pltpu.with_memory_space_constraint(v, pltpu.VMEM) for v in (keep, arrived)]
    return pl.pallas_call(
        add_body,
        name="barycenter",
        out_shape=pltpu.HBM(keep.shape, F32),
        in_specs=[pl.BlockSpec(memory_space=space) for space in (pltpu.VMEM, pltpu.VMEM, pl.ANY)],
        out_specs=pl.BlockSpec(memory_space=pltpu.HBM),
        scratch_shapes=[pltpu.VMEM(keep.shape, F32), pltpu.SemaphoreType.DMA((4,))],
        compiler_params=pltpu.CompilerParams(vmem_limit_bytes=10 * 2**20),
        cost_estimate=COST,
    )(*in_vmem, after)


def neighbours(sizes, line, even, odd):
    made = []
    for first, value in enumerate((even, odd)):
        pairs = [(i, i + 1) for i in range(first, sizes[line] - 1, 2)]
        made.append(lax.ppermute(value, AXES[line], pairs + [(j, i) for i, j in pairs]))
    return made


def corner_body(even, odd, *outs):
    ny = even.shape[1]
    for swap, out in enumerate(outs):
        for n, ref in enumerate((even, odd)):
            out[pl.ds(n * HALO, HALO)] = ref[:, edge(1, swap, ny)]


def corners(even, odd):
    inside = pl.BlockSpec(memory_space=pltpu.VMEM)
    shape = (2 * HALO, HALO, even.shape[2])
    return pl.pallas_call(
        corner_body,
        name="corners",
        out_shape=[pltpu.VMEM(shape, F32)] * 2,
        in_specs=[inside] * 2,
        out_specs=[inside] * 2,
        compiler_params=pltpu.CompilerParams(vmem_limit_bytes=4 * 2**20),
        cost_estimate=COST,
    )(*(pltpu.with_memory_space_constraint(v, pltpu.VMEM) for v in (even, odd)))


def exchange(sizes, line, made):
    if line != BOTH:
        even, odd = neighbours(sizes, line, made["even_out"], made["odd_out"])
        return dict(u=made["u_out"], even=even, odd=odd)
    even, odd = neighbours(sizes, 0, made["even_out"], made["odd_out"])
    y_even, y_odd = neighbours(sizes, 1, made["y_even_out"], made["y_odd_out"])
    corner_even, corner_odd = neighbours(sizes, 1, *corners(even, odd))
    halos = (even, odd, y_even, y_odd, corner_even, corner_odd)
    return dict(zip(EDGES, halos), u=made["u_out"])


SWAP = [(0, 1), (1, 0)]


class Case:
    def __init__(self, sizes, line, shape):
        self.sizes = sizes
        self.cut = 0 if line == 0 else None
        self.pieces = (0, 1) if line == 0 else (0,)
        self.shape = shape
        self.sent, self.begin = ((1, (0, 2)), (0, (1, 2)), (BOTH, (2,)))[line]

    def run(self, matrices, n, name, kind, arrays, fills=False, **form):
        stage = Stage(self.shape, self.cut, n, kind, fills=fills, **form)
        made = stage(f"{name}_{n}", **arrays, **{key: matrices[key] for key in stage.needs()})
        if fills:
            matrices.update({key: made.pop(key) for key in stage.matrices()})
        return made

    def scalings(self, inputs, warm, weights, reach):
        matrices = {}
        begin = dict(start=self.begin, send=self.sent)
        made = {
            n: self.run(matrices, n, "scaling", "exp", dict(warm=warm, reach=reach), fills=n == 0, **begin)
            for n in self.pieces
        }
        arrays = {n: exchange(self.sizes, self.sent, made[n]) for n in made}
        whole = {}
        for n in self.pieces:
            given = dict(inputs=inputs, reach=reach, **arrays[n], **whole)
            made[n] = self.run(matrices, n, "dual", "dual", given, finish=self.sent, **begin)
            whole = dict(d_in=made[n]["d"])
        d = whole["d_in"]
        arrays = {n: exchange(self.sizes, self.sent, made[n]) for n in made}
        whole = {}
        for n in self.pieces:
            given = dict(warm=warm, weights=weights, reach=reach, **arrays[n], **whole)
            part = self.run(matrices, n, "partial", "part", given, finish=self.sent)
            whole = {key + "_in": part[key] for key in ("send", "keep", "t")}
        return part["send"], part["keep"], part["t"], d

    def gradient(self, weights, reach, cotangent, far, t, d):
        matrices, made = {}, {}
        for n in self.pieces:
            given = dict(t=t, weights=weights, far=far, cot=cotangent, reach=reach)
            form = dict(start=self.begin, send=self.sent, fills=n == 0)
            made[n] = self.run(matrices, n, "cotangent", "cot", given, **form)
        arrays = {n: exchange(self.sizes, self.sent, made[n]) for n in made}
        whole = {}
        for n in self.pieces:
            given = dict(d=d, reach=reach, **arrays[n], **whole)
            whole = dict(grad_in=self.run(matrices, n, "gradient", "grad", given, finish=self.sent)["grad"])
        return whole["grad_in"]


def per_device(sizes, log_inputs, warm_potential, bary_weights, band_reach, bary_cotangent):
    shape = log_inputs.shape[1:]
    line = jnp.sum(jnp.where(band_reach == 0, jnp.arange(3, dtype=jnp.int32), 0))
    cases = [Case(sizes, n, shape) for n in range(3)]
    inputs, warm = log_inputs.reshape(shape), warm_potential.reshape(shape)
    far = lax.ppermute(bary_cotangent, "inp", SWAP)
    send, keep, t, d = lax.switch(
        line, [case.scalings for case in cases], inputs, warm, bary_weights, band_reach
    )
    arrived = lax.ppermute(send, "inp", SWAP)
    grad = lax.switch(
        line, [case.gradient for case in cases], bary_weights, band_reach, bary_cotangent, far, t, d
    )
    return (add(keep, arrived, grad), grad[None])


def solution(mesh):
    sizes = (mesh.shape["pa"], mesh.shape["pb"])
    return jax.shard_map(
        functools.partial(per_device, sizes),
        mesh=mesh,
        in_specs=(
            P("inp", "pa", "pb", None),
            P("inp", "pa", "pb", None),
            P("inp"),
            P(),
            P("pa", "pb", "inp"),
        ),
        out_specs=(P("pa", "pb", "inp"), P("inp", "pa", "pb", None)),
        check_vma=False,
    )
```

```python
import functools
import math

import jax
import jax.numpy as jnp
from jax import lax
from jax.experimental import pallas as pl
from jax.experimental.pallas import tpu as pltpu
from jax.sharding import PartitionSpec as P

BLOCK = 4
BLOCK_BITS = 2
HALO = 2 * BLOCK
SIGMA = 3.0
SUB = 8
GROUP = 8
SLOTS = 4
F32 = jnp.float32
BF16 = jnp.bfloat16


def tap(offset):
    gauss = math.exp(-offset * offset / (2.0 * SIGMA * SIGMA)) / (SIGMA * math.sqrt(2.0 * math.pi))
    return 0.5 * gauss + (0.5 if offset == 0 else 0.0)


def weight(i, j, reach):
    offset = (i - j).astype(F32)
    inside = jnp.abs((i >> BLOCK_BITS) - (j >> BLOCK_BITS)) <= reach
    gauss = jnp.exp(-offset * offset / (2.0 * SIGMA * SIGMA)) / (SIGMA * math.sqrt(2.0 * math.pi))
    return jnp.where(i == j, 0.5, 0.0) + 0.5 * jnp.where(inside, gauss, 0.0)


def halves(value):
    high = value.astype(BF16)
    return high, (value - high.astype(F32)).astype(BF16)


def dot(a, b):
    return jnp.dot(a, b, preferred_element_type=F32)


AXES = ("pa", "pb")


def parity(line):
    return lax.rem(lax.axis_index(AXES[line]), 2)


def edge(line, swap, size):
    return pl.ds(pl.multiple_of(jnp.where(parity(line) == swap, size - HALO, 0), HALO), HALO)


def iotas(shape):
    return (lax.broadcasted_iota(jnp.int32, shape, 0), lax.broadcasted_iota(jnp.int32, shape, 1))


def fill_z(ref, reach):
    n = ref.shape[1]
    i, j = iotas((n, n))
    high, low = halves(weight(i, j, reach))
    ref[0:n] = high
    ref[n : 2 * n] = high
    ref[2 * n : 3 * n] = low


def z_product(rows, kz):
    high, low = halves(rows)
    return dot(jnp.concatenate([high, low, high], axis=1), kz[...])


def y_depth(ny, halo):
    return 3 * (ny + 2 * halo)


def fill_y(ref, reach, halo):
    ny, depth = ref.shape
    i, c = iotas((ny, depth))
    wide = 2 * halo
    own = c < 3 * ny
    size = jnp.where(own, ny, max(wide, 1))
    c = jnp.where(own, c, c - 3 * ny)
    part = jnp.where(c >= 2 * size, 2, jnp.where(c >= size, 1, 0))
    j = c - part * size
    if halo:
        swap = jnp.where(j >= halo, 1, 0)
        e = j - swap * halo
        j = jnp.where(own, j, jnp.where(swap == parity(1), ny + e, e - halo))
    value = weight(i + HALO, j + HALO, reach)
    high = value.astype(BF16).astype(F32)
    ref[...] = jnp.where(part == 2, value - high, high).astype(BF16)


def y_product(ky, own, halo=None):
    high, low = halves(own)
    pieces = [high, low, high]
    if halo is not None:
        high, low = halves(halo)
        pieces += [high, low, high]
    return dot(ky[...], jnp.concatenate(pieces, axis=0))


def x_sum(plane, n, reach):
    phase = n % BLOCK
    span = BLOCK * reach
    total = tap(0) * plane(n)
    for d in range(1, span + 1):
        total = total + tap(d) * (plane(n - d) + plane(n + d))
    for d in range(span + 1, span + phase + 1):
        total = total + tap(d) * plane(n - d)
    for d in range(span + 1, span + BLOCK - phase):
        total = total + tap(d) * plane(n + d)
    return total


MATRICES = ("kz", "ky", "ky0")
EDGES = ("even", "odd", "y_even", "y_odd", "corner_even", "corner_odd")
INSIDE = ("warm", "inputs", "d", "far", "u", "u_out", "u_out_in", *EDGES, *(edge + "_out" for edge in EDGES), *MATRICES)
BOTH = (0, 1)
COST = pl.CostEstimate(flops=1, bytes_accessed=1, transcendentals=0)


class Stage:
    def __init__(self, shape, cut, piece, kind, finish=None, start=(), send=None, fills=False, part="all"):
        self.cut = cut
        self.piece = piece
        self.shape = tuple(n // 2 if line == cut else n for line, n in enumerate(shape))
        self.kind = kind
        self.finish = finish
        self.start = start
        self.send = send
        self.fills = fills
        self.part = part
        self.groups = self.shape[0] // GROUP

    def matrices(self):
        nx, ny, nz = self.shape
        shapes = {"kz": (3 * nz, nz)}
        if 1 in self.start:
            shapes["ky0"] = (ny, y_depth(ny, 0))
        else:
            shapes["ky"] = (ny, y_depth(ny, HALO))
        return shapes

    def needs(self):
        if self.fills:
            return ()
        wanted = {"kz": 2 in self.start, "ky": self.finish in (1, BOTH), "ky0": 1 in self.start}
        return tuple(key for key in wanted if wanted[key])

    def scratch(self):
        nx, ny, nz = self.shape
        items = {"work": pltpu.VMEM((GROUP, ny, nz), F32)}
        if self.finish == 0 and self.part != "inner":
            items["sides"] = pltpu.VMEM((2 * HALO, ny, nz), F32)
        if self.finish == BOTH:
            items["edge"] = pltpu.VMEM((GROUP, 2 * HALO, nz), F32)
            items["y_ext"] = pltpu.VMEM((nx + 2 * HALO, 2 * HALO, nz), F32)
        for key in self.reads() + self.writes():
            halved = key in ("cot", "send", "keep")
            depth = nx if key in self.reads() else SLOTS * GROUP
            items[key + "_here"] = pltpu.VMEM((depth, ny, nz // 2 if halved else nz), F32)
        streams = len(self.reads() + self.writes())
        if streams:
            items["sems"] = pltpu.SemaphoreType.DMA((streams, nx // GROUP))
        return items

    def reads(self):
        if self.kind == "cot":
            return ("t", "cot")
        return ("warm",) if self.kind == "exp" and self.piece == 0 and self.part != "inner" else ()

    def writes(self):
        return {"dual": ("d",), "part": ("send", "keep", "t"), "grad": ("grad",)}.get(self.kind, ())

    def place(self, g):
        nx, ny, _ = self.shape
        x, y = (self.piece * n if self.cut == line else 0 for line, n in enumerate((nx, ny)))
        return (pl.ds(pl.multiple_of(x + g * GROUP, GROUP), GROUP), pl.ds(y, ny))

    def step(self, r, x, n, rows, product):
        kind = self.kind
        at = (x, rows)

        there = (self.piece * self.shape[0] + x if self.cut == 0 else x, rows)

        def get(key):
            return r[key + "_here"][at] if key in self.reads() else r[key][there]

        def put(key, value):
            if key in self.writes():
                r[key + "_here"][r["slot"] * GROUP + n, rows] = value
            else:
                r[key][there] = value

        if kind == "exp":
            return jnp.exp(get("warm"))
        if kind == "none":
            return product
        if kind == "dual":
            value = jnp.exp(get("inputs")) / product
            put("d", value)
            return value
        if kind == "grad":
            put("grad", get("d") * product)
            return None
        scale = r["weights"][0]
        half = self.shape[2] // 2
        first = lax.axis_index("inp") == 0
        if kind == "part":
            part = scale * (get("warm") + jnp.log(product))
            put("t", product)
            left, right = part[:, :half], part[:, half:]
            put("keep", jnp.where(first, left, right))
            put("send", jnp.where(first, right, left))
            return None
        own, far = get("cot"), get("far")
        cot = jnp.concatenate([jnp.where(first, own, far), jnp.where(first, far, own)], axis=1)
        return scale * cot / get("t")

    def tiles(self, body):
        def tile_body(tile, carry):
            body(pl.ds(pl.multiple_of(tile * SUB, SUB), SUB))
            return carry

        lax.fori_loop(0, self.shape[1] // SUB, tile_body, 0)

    def x_sums(self, plane, reach, put):
        span = BLOCK * reach
        for q in range(0, GROUP, BLOCK):
            window = {m: plane(m) for m in range(q - span, q + BLOCK + span)}
            for n in range(q, q + BLOCK):
                put(n, x_sum(window.get, n, reach))

    def finish_x(self, r, x0, reach, first, last):
        def body(rows):
            def plane(m):
                if m < 0 and first:
                    return r["sides"][HALO + m, rows]
                if m >= GROUP and last:
                    return r["sides"][HALO + m - GROUP, rows]
                return r["u"][x0 + m, rows]

            def put(n, product):
                value = self.step(r, x0 + n, n, rows, product)
                if value is not None and self.start:
                    r["work"][n, rows] = value
                elif value is not None:
                    r["u_out"][x0 + n, rows] = value

            self.x_sums(plane, reach, put)

        self.tiles(body)

    def edge_sums(self, r, x0, reach):
        for swap in range(2):
            rows = pl.ds(swap * HALO, HALO)

            def put(n, product):
                r["edge"][n, rows] = product

            self.x_sums(lambda m: r["y_ext"][HALO + x0 + m, rows], reach, put)

    def group(self, r, g):
        nx, ny, nz = self.shape
        work, out = r["work"], r.get("u_out")
        x0 = pl.multiple_of(g * GROUP, GROUP)
        everything = pl.ds(0, ny)

        def finish_y(n):
            x = x0 + n
            if self.finish == BOTH:
                return y_product(r["ky"], r["u"][x], r["edge"][n])
            return y_product(r["ky"], r["u"][x], jnp.concatenate([r["even"][x], r["odd"][x]], axis=0))

        for reach in (1, 2):
            chosen = r["reach"][0] == reach
            if self.finish == BOTH:
                pl.when(chosen)(lambda: self.edge_sums(r, x0, reach))
            if self.finish == 0:
                last = self.groups - 1
                if self.part != "inner":
                    pl.when(chosen & (g == 0))(lambda: self.finish_x(r, x0, reach, True, last == 0))
                    if last > 0:
                        pl.when(chosen & (g == last))(lambda: self.finish_x(r, x0, reach, False, True))
                if self.part != "outer" and last > 1:
                    within = (g > 0) & (g < last)
                    pl.when(chosen & within)(lambda: self.finish_x(r, x0, reach, False, False))
        if self.finish == 0:
            if 1 in self.start:
                for n in range(GROUP):
                    work[n] = y_product(r["ky0"], work[n])
        elif 0 in self.start:
            if self.finish == 1:
                for n in range(GROUP):
                    work[n] = finish_y(n)

            def body(rows):
                for q in range(0, GROUP, BLOCK):
                    planes = {}
                    for n in range(q, q + BLOCK):
                        product = work[n, rows] if self.finish == 1 else None
                        planes[n] = self.step(r, x0 + n, n, rows, product)
                    for n in range(q, q + BLOCK):
                        work[n, rows] = x_sum(planes.get, n, 0)

            self.tiles(body)
        else:
            for n in range(GROUP):
                product = finish_y(n) if self.finish in (1, BOTH) else None
                value = self.step(r, x0 + n, n, everything, product)
                if value is not None:
                    work[n] = y_product(r["ky0"], value) if 1 in self.start else value
        if 2 in self.start:
            product = z_product(work[...].reshape(GROUP * ny, nz), r["kz"])
            out[pl.ds(x0, GROUP)] = product.reshape(GROUP, ny, nz)
        if self.send in (1, BOTH):
            names = ("y_even_out", "y_odd_out") if self.send == BOTH else ("even_out", "odd_out")
            for swap, name in enumerate(names):
                r[name][pl.ds(x0, GROUP)] = out[pl.ds(x0, GROUP), edge(1, swap, ny)]

    def complete(self, r, parts, planes):
        if "u_out_in" not in r:
            return
        others = parts["inner" if self.part == "outer" else "outer"]

        def copy(i, carry):
            at = planes(others.start + others.step * i)
            r["u_out"][at] = r["u_out_in"][at]
            return carry

        lax.fori_loop(0, len(others), copy, 0)

    def body(self, r):
        last = self.groups - 1
        parts = {"all": range(last + 1), "inner": range(1, last), "outer": range(0, last + 1, max(last, 1))}
        groups = parts[self.part]
        planes = lambda g: pl.ds(pl.multiple_of(g * GROUP, GROUP), GROUP)

        reads, writes = self.reads(), self.writes()

        def load(n, g):
            source = r[reads[n]]
            source = source.at[self.place(g)]
            return pltpu.make_async_copy(source, r[reads[n] + "_here"].at[planes(g)], r["sems"].at[n, g])

        def slot(g):
            return jnp.minimum(g, 1) if self.part == "outer" else lax.rem(g, SLOTS)

        def save(n, g):
            target = r[writes[n]]
            target = target.at[self.place(g)]
            sem = r["sems"].at[len(reads) + n, g]
            return pltpu.make_async_copy(r[writes[n] + "_here"].at[planes(slot(g))], target, sem)

        for g in groups:
            for n in range(len(reads)):
                load(n, g).start()
        if self.fills:
            fill_z(r["kz"], r["reach"][2])
            if "ky" in r:
                fill_y(r["ky"], r["reach"][1], HALO)
            if "ky0" in r:
                fill_y(r["ky0"], 0, 0)
        nx = self.shape[0]
        for swap, name in enumerate(("even", "odd")):
            if "sides" in r:
                r["sides"][edge(0, swap, 2 * HALO)] = r[name][...]
            if "y_ext" in r:
                rows = pl.ds(swap * HALO, HALO)
                r["y_ext"][HALO : HALO + nx, rows] = r["y_" + name][...]
                for n in range(2):
                    corner = r["corner_" + name][n * HALO : (n + 1) * HALO]
                    r["y_ext"][edge(0, n, nx + 2 * HALO), rows] = corner

        def run(i, carry):
            g = groups.start + groups.step * i
            for n in range(len(reads)):
                load(n, g).wait()
            for n in range(len(writes) if len(groups) > SLOTS else 0):
                pl.when(i >= SLOTS)(lambda: save(n, g - SLOTS).wait())
            self.group(dict(r, slot=slot(g)), g)
            for n in range(len(writes)):
                save(n, g).start()
            return carry

        lax.fori_loop(0, len(groups), run, 0)
        self.complete(r, parts, planes)
        if "even_out" in r and self.send in (0, BOTH):
            for swap, name in enumerate(("even_out", "odd_out")):
                r[name][...] = r["u_out"][edge(0, swap, nx)]
        for g in groups[-SLOTS:]:
            for n in range(len(writes)):
                save(n, g).wait()

    def __call__(self, name, **arrays):
        nx, ny, nz = self.shape
        whole = tuple(n * 2 if line == self.cut else n for line, n in enumerate(self.shape))
        outs = {}
        aliases = {}
        if self.kind == "dual":
            outs["d"] = whole
        if self.kind == "part":
            outs.update(send=(*whole[:2], nz // 2), keep=(*whole[:2], nz // 2), t=whole)
        if self.kind == "grad":
            outs["grad"] = whole
        if self.start or self.kind == "none":
            outs["u_out"] = self.shape
        if self.part != "inner":
            if self.send in (0, BOTH):
                outs["even_out"] = outs["odd_out"] = (HALO, ny, nz)
            if self.send == 1:
                outs["even_out"] = outs["odd_out"] = (nx, HALO, nz)
            if self.send == BOTH:
                outs["y_even_out"] = outs["y_odd_out"] = (nx, HALO, nz)
        if self.fills:
            outs.update(self.matrices())
        for n, key in enumerate(arrays):
            if key.endswith("_in"):
                aliases[n] = list(outs).index(key[:-3])
        scratch = self.scratch()
        names = list(arrays) + list(outs) + list(scratch)
        operands, in_specs = [], []
        stage_reads = self.reads()
        for key, value in arrays.items():
            if key in ("weights", "reach"):
                in_specs.append(pl.BlockSpec(memory_space=pltpu.SMEM))
            elif key in INSIDE and key not in stage_reads:
                value = pltpu.with_memory_space_constraint(value, pltpu.VMEM)
                in_specs.append(pl.BlockSpec(memory_space=pltpu.VMEM))
            else:
                in_specs.append(pl.BlockSpec(memory_space=pl.ANY))
            operands.append(value)
        out_shape, out_specs = [], []
        for key, shape in outs.items():
            space = pltpu.VMEM if key in INSIDE and key not in self.writes() else pltpu.HBM
            out_shape.append(space(shape, BF16 if key in MATRICES else F32))
            out_specs.append(pl.BlockSpec(memory_space=space))
        result = pl.pallas_call(
            lambda *refs: self.body(dict(zip(names, refs))),
            name=name,
            out_shape=out_shape,
            in_specs=in_specs,
            out_specs=out_specs,
            input_output_aliases=aliases,
            scratch_shapes=list(scratch.values()),
            compiler_params=pltpu.CompilerParams(vmem_limit_bytes=(14 if "sems" in scratch else 8) * 2**20),
            cost_estimate=COST,
        )(*operands)
        return dict(zip(outs, result))


def add_body(keep, arrived, after, out, left, right, total, sems):
    parts = sems.shape[1]
    step = total.shape[0] // parts
    planes = [pl.ds(n * step, step) for n in range(parts)]
    loads = [
        pltpu.make_async_copy(source.at[p], target.at[p], sems.at[m, n])
        for n, p in enumerate(planes)
        for m, (source, target) in enumerate(((keep, left), (arrived, right)))
    ]
    saves = [pltpu.make_async_copy(total.at[p], out.at[p], sems.at[2, n]) for n, p in enumerate(planes)]
    for copy in loads:
        copy.start()
    for n, p in enumerate(planes):
        loads[2 * n].wait()
        loads[2 * n + 1].wait()
        total[p] = left[p] + right[p]
        saves[n].start()
    for copy in saves:
        copy.wait()


def add(keep, arrived, after):
    return pl.pallas_call(
        add_body,
        name="barycenter",
        out_shape=pltpu.HBM(keep.shape, F32),
        in_specs=[pl.BlockSpec(memory_space=pl.ANY)] * 3,
        out_specs=pl.BlockSpec(memory_space=pltpu.HBM),
        scratch_shapes=[pltpu.VMEM(keep.shape, F32)] * 3 + [pltpu.SemaphoreType.DMA((3, 4))],
        compiler_params=pltpu.CompilerParams(vmem_limit_bytes=8 * 2**20),
        cost_estimate=COST,
    )(keep, arrived, after)


def neighbours(sizes, line, even, odd):
    made = []
    for first, value in enumerate((even, odd)):
        pairs = [(i, i + 1) for i in range(first, sizes[line] - 1, 2)]
        made.append(lax.ppermute(value, AXES[line], pairs + [(j, i) for i, j in pairs]))
    return made


def corner_body(even, odd, after, *outs):
    ny = even.shape[1]
    for swap, out in enumerate(outs):
        for n, ref in enumerate((even, odd)):
            out[pl.ds(n * HALO, HALO)] = ref[:, edge(1, swap, ny)]


def corners(even, odd, after):
    inside = pl.BlockSpec(memory_space=pltpu.VMEM)
    shape = (2 * HALO, HALO, even.shape[2])
    return pl.pallas_call(
        corner_body,
        name="corners",
        out_shape=[pltpu.VMEM(shape, F32)] * 2,
        in_specs=[inside] * 2 + [pl.BlockSpec(memory_space=pl.ANY)],
        out_specs=[inside] * 2,
        compiler_params=pltpu.CompilerParams(vmem_limit_bytes=4 * 2**20),
        cost_estimate=COST,
    )(*(pltpu.with_memory_space_constraint(v, pltpu.VMEM) for v in (even, odd)), after)


def exchange(sizes, line, made):
    if line != BOTH:
        return dict(zip(EDGES, neighbours(sizes, line, made["even_out"], made["odd_out"])))
    x = neighbours(sizes, 0, made["even_out"], made["odd_out"])
    y = neighbours(sizes, 1, made["y_even_out"], made["y_odd_out"])
    return dict(zip(EDGES, (*x, *y)))


SWAP = [(0, 1), (1, 0)]


class Case:
    def __init__(self, sizes, line, shape):
        self.sizes = sizes
        self.cut = 0 if line == 0 else None
        self.pieces = (0, 1) if line == 0 else (0,)
        self.shape = shape
        self.groups = shape[0] // GROUP
        self.sent, self.begin = ((1, (0, 2)), (0, (1, 2)), (BOTH, (2,)))[line]

    def run(self, matrices, n, name, kind, arrays, fills=False, **form):
        stage = Stage(self.shape, self.cut, n, kind, fills=fills, **form)
        made = stage(f"{name}_{n}", **arrays, **{key: matrices[key] for key in stage.needs()})
        if fills:
            matrices.update({key: made.pop(key) for key in stage.matrices()})
        return made

    def begin_lines(self, matrices, n, name, kind, arrays, fills):
        form = dict(start=self.begin, send=self.sent)
        if self.sent != 0 or self.groups < 3:
            return self.run(matrices, n, name, kind, arrays, fills=fills, **form)
        made = self.run(matrices, n, name + "_outer", kind, arrays, fills=fills, part="outer", **form)
        arrays = dict(arrays, u_out_in=made["u_out"])
        made.update(self.run(matrices, n, name + "_inner", kind, arrays, part="inner", **form))
        return made

    def end_lines(self, matrices, n, name, kind, arrays, u, halos, **form):
        if self.sent == 1:
            return self.run(matrices, n, name, kind, dict(arrays, u=u, **halos), finish=1, **form)
        x_halos = {key: halos.pop(key) for key in ("even", "odd")}
        if self.sent == 0:
            x_name, x_kind, x_form, given = name, kind, form, dict(arrays, u=u)
        else:
            x_name, x_kind, x_form, given = name + "_x", "none", {}, dict(reach=arrays["reach"], u=u)
        whole, part = {}, "all"
        if self.groups > 2:
            made = self.run(matrices, n, x_name + "_inner", x_kind, given, finish=0, part="inner", **x_form)
            whole, part = {key + "_in": made[key] for key in made}, "outer"
        if self.sent == BOTH:
            made = corners(*x_halos.values(), whole.get("u_out_in", u))
            halos.update(zip(EDGES[4:], neighbours(self.sizes, 1, *made)))
        given = dict(given, **whole, **x_halos)
        made = self.run(matrices, n, f"{x_name}_{part}", x_kind, given, finish=0, part=part, **x_form)
        if self.sent == 0:
            return made
        return self.run(matrices, n, name, kind, dict(arrays, u=made["u_out"], **halos), finish=BOTH, **form)

    def scalings(self, inputs, warm, weights, reach):
        matrices = {}
        form = dict(start=self.begin, send=self.sent)
        given = dict(warm=warm, reach=reach)
        made = {n: self.begin_lines(matrices, n, "scaling", "exp", given, n == 0) for n in self.pieces}
        halos = {n: exchange(self.sizes, self.sent, made[n]) for n in made}
        whole = {}
        for n in self.pieces:
            given = dict(inputs=inputs, reach=reach, **whole)
            made[n] = self.end_lines(matrices, n, "dual", "dual", given, made[n]["u_out"], halos[n], **form)
            whole = dict(d_in=made[n]["d"])
        d = whole["d_in"]
        halos = {n: exchange(self.sizes, self.sent, made[n]) for n in made}
        whole = {}
        for n in self.pieces:
            given = dict(warm=warm, weights=weights, reach=reach, **whole)
            part = self.end_lines(matrices, n, "partial", "part", given, made[n]["u_out"], halos[n])
            whole = {key + "_in": part[key] for key in ("send", "keep", "t")}
        return part["send"], part["keep"], part["t"], d

    def gradient(self, weights, reach, cotangent, far, t, d):
        matrices = {}
        given = dict(t=t, weights=weights, far=far, cot=cotangent, reach=reach)
        made = {n: self.begin_lines(matrices, n, "cotangent", "cot", given, n == 0) for n in self.pieces}
        halos = {n: exchange(self.sizes, self.sent, made[n]) for n in made}
        whole = {}
        for n in self.pieces:
            given = dict(d=d, reach=reach, **whole)
            made[n] = self.end_lines(matrices, n, "gradient", "grad", given, made[n]["u_out"], halos[n])
            whole = dict(grad_in=made[n]["grad"])
        return whole["grad_in"]


def per_device(sizes, log_inputs, warm_potential, bary_weights, band_reach, bary_cotangent):
    shape = log_inputs.shape[1:]
    line = jnp.sum(jnp.where(band_reach == 0, jnp.arange(3, dtype=jnp.int32), 0))
    cases = [Case(sizes, n, shape) for n in range(3)]
    inputs, warm = log_inputs.reshape(shape), warm_potential.reshape(shape)
    far = lax.ppermute(bary_cotangent, "inp", SWAP)
    send, keep, t, d = lax.switch(
        line, [case.scalings for case in cases], inputs, warm, bary_weights, band_reach
    )
    arrived = lax.ppermute(send, "inp", SWAP)
    grad = lax.switch(
        line, [case.gradient for case in cases], bary_weights, band_reach, bary_cotangent, far, t, d
    )
    return (add(keep, arrived, grad), grad[None])


def solution(mesh):
    sizes = (mesh.shape["pa"], mesh.shape["pb"])
    return jax.shard_map(
        functools.partial(per_device, sizes),
        mesh=mesh,
        in_specs=(
            P("inp", "pa", "pb", None),
            P("inp", "pa", "pb", None),
            P("inp"),
            P(),
            P("pa", "pb", "inp"),
        ),
        out_specs=(P("pa", "pb", "inp"), P("inp", "pa", "pb", None)),
        check_vma=False,
    )
```

```python
import functools
import math

import jax
import jax.numpy as jnp
from jax import lax
from jax.experimental import pallas as pl
from jax.experimental.pallas import tpu as pltpu
from jax.sharding import PartitionSpec as P

BLOCK = 4
BLOCK_BITS = 2
HALO = 2 * BLOCK
SIGMA = 3.0
SUB = 8
GROUP = 8
SLOTS = 4
F32 = jnp.float32
BF16 = jnp.bfloat16


def tap(offset):
    gauss = math.exp(-offset * offset / (2.0 * SIGMA * SIGMA)) / (SIGMA * math.sqrt(2.0 * math.pi))
    return 0.5 * gauss + (0.5 if offset == 0 else 0.0)


def weight(i, j, reach):
    offset = (i - j).astype(F32)
    inside = jnp.abs((i >> BLOCK_BITS) - (j >> BLOCK_BITS)) <= reach
    gauss = jnp.exp(-offset * offset / (2.0 * SIGMA * SIGMA)) / (SIGMA * math.sqrt(2.0 * math.pi))
    return jnp.where(i == j, 0.5, 0.0) + 0.5 * jnp.where(inside, gauss, 0.0)


def halves(value):
    high = value.astype(BF16)
    return high, (value - high.astype(F32)).astype(BF16)


def dot(a, b):
    return jnp.dot(a, b, preferred_element_type=F32)


AXES = ("pa", "pb")


def parity(line):
    return lax.rem(lax.axis_index(AXES[line]), 2)


def edge(line, swap, size):
    return pl.ds(pl.multiple_of(jnp.where(parity(line) == swap, size - HALO, 0), HALO), HALO)


def iotas(shape):
    return (lax.broadcasted_iota(jnp.int32, shape, 0), lax.broadcasted_iota(jnp.int32, shape, 1))


def fill_z(ref, reach):
    n = ref.shape[1]
    i, j = iotas((n, n))
    high, low = halves(weight(i, j, reach))
    ref[0:n] = high
    ref[n : 2 * n] = high
    ref[2 * n : 3 * n] = low


def z_product(rows, kz):
    high, low = halves(rows)
    return dot(jnp.concatenate([high, low, high], axis=1), kz[...])


def y_depth(ny, halo):
    return 3 * (ny + 2 * halo)


def fill_y(ref, reach, halo):
    ny, depth = ref.shape
    i, c = iotas((ny, depth))
    wide = 2 * halo
    own = c < 3 * ny
    size = jnp.where(own, ny, max(wide, 1))
    c = jnp.where(own, c, c - 3 * ny)
    part = jnp.where(c >= 2 * size, 2, jnp.where(c >= size, 1, 0))
    j = c - part * size
    if halo:
        swap = jnp.where(j >= halo, 1, 0)
        e = j - swap * halo
        j = jnp.where(own, j, jnp.where(swap == parity(1), ny + e, e - halo))
    value = weight(i + HALO, j + HALO, reach)
    high = value.astype(BF16).astype(F32)
    ref[...] = jnp.where(part == 2, value - high, high).astype(BF16)


def y_product(ky, own, halo=None):
    high, low = halves(own)
    pieces = [high, low, high]
    if halo is not None:
        high, low = halves(halo)
        pieces += [high, low, high]
    return dot(ky[...], jnp.concatenate(pieces, axis=0))


def x_sum(plane, n, reach):
    phase = n % BLOCK
    span = BLOCK * reach
    total = tap(0) * plane(n)
    for d in range(1, span + 1):
        total = total + tap(d) * (plane(n - d) + plane(n + d))
    for d in range(span + 1, span + phase + 1):
        total = total + tap(d) * plane(n - d)
    for d in range(span + 1, span + BLOCK - phase):
        total = total + tap(d) * plane(n + d)
    return total


MATRICES = ("kz", "ky", "ky0")
EDGES = ("even", "odd", "y_even", "y_odd", "corner_even", "corner_odd")
INSIDE = ("warm", "inputs", "d", "far", "u", "u_out", "u_out_in", *EDGES, *(edge + "_out" for edge in EDGES), *MATRICES)
BOTH = (0, 1)
COST = pl.CostEstimate(flops=1, bytes_accessed=1, transcendentals=0)


class Stage:
    def __init__(self, shape, cut, piece, kind, finish=None, start=(), send=None, fills=False, part="all"):
        self.cut = cut
        self.piece = piece
        self.shape = tuple(n // 2 if line == cut else n for line, n in enumerate(shape))
        self.kind = kind
        self.finish = finish
        self.start = start
        self.send = send
        self.fills = fills
        self.part = part
        self.groups = self.shape[0] // GROUP

    def matrices(self):
        nx, ny, nz = self.shape
        shapes = {"kz": (3 * nz, nz)}
        if 1 in self.start:
            shapes["ky0"] = (ny, y_depth(ny, 0))
        else:
            shapes["ky"] = (ny, y_depth(ny, HALO))
        return shapes

    def needs(self):
        if self.fills:
            return ()
        wanted = {"kz": 2 in self.start, "ky": self.finish in (1, BOTH), "ky0": 1 in self.start}
        return tuple(key for key in wanted if wanted[key])

    def scratch(self):
        nx, ny, nz = self.shape
        items = {"work": pltpu.VMEM((GROUP, ny, nz), F32)}
        if self.finish == 0 and self.part != "inner":
            items["sides"] = pltpu.VMEM((2 * HALO, ny, nz), F32)
        if self.finish == BOTH:
            items["edge"] = pltpu.VMEM((GROUP, 2 * HALO, nz), F32)
            items["y_ext"] = pltpu.VMEM((nx + 2 * HALO, 2 * HALO, nz), F32)
        for key in self.reads() + self.writes():
            halved = key in ("cot", "send", "keep")
            depth = nx if key in self.reads() else SLOTS * GROUP
            items[key + "_here"] = pltpu.VMEM((depth, ny, nz // 2 if halved else nz), F32)
        streams = len(self.reads() + self.writes())
        if streams:
            items["sems"] = pltpu.SemaphoreType.DMA((streams, nx // GROUP))
        return items

    def reads(self):
        if self.kind == "cot":
            return ("t", "cot")
        return ("warm",) if self.kind == "exp" and self.piece == 0 and self.part != "inner" else ()

    def writes(self):
        return {"dual": ("d",), "part": ("send", "keep", "t"), "grad": ("grad",)}.get(self.kind, ())

    def place(self, g):
        nx, ny, _ = self.shape
        x, y = (self.piece * n if self.cut == line else 0 for line, n in enumerate((nx, ny)))
        return (pl.ds(pl.multiple_of(x + g * GROUP, GROUP), GROUP), pl.ds(y, ny))

    def step(self, r, x, n, rows, product):
        kind = self.kind
        at = (x, rows)

        there = (self.piece * self.shape[0] + x if self.cut == 0 else x, rows)

        def get(key):
            return r[key + "_here"][at] if key in self.reads() else r[key][there]

        def put(key, value):
            if key in self.writes():
                r[key + "_here"][r["slot"] * GROUP + n, rows] = value
            else:
                r[key][there] = value

        if kind == "exp":
            return jnp.exp(get("warm"))
        if kind == "none":
            return product
        if kind == "dual":
            value = jnp.exp(get("inputs")) / product
            put("d", value)
            return value
        if kind == "grad":
            put("grad", get("d") * product)
            return None
        scale = r["weights"][0]
        half = self.shape[2] // 2
        first = lax.axis_index("inp") == 0
        if kind == "part":
            part = scale * (get("warm") + jnp.log(product))
            put("t", product)
            left, right = part[:, :half], part[:, half:]
            put("keep", jnp.where(first, left, right))
            put("send", jnp.where(first, right, left))
            return None
        own, far = get("cot"), get("far")
        cot = jnp.concatenate([jnp.where(first, own, far), jnp.where(first, far, own)], axis=1)
        return scale * cot / get("t")

    def tiles(self, body):
        def tile_body(tile, carry):
            body(pl.ds(pl.multiple_of(tile * SUB, SUB), SUB))
            return carry

        lax.fori_loop(0, self.shape[1] // SUB, tile_body, 0)

    def x_sums(self, plane, reach, put):
        span = BLOCK * reach
        for q in range(0, GROUP, BLOCK):
            window = {m: plane(m) for m in range(q - span, q + BLOCK + span)}
            for n in range(q, q + BLOCK):
                put(n, x_sum(window.get, n, reach))

    def finish_x(self, r, x0, reach, first, last):
        def body(rows):
            def plane(m):
                if m < 0 and first:
                    return r["sides"][HALO + m, rows]
                if m >= GROUP and last:
                    return r["sides"][HALO + m - GROUP, rows]
                return r["u"][x0 + m, rows]

            def put(n, product):
                value = self.step(r, x0 + n, n, rows, product)
                if value is not None and self.start:
                    r["work"][n, rows] = value
                elif value is not None:
                    r["u_out"][x0 + n, rows] = value

            self.x_sums(plane, reach, put)

        self.tiles(body)

    def edge_sums(self, r, x0, reach):
        for swap in range(2):
            rows = pl.ds(swap * HALO, HALO)

            def put(n, product):
                r["edge"][n, rows] = product

            self.x_sums(lambda m: r["y_ext"][HALO + x0 + m, rows], reach, put)

    def group(self, r, g):
        nx, ny, nz = self.shape
        work, out = r["work"], r.get("u_out")
        x0 = pl.multiple_of(g * GROUP, GROUP)
        everything = pl.ds(0, ny)

        def finish_y(n):
            x = x0 + n
            if self.finish == BOTH:
                return y_product(r["ky"], r["u"][x], r["edge"][n])
            return y_product(r["ky"], r["u"][x], jnp.concatenate([r["even"][x], r["odd"][x]], axis=0))

        for reach in (1, 2):
            chosen = r["reach"][0] == reach
            if self.finish == BOTH:
                pl.when(chosen)(lambda: self.edge_sums(r, x0, reach))
            if self.finish == 0:
                last = self.groups - 1
                if self.part != "inner":
                    pl.when(chosen & (g == 0))(lambda: self.finish_x(r, x0, reach, True, last == 0))
                    if last > 0:
                        pl.when(chosen & (g == last))(lambda: self.finish_x(r, x0, reach, False, True))
                if self.part != "outer" and last > 1:
                    within = (g > 0) & (g < last)
                    pl.when(chosen & within)(lambda: self.finish_x(r, x0, reach, False, False))
        if self.finish == 0:
            if 1 in self.start:
                for n in range(GROUP):
                    work[n] = y_product(r["ky0"], work[n])
        elif 0 in self.start:
            if self.finish == 1:
                for n in range(GROUP):
                    work[n] = finish_y(n)

            def body(rows):
                for q in range(0, GROUP, BLOCK):
                    planes = {}
                    for n in range(q, q + BLOCK):
                        product = work[n, rows] if self.finish == 1 else None
                        planes[n] = self.step(r, x0 + n, n, rows, product)
                    for n in range(q, q + BLOCK):
                        work[n, rows] = x_sum(planes.get, n, 0)

            self.tiles(body)
        else:
            for n in range(GROUP):
                product = finish_y(n) if self.finish in (1, BOTH) else None
                value = self.step(r, x0 + n, n, everything, product)
                if value is not None:
                    work[n] = y_product(r["ky0"], value) if 1 in self.start else value
        if 2 in self.start:
            product = z_product(work[...].reshape(GROUP * ny, nz), r["kz"])
            out[pl.ds(x0, GROUP)] = product.reshape(GROUP, ny, nz)
        if self.send in (1, BOTH):
            names = ("y_even_out", "y_odd_out") if self.send == BOTH else ("even_out", "odd_out")
            for swap, name in enumerate(names):
                r[name][pl.ds(x0, GROUP)] = out[pl.ds(x0, GROUP), edge(1, swap, ny)]

    def complete(self, r, parts, planes):
        if "u_out_in" not in r:
            return
        others = parts["inner" if self.part == "outer" else "outer"]

        def copy(i, carry):
            at = planes(others.start + others.step * i)
            r["u_out"][at] = r["u_out_in"][at]
            return carry

        lax.fori_loop(0, len(others), copy, 0)

    def body(self, r):
        last = self.groups - 1
        parts = {"all": range(last + 1), "inner": range(1, last), "outer": range(0, last + 1, max(last, 1))}
        groups = parts[self.part]
        planes = lambda g: pl.ds(pl.multiple_of(g * GROUP, GROUP), GROUP)

        reads, writes = self.reads(), self.writes()

        def load(n, g):
            source = r[reads[n]]
            source = source.at[self.place(g)]
            return pltpu.make_async_copy(source, r[reads[n] + "_here"].at[planes(g)], r["sems"].at[n, g])

        def slot(g):
            return jnp.minimum(g, 1) if self.part == "outer" else lax.rem(g, SLOTS)

        def save(n, g):
            target = r[writes[n]]
            target = target.at[self.place(g)]
            sem = r["sems"].at[len(reads) + n, g]
            return pltpu.make_async_copy(r[writes[n] + "_here"].at[planes(slot(g))], target, sem)

        for g in groups:
            for n in range(len(reads)):
                load(n, g).start()
        if self.fills:
            fill_z(r["kz"], r["reach"][2])
            if "ky" in r:
                fill_y(r["ky"], r["reach"][1], HALO)
            if "ky0" in r:
                fill_y(r["ky0"], 0, 0)
        nx = self.shape[0]
        for swap, name in enumerate(("even", "odd")):
            if "sides" in r:
                r["sides"][edge(0, swap, 2 * HALO)] = r[name][...]
            if "y_ext" in r:
                rows = pl.ds(swap * HALO, HALO)
                r["y_ext"][HALO : HALO + nx, rows] = r["y_" + name][...]
                for n in range(2):
                    corner = r["corner_" + name][n * HALO : (n + 1) * HALO]
                    r["y_ext"][edge(0, n, nx + 2 * HALO), rows] = corner

        def run(i, carry):
            g = groups.start + groups.step * i
            for n in range(len(reads)):
                load(n, g).wait()
            for n in range(len(writes) if len(groups) > SLOTS else 0):
                pl.when(i >= SLOTS)(lambda: save(n, g - SLOTS).wait())
            self.group(dict(r, slot=slot(g)), g)
            for n in range(len(writes)):
                save(n, g).start()
            return carry

        lax.fori_loop(0, len(groups), run, 0)
        self.complete(r, parts, planes)
        if "even_out" in r and self.send in (0, BOTH):
            for swap, name in enumerate(("even_out", "odd_out")):
                r[name][...] = r["u_out"][edge(0, swap, nx)]
        for g in groups[-SLOTS:]:
            for n in range(len(writes)):
                save(n, g).wait()

    def __call__(self, name, **arrays):
        nx, ny, nz = self.shape
        whole = tuple(n * 2 if line == self.cut else n for line, n in enumerate(self.shape))
        outs = {}
        aliases = {}
        if self.kind == "dual":
            outs["d"] = whole
        if self.kind == "part":
            outs.update(send=(*whole[:2], nz // 2), keep=(*whole[:2], nz // 2), t=whole)
        if self.kind == "grad":
            outs["grad"] = whole
        if self.start or self.kind == "none":
            outs["u_out"] = self.shape
        if self.part != "inner":
            if self.send in (0, BOTH):
                outs["even_out"] = outs["odd_out"] = (HALO, ny, nz)
            if self.send == 1:
                outs["even_out"] = outs["odd_out"] = (nx, HALO, nz)
            if self.send == BOTH:
                outs["y_even_out"] = outs["y_odd_out"] = (nx, HALO, nz)
        if self.fills:
            outs.update(self.matrices())
        for n, key in enumerate(arrays):
            if key.endswith("_in"):
                aliases[n] = list(outs).index(key[:-3])
        scratch = self.scratch()
        names = list(arrays) + list(outs) + list(scratch)
        operands, in_specs = [], []
        stage_reads = self.reads()
        for key, value in arrays.items():
            if key in ("weights", "reach"):
                in_specs.append(pl.BlockSpec(memory_space=pltpu.SMEM))
            elif key in INSIDE and key not in stage_reads:
                value = pltpu.with_memory_space_constraint(value, pltpu.VMEM)
                in_specs.append(pl.BlockSpec(memory_space=pltpu.VMEM))
            else:
                in_specs.append(pl.BlockSpec(memory_space=pl.ANY))
            operands.append(value)
        out_shape, out_specs = [], []
        for key, shape in outs.items():
            space = pltpu.VMEM if key in INSIDE and key not in self.writes() else pltpu.HBM
            out_shape.append(space(shape, BF16 if key in MATRICES else F32))
            out_specs.append(pl.BlockSpec(memory_space=space))
        result = pl.pallas_call(
            lambda *refs: self.body(dict(zip(names, refs))),
            name=name,
            out_shape=out_shape,
            in_specs=in_specs,
            out_specs=out_specs,
            input_output_aliases=aliases,
            scratch_shapes=list(scratch.values()),
            compiler_params=pltpu.CompilerParams(vmem_limit_bytes=(14 if "sems" in scratch else 8) * 2**20),
            cost_estimate=COST,
        )(*operands)
        return dict(zip(outs, result))


def fetch_body(source, after, out, sem):
    copy = pltpu.make_async_copy(source, out, sem.at[0])
    copy.start()
    copy.wait()


def fetch(value, after):
    return pl.pallas_call(
        fetch_body,
        name="fetch",
        out_shape=pltpu.VMEM(value.shape, F32),
        in_specs=[pl.BlockSpec(memory_space=pl.ANY)] * 2,
        out_specs=pl.BlockSpec(memory_space=pltpu.VMEM),
        scratch_shapes=[pltpu.SemaphoreType.DMA((1,))],
        compiler_params=pltpu.CompilerParams(vmem_limit_bytes=6 * 2**20),
        cost_estimate=COST,
    )(value, after)


def add_body(keep, arrived, out, here, sems):
    parts = sems.shape[1]
    step = here.shape[0] // parts
    planes = [pl.ds(n * step, step) for n in range(parts)]
    loads = [pltpu.make_async_copy(arrived.at[p], here.at[p], sems.at[0, n]) for n, p in enumerate(planes)]
    saves = [pltpu.make_async_copy(here.at[p], out.at[p], sems.at[1, n]) for n, p in enumerate(planes)]
    for copy in loads:
        copy.start()
    for n, p in enumerate(planes):
        loads[n].wait()
        here[p] = here[p] + keep[p]
        saves[n].start()
    for copy in saves:
        copy.wait()


def add(keep, arrived):
    return pl.pallas_call(
        add_body,
        name="barycenter",
        out_shape=pltpu.HBM(keep.shape, F32),
        in_specs=[pl.BlockSpec(memory_space=pltpu.VMEM), pl.BlockSpec(memory_space=pl.ANY)],
        out_specs=pl.BlockSpec(memory_space=pltpu.HBM),
        scratch_shapes=[pltpu.VMEM(keep.shape, F32), pltpu.SemaphoreType.DMA((2, 8))],
        compiler_params=pltpu.CompilerParams(vmem_limit_bytes=8 * 2**20),
        cost_estimate=COST,
    )(pltpu.with_memory_space_constraint(keep, pltpu.VMEM), arrived)


def neighbours(sizes, line, even, odd):
    made = []
    for first, value in enumerate((even, odd)):
        pairs = [(i, i + 1) for i in range(first, sizes[line] - 1, 2)]
        made.append(lax.ppermute(value, AXES[line], pairs + [(j, i) for i, j in pairs]))
    return made


def corner_body(even, odd, after, *outs):
    ny = even.shape[1]
    for swap, out in enumerate(outs):
        for n, ref in enumerate((even, odd)):
            out[pl.ds(n * HALO, HALO)] = ref[:, edge(1, swap, ny)]


def corners(even, odd, after):
    inside = pl.BlockSpec(memory_space=pltpu.VMEM)
    shape = (2 * HALO, HALO, even.shape[2])
    return pl.pallas_call(
        corner_body,
        name="corners",
        out_shape=[pltpu.VMEM(shape, F32)] * 2,
        in_specs=[inside] * 2 + [pl.BlockSpec(memory_space=pl.ANY)],
        out_specs=[inside] * 2,
        compiler_params=pltpu.CompilerParams(vmem_limit_bytes=4 * 2**20),
        cost_estimate=COST,
    )(*(pltpu.with_memory_space_constraint(v, pltpu.VMEM) for v in (even, odd)), after)


def exchange(sizes, line, made):
    if line != BOTH:
        return dict(zip(EDGES, neighbours(sizes, line, made["even_out"], made["odd_out"])))
    x = neighbours(sizes, 0, made["even_out"], made["odd_out"])
    y = neighbours(sizes, 1, made["y_even_out"], made["y_odd_out"])
    return dict(zip(EDGES, (*x, *y)))


SWAP = [(0, 1), (1, 0)]


class Case:
    def __init__(self, sizes, line, shape):
        self.sizes = sizes
        self.cut = 0 if line == 0 else None
        self.pieces = (0, 1) if line == 0 else (0,)
        self.shape = shape
        self.groups = shape[0] // GROUP
        self.sent, self.begin = ((1, (0, 2)), (0, (1, 2)), (BOTH, (2,)))[line]

    def run(self, matrices, n, name, kind, arrays, fills=False, **form):
        stage = Stage(self.shape, self.cut, n, kind, fills=fills, **form)
        made = stage(f"{name}_{n}", **arrays, **{key: matrices[key] for key in stage.needs()})
        if fills:
            matrices.update({key: made.pop(key) for key in stage.matrices()})
        return made

    def begin_lines(self, matrices, n, name, kind, arrays, fills):
        form = dict(start=self.begin, send=self.sent)
        if self.sent != 0 or self.groups < 3:
            return self.run(matrices, n, name, kind, arrays, fills=fills, **form)
        made = self.run(matrices, n, name + "_outer", kind, arrays, fills=fills, part="outer", **form)
        arrays = dict(arrays, u_out_in=made["u_out"])
        made.update(self.run(matrices, n, name + "_inner", kind, arrays, part="inner", **form))
        return made

    def end_lines(self, matrices, n, name, kind, arrays, u, halos, **form):
        if self.sent == 1:
            return self.run(matrices, n, name, kind, dict(arrays, u=u, **halos), finish=1, **form)
        x_halos = {key: halos.pop(key) for key in ("even", "odd")}
        if self.sent == 0:
            x_name, x_kind, x_form, given = name, kind, form, dict(arrays, u=u)
        else:
            x_name, x_kind, x_form, given = name + "_x", "none", {}, dict(reach=arrays["reach"], u=u)
        whole, part = {}, "all"
        if self.groups > 2:
            made = self.run(matrices, n, x_name + "_inner", x_kind, given, finish=0, part="inner", **x_form)
            whole, part = {key + "_in": made[key] for key in made}, "outer"
        if self.sent == BOTH:
            made = corners(*x_halos.values(), whole.get("u_out_in", u))
            halos.update(zip(EDGES[4:], neighbours(self.sizes, 1, *made)))
        given = dict(given, **whole, **x_halos)
        made = self.run(matrices, n, f"{x_name}_{part}", x_kind, given, finish=0, part=part, **x_form)
        if self.sent == 0:
            return made
        return self.run(matrices, n, name, kind, dict(arrays, u=made["u_out"], **halos), finish=BOTH, **form)

    def scalings(self, inputs, warm, weights, reach):
        matrices = {}
        form = dict(start=self.begin, send=self.sent)
        given = dict(warm=warm, reach=reach)
        made = {n: self.begin_lines(matrices, n, "scaling", "exp", given, n == 0) for n in self.pieces}
        halos = {n: exchange(self.sizes, self.sent, made[n]) for n in made}
        whole = {}
        for n in self.pieces:
            given = dict(inputs=inputs, reach=reach, **whole)
            made[n] = self.end_lines(matrices, n, "dual", "dual", given, made[n]["u_out"], halos[n], **form)
            whole = dict(d_in=made[n]["d"])
        d = whole["d_in"]
        halos = {n: exchange(self.sizes, self.sent, made[n]) for n in made}
        whole = {}
        for n in self.pieces:
            given = dict(warm=warm, weights=weights, reach=reach, **whole)
            part = self.end_lines(matrices, n, "partial", "part", given, made[n]["u_out"], halos[n])
            whole = {key + "_in": part[key] for key in ("send", "keep", "t")}
        return part["send"], part["keep"], part["t"], d

    def gradient(self, weights, reach, cotangent, far, t, d):
        matrices = {}
        given = dict(t=t, weights=weights, far=far, cot=cotangent, reach=reach)
        made = {n: self.begin_lines(matrices, n, "cotangent", "cot", given, n == 0) for n in self.pieces}
        halos = {n: exchange(self.sizes, self.sent, made[n]) for n in made}
        whole = {}
        for n in self.pieces:
            given = dict(d=d, reach=reach, **whole)
            made[n] = self.end_lines(matrices, n, "gradient", "grad", given, made[n]["u_out"], halos[n])
            whole = dict(grad_in=made[n]["grad"])
        return whole["grad_in"]


def per_device(sizes, log_inputs, warm_potential, bary_weights, band_reach, bary_cotangent):
    shape = log_inputs.shape[1:]
    line = jnp.sum(jnp.where(band_reach == 0, jnp.arange(3, dtype=jnp.int32), 0))
    cases = [Case(sizes, n, shape) for n in range(3)]
    inputs, warm = log_inputs.reshape(shape), warm_potential.reshape(shape)
    far = lax.ppermute(bary_cotangent, "inp", SWAP)
    send, keep, t, d = lax.switch(
        line, [case.scalings for case in cases], inputs, warm, bary_weights, band_reach
    )
    arrived = lax.ppermute(send, "inp", SWAP)
    grad = lax.switch(
        line, [case.gradient for case in cases], bary_weights, band_reach, bary_cotangent, far, t, d
    )
    return (add(fetch(keep, grad), arrived), grad[None])


def solution(mesh):
    sizes = (mesh.shape["pa"], mesh.shape["pb"])
    return jax.shard_map(
        functools.partial(per_device, sizes),
        mesh=mesh,
        in_specs=(
            P("inp", "pa", "pb", None),
            P("inp", "pa", "pb", None),
            P("inp"),
            P(),
            P("pa", "pb", "inp"),
        ),
        out_specs=(P("pa", "pb", "inp"), P("inp", "pa", "pb", None)),
        check_vma=False,
    )
```

```python
import functools
import math

import jax
import jax.numpy as jnp
from jax import lax
from jax.experimental import pallas as pl
from jax.experimental.pallas import tpu as pltpu
from jax.sharding import PartitionSpec as P

BLOCK = 4
BLOCK_BITS = 2
HALO = 2 * BLOCK
SIGMA = 3.0
SUB = 8
SUB_BITS = 3
XOUT = 16
GROUP = 8
SLOTS = 4
F32 = jnp.float32
BF16 = jnp.bfloat16


def tap(offset):
    gauss = math.exp(-offset * offset / (2.0 * SIGMA * SIGMA)) / (SIGMA * math.sqrt(2.0 * math.pi))
    return 0.5 * gauss + (0.5 if offset == 0 else 0.0)


def weight(i, j, reach):
    offset = (i - j).astype(F32)
    inside = jnp.abs((i >> BLOCK_BITS) - (j >> BLOCK_BITS)) <= reach
    gauss = jnp.exp(-offset * offset / (2.0 * SIGMA * SIGMA)) / (SIGMA * math.sqrt(2.0 * math.pi))
    return jnp.where(i == j, 0.5, 0.0) + 0.5 * jnp.where(inside, gauss, 0.0)


def halves(value):
    high = value.astype(BF16)
    return high, (value - high.astype(F32)).astype(BF16)


def dot(a, b):
    return jnp.dot(a, b, preferred_element_type=F32)


AXES = ("pa", "pb")


def parity(line):
    return lax.rem(lax.axis_index(AXES[line]), 2)


def edge(line, swap, size):
    return pl.ds(pl.multiple_of(jnp.where(parity(line) == swap, size - HALO, 0), HALO), HALO)


def iotas(shape):
    return (lax.broadcasted_iota(jnp.int32, shape, 0), lax.broadcasted_iota(jnp.int32, shape, 1))


def fill_z(ref, reach):
    n = ref.shape[1]
    i, j = iotas((n, n))
    high, low = halves(weight(i, j, reach))
    ref[0:n] = high
    ref[n : 2 * n] = high
    ref[2 * n : 3 * n] = low


def z_product(rows, kz):
    high, low = halves(rows)
    return dot(jnp.concatenate([high, low, high], axis=1), kz[...])


def y_depth(ny, halo):
    return 3 * (ny + 2 * halo)


def fill_y(ref, reach, halo):
    ny, depth = ref.shape
    i, c = iotas((ny, depth))
    wide = 2 * halo
    own = c < 3 * ny
    size = jnp.where(own, ny, max(wide, 1))
    c = jnp.where(own, c, c - 3 * ny)
    part = jnp.where(c >= 2 * size, 2, jnp.where(c >= size, 1, 0))
    j = c - part * size
    if halo:
        swap = jnp.where(j >= halo, 1, 0)
        e = j - swap * halo
        j = jnp.where(own, j, jnp.where(swap == parity(1), ny + e, e - halo))
    value = weight(i + HALO, j + HALO, reach)
    high = value.astype(BF16).astype(F32)
    ref[...] = jnp.where(part == 2, value - high, high).astype(BF16)


def y_product(ky, own, halo=None):
    high, low = halves(own)
    pieces = [high, low, high]
    if halo is not None:
        high, low = halves(halo)
        pieces += [high, low, high]
    return dot(ky[...], jnp.concatenate(pieces, axis=0))


def fill_x(ref, reach):
    m = (XOUT + 2 * HALO) * SUB
    i, j = iotas((XOUT * SUB, m))
    value = jnp.where((i & (SUB - 1)) == (j & (SUB - 1)), weight((i >> SUB_BITS) + HALO, j >> SUB_BITS, reach), 0.0)
    high, low = halves(value)
    ref[:, 0:m] = high
    ref[:, m : 2 * m] = high
    ref[:, 2 * m : 3 * m] = low


def x_sum(plane, n, reach):
    phase = n % BLOCK
    span = BLOCK * reach
    total = tap(0) * plane(n)
    for d in range(1, span + 1):
        total = total + tap(d) * (plane(n - d) + plane(n + d))
    for d in range(span + 1, span + phase + 1):
        total = total + tap(d) * plane(n - d)
    for d in range(span + 1, span + BLOCK - phase):
        total = total + tap(d) * plane(n + d)
    return total


MATRICES = ("kz", "ky", "ky0", "kx")
EDGES = ("even", "odd", "y_even", "y_odd", "corner_even", "corner_odd")
INSIDE = ("warm", "inputs", "d", "far", "u", "u_out", "u_out_in", *EDGES, *(edge + "_out" for edge in EDGES), *MATRICES)
BOTH = (0, 1)
COST = pl.CostEstimate(flops=1, bytes_accessed=1, transcendentals=0)


class Stage:
    def __init__(self, shape, cut, piece, kind, finish=None, start=(), send=None, fills=False, part="all"):
        self.cut = cut
        self.piece = piece
        self.shape = tuple(n // 2 if line == cut else n for line, n in enumerate(shape))
        self.kind = kind
        self.finish = finish
        self.start = start
        self.send = send
        self.fills = fills
        self.part = part
        self.groups = self.shape[0] // GROUP

    def matrices(self):
        nx, ny, nz = self.shape
        shapes = {"kz": (3 * nz, nz)}
        if 1 in self.start:
            shapes["ky0"] = (ny, y_depth(ny, 0))
        else:
            shapes["ky"] = (ny, y_depth(ny, HALO))
        if self.send == BOTH:
            shapes["kx"] = (XOUT * SUB, 3 * (XOUT + 2 * HALO) * SUB)
        return shapes

    def by_blocks(self):
        return self.kind == "none" and self.part == "inner" and (self.shape[0] - 2 * HALO) % XOUT == 0

    def needs(self):
        if self.fills:
            return ()
        wanted = {"kz": 2 in self.start, "ky": self.finish in (1, BOTH), "ky0": 1 in self.start}
        wanted["kx"] = self.by_blocks()
        return tuple(key for key in wanted if wanted[key])

    def scratch(self):
        nx, ny, nz = self.shape
        items = {"work": pltpu.VMEM((GROUP, ny, nz), F32)}
        if self.finish == 0 and self.part != "inner":
            items["sides"] = pltpu.VMEM((2 * HALO, ny, nz), F32)
        if self.finish == BOTH:
            items["edge"] = pltpu.VMEM((GROUP, 2 * HALO, nz), F32)
            items["y_ext"] = pltpu.VMEM((nx + 2 * HALO, 2 * HALO, nz), F32)
        for key in self.reads() + self.writes():
            halved = key in ("cot", "send", "keep")
            depth = nx if key in self.reads() else SLOTS * GROUP
            items[key + "_here"] = pltpu.VMEM((depth, ny, nz // 2 if halved else nz), F32)
        streams = len(self.reads() + self.writes())
        if streams:
            items["sems"] = pltpu.SemaphoreType.DMA((streams, nx // GROUP))
        return items

    def reads(self):
        if self.kind == "cot":
            return ("t", "cot")
        return ("warm",) if self.kind == "exp" and self.piece == 0 and self.part != "inner" else ()

    def writes(self):
        return {"dual": ("d",), "part": ("send", "keep", "t"), "grad": ("grad",)}.get(self.kind, ())

    def place(self, g):
        nx, ny, _ = self.shape
        x, y = (self.piece * n if self.cut == line else 0 for line, n in enumerate((nx, ny)))
        return (pl.ds(pl.multiple_of(x + g * GROUP, GROUP), GROUP), pl.ds(y, ny))

    def step(self, r, x, n, rows, product):
        kind = self.kind
        at = (x, rows)

        there = (self.piece * self.shape[0] + x if self.cut == 0 else x, rows)

        def get(key):
            return r[key + "_here"][at] if key in self.reads() else r[key][there]

        def put(key, value):
            if key in self.writes():
                r[key + "_here"][r["slot"] * GROUP + n, rows] = value
            else:
                r[key][there] = value

        if kind == "exp":
            return jnp.exp(get("warm"))
        if kind == "none":
            return product
        if kind == "dual":
            value = jnp.exp(get("inputs")) / product
            put("d", value)
            return value
        if kind == "grad":
            put("grad", get("d") * product)
            return None
        scale = r["weights"][0]
        half = self.shape[2] // 2
        first = lax.axis_index("inp") == 0
        if kind == "part":
            part = scale * (get("warm") + jnp.log(product))
            put("t", product)
            left, right = part[:, :half], part[:, half:]
            put("keep", jnp.where(first, left, right))
            put("send", jnp.where(first, right, left))
            return None
        own, far = get("cot"), get("far")
        cot = jnp.concatenate([jnp.where(first, own, far), jnp.where(first, far, own)], axis=1)
        return scale * cot / get("t")

    def tiles(self, body):
        def tile_body(tile, carry):
            body(pl.ds(pl.multiple_of(tile * SUB, SUB), SUB))
            return carry

        lax.fori_loop(0, self.shape[1] // SUB, tile_body, 0)

    def x_sums(self, plane, reach, put):
        span = BLOCK * reach
        for q in range(0, GROUP, BLOCK):
            window = {m: plane(m) for m in range(q - span, q + BLOCK + span)}
            for n in range(q, q + BLOCK):
                put(n, x_sum(window.get, n, reach))

    def finish_x(self, r, x0, reach, first, last):
        def body(rows):
            def plane(m):
                if m < 0 and first:
                    return r["sides"][HALO + m, rows]
                if m >= GROUP and last:
                    return r["sides"][HALO + m - GROUP, rows]
                return r["u"][x0 + m, rows]

            def put(n, product):
                value = self.step(r, x0 + n, n, rows, product)
                if value is not None and self.start:
                    r["work"][n, rows] = value
                elif value is not None:
                    r["u_out"][x0 + n, rows] = value

            self.x_sums(plane, reach, put)

        self.tiles(body)

    def edge_sums(self, r, x0, reach):
        for swap in range(2):
            rows = pl.ds(swap * HALO, HALO)

            def put(n, product):
                r["edge"][n, rows] = product

            self.x_sums(lambda m: r["y_ext"][HALO + x0 + m, rows], reach, put)

    def group(self, r, g):
        nx, ny, nz = self.shape
        work, out = r["work"], r.get("u_out")
        x0 = pl.multiple_of(g * GROUP, GROUP)
        everything = pl.ds(0, ny)

        def finish_y(n):
            x = x0 + n
            if self.finish == BOTH:
                return y_product(r["ky"], r["u"][x], r["edge"][n])
            return y_product(r["ky"], r["u"][x], jnp.concatenate([r["even"][x], r["odd"][x]], axis=0))

        for reach in (1, 2):
            chosen = r["reach"][0] == reach
            if self.finish == BOTH:
                pl.when(chosen)(lambda: self.edge_sums(r, x0, reach))
            if self.finish == 0:
                last = self.groups - 1
                if self.part != "inner":
                    pl.when(chosen & (g == 0))(lambda: self.finish_x(r, x0, reach, True, last == 0))
                    if last > 0:
                        pl.when(chosen & (g == last))(lambda: self.finish_x(r, x0, reach, False, True))
                if self.part != "outer" and last > 1:
                    within = (g > 0) & (g < last)
                    pl.when(chosen & within)(lambda: self.finish_x(r, x0, reach, False, False))
        if self.finish == 0:
            if 1 in self.start:
                for n in range(GROUP):
                    work[n] = y_product(r["ky0"], work[n])
        elif 0 in self.start:
            if self.finish == 1:
                for n in range(GROUP):
                    work[n] = finish_y(n)

            def body(rows):
                for q in range(0, GROUP, BLOCK):
                    planes = {}
                    for n in range(q, q + BLOCK):
                        product = work[n, rows] if self.finish == 1 else None
                        planes[n] = self.step(r, x0 + n, n, rows, product)
                    for n in range(q, q + BLOCK):
                        work[n, rows] = x_sum(planes.get, n, 0)

            self.tiles(body)
        else:
            for n in range(GROUP):
                product = finish_y(n) if self.finish in (1, BOTH) else None
                value = self.step(r, x0 + n, n, everything, product)
                if value is not None:
                    work[n] = y_product(r["ky0"], value) if 1 in self.start else value
        if 2 in self.start:
            product = z_product(work[...].reshape(GROUP * ny, nz), r["kz"])
            out[pl.ds(x0, GROUP)] = product.reshape(GROUP, ny, nz)
        if self.send in (1, BOTH):
            names = ("y_even_out", "y_odd_out") if self.send == BOTH else ("even_out", "odd_out")
            for swap, name in enumerate(names):
                r[name][pl.ds(x0, GROUP)] = out[pl.ds(x0, GROUP), edge(1, swap, ny)]

    def blocks(self, r):
        nx, _, nz = self.shape
        wide = XOUT + 2 * HALO

        def body(rows):
            for x in range(0, nx - 2 * HALO, XOUT):
                high, low = halves(r["u"][x : x + wide, rows].reshape(wide * SUB, nz))
                product = dot(r["kx"][...], jnp.concatenate([high, low, high], axis=0))
                r["u_out"][x + HALO : x + HALO + XOUT, rows] = product.reshape(XOUT, SUB, nz)

        self.tiles(body)

    def complete(self, r, parts, planes):
        if "u_out_in" not in r:
            return
        others = parts["inner" if self.part == "outer" else "outer"]

        def copy(i, carry):
            at = planes(others.start + others.step * i)
            r["u_out"][at] = r["u_out_in"][at]
            return carry

        lax.fori_loop(0, len(others), copy, 0)

    def body(self, r):
        if self.by_blocks():
            self.blocks(r)
            return
        last = self.groups - 1
        parts = {"all": range(last + 1), "inner": range(1, last), "outer": range(0, last + 1, max(last, 1))}
        groups = parts[self.part]
        planes = lambda g: pl.ds(pl.multiple_of(g * GROUP, GROUP), GROUP)

        reads, writes = self.reads(), self.writes()

        def load(n, g):
            source = r[reads[n]]
            source = source.at[self.place(g)]
            return pltpu.make_async_copy(source, r[reads[n] + "_here"].at[planes(g)], r["sems"].at[n, g])

        def slot(g):
            return jnp.minimum(g, 1) if self.part == "outer" else lax.rem(g, SLOTS)

        def save(n, g):
            target = r[writes[n]]
            target = target.at[self.place(g)]
            sem = r["sems"].at[len(reads) + n, g]
            return pltpu.make_async_copy(r[writes[n] + "_here"].at[planes(slot(g))], target, sem)

        for g in groups:
            for n in range(len(reads)):
                load(n, g).start()
        if self.fills:
            fill_z(r["kz"], r["reach"][2])
            if "ky" in r:
                fill_y(r["ky"], r["reach"][1], HALO)
            if "ky0" in r:
                fill_y(r["ky0"], 0, 0)
            if "kx" in r:
                fill_x(r["kx"], r["reach"][0])
        nx = self.shape[0]
        for swap, name in enumerate(("even", "odd")):
            if "sides" in r:
                r["sides"][edge(0, swap, 2 * HALO)] = r[name][...]
            if "y_ext" in r:
                rows = pl.ds(swap * HALO, HALO)
                r["y_ext"][HALO : HALO + nx, rows] = r["y_" + name][...]
                for n in range(2):
                    corner = r["corner_" + name][n * HALO : (n + 1) * HALO]
                    r["y_ext"][edge(0, n, nx + 2 * HALO), rows] = corner

        def run(i, carry):
            g = groups.start + groups.step * i
            for n in range(len(reads)):
                load(n, g).wait()
            for n in range(len(writes) if len(groups) > SLOTS else 0):
                pl.when(i >= SLOTS)(lambda: save(n, g - SLOTS).wait())
            self.group(dict(r, slot=slot(g)), g)
            for n in range(len(writes)):
                save(n, g).start()
            return carry

        lax.fori_loop(0, len(groups), run, 0)
        self.complete(r, parts, planes)
        if "even_out" in r and self.send in (0, BOTH):
            for swap, name in enumerate(("even_out", "odd_out")):
                r[name][...] = r["u_out"][edge(0, swap, nx)]
        for g in groups[-SLOTS:]:
            for n in range(len(writes)):
                save(n, g).wait()

    def __call__(self, name, **arrays):
        nx, ny, nz = self.shape
        whole = tuple(n * 2 if line == self.cut else n for line, n in enumerate(self.shape))
        outs = {}
        aliases = {}
        if self.kind == "dual":
            outs["d"] = whole
        if self.kind == "part":
            outs.update(send=(*whole[:2], nz // 2), keep=(*whole[:2], nz // 2), t=whole)
        if self.kind == "grad":
            outs["grad"] = whole
        if self.start or self.kind == "none":
            outs["u_out"] = self.shape
        if self.part != "inner":
            if self.send in (0, BOTH):
                outs["even_out"] = outs["odd_out"] = (HALO, ny, nz)
            if self.send == 1:
                outs["even_out"] = outs["odd_out"] = (nx, HALO, nz)
            if self.send == BOTH:
                outs["y_even_out"] = outs["y_odd_out"] = (nx, HALO, nz)
        if self.fills:
            outs.update(self.matrices())
        for n, key in enumerate(arrays):
            if key.endswith("_in"):
                aliases[n] = list(outs).index(key[:-3])
        scratch = self.scratch()
        names = list(arrays) + list(outs) + list(scratch)
        operands, in_specs = [], []
        stage_reads = self.reads()
        for key, value in arrays.items():
            if key in ("weights", "reach"):
                in_specs.append(pl.BlockSpec(memory_space=pltpu.SMEM))
            elif key in INSIDE and key not in stage_reads:
                value = pltpu.with_memory_space_constraint(value, pltpu.VMEM)
                in_specs.append(pl.BlockSpec(memory_space=pltpu.VMEM))
            else:
                in_specs.append(pl.BlockSpec(memory_space=pl.ANY))
            operands.append(value)
        out_shape, out_specs = [], []
        for key, shape in outs.items():
            space = pltpu.VMEM if key in INSIDE and key not in self.writes() else pltpu.HBM
            out_shape.append(space(shape, BF16 if key in MATRICES else F32))
            out_specs.append(pl.BlockSpec(memory_space=space))
        result = pl.pallas_call(
            lambda *refs: self.body(dict(zip(names, refs))),
            name=name,
            out_shape=out_shape,
            in_specs=in_specs,
            out_specs=out_specs,
            input_output_aliases=aliases,
            scratch_shapes=list(scratch.values()),
            compiler_params=pltpu.CompilerParams(vmem_limit_bytes=(14 if "sems" in scratch else 8) * 2**20),
            cost_estimate=COST,
        )(*operands)
        return dict(zip(outs, result))


def fetch_body(source, after, out, sem):
    copy = pltpu.make_async_copy(source, out, sem.at[0])
    copy.start()
    copy.wait()


def fetch(value, after):
    return pl.pallas_call(
        fetch_body,
        name="fetch",
        out_shape=pltpu.VMEM(value.shape, F32),
        in_specs=[pl.BlockSpec(memory_space=pl.ANY)] * 2,
        out_specs=pl.BlockSpec(memory_space=pltpu.VMEM),
        scratch_shapes=[pltpu.SemaphoreType.DMA((1,))],
        compiler_params=pltpu.CompilerParams(vmem_limit_bytes=6 * 2**20),
        cost_estimate=COST,
    )(value, after)


def add_body(keep, arrived, out, here, sems):
    parts = sems.shape[1]
    step = here.shape[0] // parts
    planes = [pl.ds(n * step, step) for n in range(parts)]
    loads = [pltpu.make_async_copy(arrived.at[p], here.at[p], sems.at[0, n]) for n, p in enumerate(planes)]
    saves = [pltpu.make_async_copy(here.at[p], out.at[p], sems.at[1, n]) for n, p in enumerate(planes)]
    for copy in loads:
        copy.start()
    for n, p in enumerate(planes):
        loads[n].wait()
        here[p] = here[p] + keep[p]
        saves[n].start()
    for copy in saves:
        copy.wait()


def add(keep, arrived):
    return pl.pallas_call(
        add_body,
        name="barycenter",
        out_shape=pltpu.HBM(keep.shape, F32),
        in_specs=[pl.BlockSpec(memory_space=pltpu.VMEM), pl.BlockSpec(memory_space=pl.ANY)],
        out_specs=pl.BlockSpec(memory_space=pltpu.HBM),
        scratch_shapes=[pltpu.VMEM(keep.shape, F32), pltpu.SemaphoreType.DMA((2, 8))],
        compiler_params=pltpu.CompilerParams(vmem_limit_bytes=8 * 2**20),
        cost_estimate=COST,
    )(pltpu.with_memory_space_constraint(keep, pltpu.VMEM), arrived)


def neighbours(sizes, line, even, odd):
    made = []
    for first, value in enumerate((even, odd)):
        pairs = [(i, i + 1) for i in range(first, sizes[line] - 1, 2)]
        made.append(lax.ppermute(value, AXES[line], pairs + [(j, i) for i, j in pairs]))
    return made


def corner_body(even, odd, after, *outs):
    ny = even.shape[1]
    for swap, out in enumerate(outs):
        for n, ref in enumerate((even, odd)):
            out[pl.ds(n * HALO, HALO)] = ref[:, edge(1, swap, ny)]


def corners(even, odd, after):
    inside = pl.BlockSpec(memory_space=pltpu.VMEM)
    shape = (2 * HALO, HALO, even.shape[2])
    return pl.pallas_call(
        corner_body,
        name="corners",
        out_shape=[pltpu.VMEM(shape, F32)] * 2,
        in_specs=[inside] * 2 + [pl.BlockSpec(memory_space=pl.ANY)],
        out_specs=[inside] * 2,
        compiler_params=pltpu.CompilerParams(vmem_limit_bytes=4 * 2**20),
        cost_estimate=COST,
    )(*(pltpu.with_memory_space_constraint(v, pltpu.VMEM) for v in (even, odd)), after)


def exchange(sizes, line, made):
    if line != BOTH:
        return dict(zip(EDGES, neighbours(sizes, line, made["even_out"], made["odd_out"])))
    x = neighbours(sizes, 0, made["even_out"], made["odd_out"])
    y = neighbours(sizes, 1, made["y_even_out"], made["y_odd_out"])
    return dict(zip(EDGES, (*x, *y)))


SWAP = [(0, 1), (1, 0)]


class Case:
    def __init__(self, sizes, line, shape):
        self.sizes = sizes
        self.cut = 0 if line == 0 else None
        self.pieces = (0, 1) if line == 0 else (0,)
        self.shape = shape
        self.groups = shape[0] // GROUP
        self.sent, self.begin = ((1, (0, 2)), (0, (1, 2)), (BOTH, (2,)))[line]

    def run(self, matrices, n, name, kind, arrays, fills=False, **form):
        stage = Stage(self.shape, self.cut, n, kind, fills=fills, **form)
        made = stage(f"{name}_{n}", **arrays, **{key: matrices[key] for key in stage.needs()})
        if fills:
            matrices.update({key: made.pop(key) for key in stage.matrices()})
        return made

    def begin_lines(self, matrices, n, name, kind, arrays, fills):
        form = dict(start=self.begin, send=self.sent)
        if self.sent != 0 or self.groups < 3:
            return self.run(matrices, n, name, kind, arrays, fills=fills, **form)
        made = self.run(matrices, n, name + "_outer", kind, arrays, fills=fills, part="outer", **form)
        arrays = dict(arrays, u_out_in=made["u_out"])
        made.update(self.run(matrices, n, name + "_inner", kind, arrays, part="inner", **form))
        return made

    def end_lines(self, matrices, n, name, kind, arrays, u, halos, **form):
        if self.sent == 1:
            return self.run(matrices, n, name, kind, dict(arrays, u=u, **halos), finish=1, **form)
        x_halos = {key: halos.pop(key) for key in ("even", "odd")}
        if self.sent == 0:
            x_name, x_kind, x_form, given = name, kind, form, dict(arrays, u=u)
        else:
            x_name, x_kind, x_form, given = name + "_x", "none", {}, dict(reach=arrays["reach"], u=u)
        whole, part = {}, "all"
        if self.groups > 2:
            made = self.run(matrices, n, x_name + "_inner", x_kind, given, finish=0, part="inner", **x_form)
            whole, part = {key + "_in": made[key] for key in made}, "outer"
        if self.sent == BOTH:
            made = corners(*x_halos.values(), whole.get("u_out_in", u))
            halos.update(zip(EDGES[4:], neighbours(self.sizes, 1, *made)))
        given = dict(given, **whole, **x_halos)
        made = self.run(matrices, n, f"{x_name}_{part}", x_kind, given, finish=0, part=part, **x_form)
        if self.sent == 0:
            return made
        return self.run(matrices, n, name, kind, dict(arrays, u=made["u_out"], **halos), finish=BOTH, **form)

    def scalings(self, inputs, warm, weights, reach):
        matrices = {}
        form = dict(start=self.begin, send=self.sent)
        given = dict(warm=warm, reach=reach)
        made = {n: self.begin_lines(matrices, n, "scaling", "exp", given, n == 0) for n in self.pieces}
        halos = {n: exchange(self.sizes, self.sent, made[n]) for n in made}
        whole = {}
        for n in self.pieces:
            given = dict(inputs=inputs, reach=reach, **whole)
            made[n] = self.end_lines(matrices, n, "dual", "dual", given, made[n]["u_out"], halos[n], **form)
            whole = dict(d_in=made[n]["d"])
        d = whole["d_in"]
        halos = {n: exchange(self.sizes, self.sent, made[n]) for n in made}
        whole = {}
        for n in self.pieces:
            given = dict(warm=warm, weights=weights, reach=reach, **whole)
            part = self.end_lines(matrices, n, "partial", "part", given, made[n]["u_out"], halos[n])
            whole = {key + "_in": part[key] for key in ("send", "keep", "t")}
        return part["send"], part["keep"], part["t"], d

    def gradient(self, weights, reach, cotangent, far, t, d):
        matrices = {}
        given = dict(t=t, weights=weights, far=far, cot=cotangent, reach=reach)
        made = {n: self.begin_lines(matrices, n, "cotangent", "cot", given, n == 0) for n in self.pieces}
        halos = {n: exchange(self.sizes, self.sent, made[n]) for n in made}
        whole = {}
        for n in self.pieces:
            given = dict(d=d, reach=reach, **whole)
            made[n] = self.end_lines(matrices, n, "gradient", "grad", given, made[n]["u_out"], halos[n])
            whole = dict(grad_in=made[n]["grad"])
        return whole["grad_in"]


def per_device(sizes, log_inputs, warm_potential, bary_weights, band_reach, bary_cotangent):
    shape = log_inputs.shape[1:]
    line = jnp.sum(jnp.where(band_reach == 0, jnp.arange(3, dtype=jnp.int32), 0))
    cases = [Case(sizes, n, shape) for n in range(3)]
    inputs, warm = log_inputs.reshape(shape), warm_potential.reshape(shape)
    far = lax.ppermute(bary_cotangent, "inp", SWAP)
    send, keep, t, d = lax.switch(
        line, [case.scalings for case in cases], inputs, warm, bary_weights, band_reach
    )
    arrived = lax.ppermute(send, "inp", SWAP)
    grad = lax.switch(
        line, [case.gradient for case in cases], bary_weights, band_reach, bary_cotangent, far, t, d
    )
    return (add(fetch(keep, grad), arrived), grad[None])


def solution(mesh):
    sizes = (mesh.shape["pa"], mesh.shape["pb"])
    return jax.shard_map(
        functools.partial(per_device, sizes),
        mesh=mesh,
        in_specs=(
            P("inp", "pa", "pb", None),
            P("inp", "pa", "pb", None),
            P("inp"),
            P(),
            P("pa", "pb", "inp"),
        ),
        out_specs=(P("pa", "pb", "inp"), P("inp", "pa", "pb", None)),
        check_vma=False,
    )
```

```python
import functools
import math

import jax
import jax.numpy as jnp
from jax import lax
from jax.experimental import pallas as pl
from jax.experimental.pallas import tpu as pltpu
from jax.sharding import PartitionSpec as P

BLOCK = 4
BLOCK_BITS = 2
HALO = 2 * BLOCK
SIGMA = 3.0
SUB = 8
GROUP = 8
SLOTS = 4
F32 = jnp.float32
BF16 = jnp.bfloat16


def tap(offset):
    gauss = math.exp(-offset * offset / (2.0 * SIGMA * SIGMA)) / (SIGMA * math.sqrt(2.0 * math.pi))
    return 0.5 * gauss + (0.5 if offset == 0 else 0.0)


def weight(i, j, reach):
    offset = (i - j).astype(F32)
    inside = jnp.abs((i >> BLOCK_BITS) - (j >> BLOCK_BITS)) <= reach
    gauss = jnp.exp(-offset * offset / (2.0 * SIGMA * SIGMA)) / (SIGMA * math.sqrt(2.0 * math.pi))
    return jnp.where(i == j, 0.5, 0.0) + 0.5 * jnp.where(inside, gauss, 0.0)


def halves(value):
    high = value.astype(BF16)
    return high, (value - high.astype(F32)).astype(BF16)


def dot(a, b):
    return jnp.dot(a, b, preferred_element_type=F32)


AXES = ("pa", "pb")


def parity(line):
    return lax.rem(lax.axis_index(AXES[line]), 2)


def edge(line, swap, size):
    return pl.ds(pl.multiple_of(jnp.where(parity(line) == swap, size - HALO, 0), HALO), HALO)


def iotas(shape):
    return (lax.broadcasted_iota(jnp.int32, shape, 0), lax.broadcasted_iota(jnp.int32, shape, 1))


def fill_z(ref, reach):
    n = ref.shape[1]
    i, j = iotas((n, n))
    high, low = halves(weight(i, j, reach))
    ref[0:n] = high
    ref[n : 2 * n] = high
    ref[2 * n : 3 * n] = low


def z_product(rows, kz):
    high, low = halves(rows)
    return dot(jnp.concatenate([high, low, high], axis=1), kz[...])


def y_depth(ny, halo):
    return 3 * (ny + 2 * halo)


def fill_y(ref, reach, halo):
    ny, depth = ref.shape
    i, c = iotas((ny, depth))
    wide = 2 * halo
    own = c < 3 * ny
    size = jnp.where(own, ny, max(wide, 1))
    c = jnp.where(own, c, c - 3 * ny)
    part = jnp.where(c >= 2 * size, 2, jnp.where(c >= size, 1, 0))
    j = c - part * size
    if halo:
        swap = jnp.where(j >= halo, 1, 0)
        e = j - swap * halo
        j = jnp.where(own, j, jnp.where(swap == parity(1), ny + e, e - halo))
    value = weight(i + HALO, j + HALO, reach)
    high = value.astype(BF16).astype(F32)
    ref[...] = jnp.where(part == 2, value - high, high).astype(BF16)


def y_product(ky, own, halo=None):
    high, low = halves(own)
    pieces = [high, low, high]
    if halo is not None:
        high, low = halves(halo)
        pieces += [high, low, high]
    return dot(ky[...], jnp.concatenate(pieces, axis=0))


def x_sum(plane, n, reach):
    phase = n % BLOCK
    span = BLOCK * reach
    total = tap(0) * plane(n)
    for d in range(1, span + 1):
        total = total + tap(d) * (plane(n - d) + plane(n + d))
    for d in range(span + 1, span + phase + 1):
        total = total + tap(d) * plane(n - d)
    for d in range(span + 1, span + BLOCK - phase):
        total = total + tap(d) * plane(n + d)
    return total


MATRICES = ("kz", "ky", "ky0")
EDGES = ("even", "odd", "y_even", "y_odd", "corner_even", "corner_odd")
INSIDE = ("warm", "inputs", "d", "far", "u", "u_out", "u_out_in", *EDGES, *(edge + "_out" for edge in EDGES), *MATRICES)
BOTH = (0, 1)
COST = pl.CostEstimate(flops=1, bytes_accessed=1, transcendentals=0)


class Stage:
    def __init__(self, shape, cut, piece, kind, finish=None, start=(), send=None, fills=False, part="all"):
        self.cut = cut
        self.piece = piece
        self.shape = tuple(n // 2 if line == cut else n for line, n in enumerate(shape))
        self.kind = kind
        self.finish = finish
        self.start = start
        self.send = send
        self.fills = fills
        self.part = part
        self.groups = self.shape[0] // GROUP

    def matrices(self):
        nx, ny, nz = self.shape
        shapes = {"kz": (3 * nz, nz)}
        if 1 in self.start:
            shapes["ky0"] = (ny, y_depth(ny, 0))
        else:
            shapes["ky"] = (ny, y_depth(ny, HALO))
        return shapes

    def needs(self):
        if self.fills:
            return ()
        wanted = {"kz": 2 in self.start, "ky": self.finish in (1, BOTH), "ky0": 1 in self.start}
        return tuple(key for key in wanted if wanted[key])

    def scratch(self):
        nx, ny, nz = self.shape
        items = {"work": pltpu.VMEM((GROUP, ny, nz), F32)}
        if self.finish == 0 and self.part != "inner":
            items["sides"] = pltpu.VMEM((2 * HALO, ny, nz), F32)
        if self.finish == BOTH:
            items["edge"] = pltpu.VMEM((GROUP, 2 * HALO, nz), F32)
            items["y_ext"] = pltpu.VMEM((nx + 2 * HALO, 2 * HALO, nz), F32)
        for key in self.reads() + self.writes():
            halved = key in ("cot", "send", "keep")
            depth = nx if key in self.reads() else SLOTS * GROUP
            items[key + "_here"] = pltpu.VMEM((depth, ny, nz // 2 if halved else nz), F32)
        streams = len(self.reads() + self.writes())
        if streams:
            items["sems"] = pltpu.SemaphoreType.DMA((streams, nx // GROUP))
        return items

    def reads(self):
        if self.kind == "cot":
            return ("t", "cot")
        return ("warm",) if self.kind == "exp" and self.piece == 0 and self.part != "inner" else ()

    def writes(self):
        return {"dual": ("d",), "part": ("send", "keep", "t"), "grad": ("grad",)}.get(self.kind, ())

    def place(self, g):
        nx, ny, _ = self.shape
        x, y = (self.piece * n if self.cut == line else 0 for line, n in enumerate((nx, ny)))
        return (pl.ds(pl.multiple_of(x + g * GROUP, GROUP), GROUP), pl.ds(y, ny))

    def step(self, r, x, n, rows, product):
        kind = self.kind
        at = (x, rows)

        there = (self.piece * self.shape[0] + x if self.cut == 0 else x, rows)

        def get(key):
            return r[key + "_here"][at] if key in self.reads() else r[key][there]

        def put(key, value):
            if key in self.writes():
                r[key + "_here"][r["slot"] * GROUP + n, rows] = value
            else:
                r[key][there] = value

        if kind == "exp":
            return jnp.exp(get("warm"))
        if kind == "none":
            return product
        if kind == "dual":
            value = jnp.exp(get("inputs")) / product
            put("d", value)
            return value
        if kind == "grad":
            put("grad", get("d") * product)
            return None
        scale = r["weights"][0]
        half = self.shape[2] // 2
        first = lax.axis_index("inp") == 0
        if kind == "part":
            part = scale * (get("warm") + jnp.log(product))
            put("t", product)
            left, right = part[:, :half], part[:, half:]
            put("keep", jnp.where(first, left, right))
            put("send", jnp.where(first, right, left))
            return None
        own, far = get("cot"), get("far")
        cot = jnp.concatenate([jnp.where(first, own, far), jnp.where(first, far, own)], axis=1)
        return scale * cot / get("t")

    def tiles(self, body):
        def tile_body(tile, carry):
            body(pl.ds(pl.multiple_of(tile * SUB, SUB), SUB))
            return carry

        lax.fori_loop(0, self.shape[1] // SUB, tile_body, 0)

    def x_sums(self, plane, reach, put):
        span = BLOCK * reach
        for q in range(0, GROUP, BLOCK):
            window = {m: plane(m) for m in range(q - span, q + BLOCK + span)}
            for n in range(q, q + BLOCK):
                put(n, x_sum(window.get, n, reach))

    def finish_x(self, r, x0, reach, first, last):
        def body(rows):
            def plane(m):
                if m < 0 and first:
                    return r["sides"][HALO + m, rows]
                if m >= GROUP and last:
                    return r["sides"][HALO + m - GROUP, rows]
                return r["u"][x0 + m, rows]

            def put(n, product):
                value = self.step(r, x0 + n, n, rows, product)
                if value is not None and self.start:
                    r["work"][n, rows] = value
                elif value is not None:
                    r["u_out"][x0 + n, rows] = value

            self.x_sums(plane, reach, put)

        self.tiles(body)

    def edge_sums(self, r, x0, reach):
        for swap in range(2):
            rows = pl.ds(swap * HALO, HALO)

            def put(n, product):
                r["edge"][n, rows] = product

            self.x_sums(lambda m: r["y_ext"][HALO + x0 + m, rows], reach, put)

    def group(self, r, g):
        nx, ny, nz = self.shape
        work, out = r["work"], r.get("u_out")
        x0 = pl.multiple_of(g * GROUP, GROUP)
        everything = pl.ds(0, ny)

        def finish_y(n):
            x = x0 + n
            if self.finish == BOTH:
                return y_product(r["ky"], r["u"][x], r["edge"][n])
            return y_product(r["ky"], r["u"][x], jnp.concatenate([r["even"][x], r["odd"][x]], axis=0))

        for reach in (1, 2):
            chosen = r["reach"][0] == reach
            if self.finish == BOTH:
                pl.when(chosen)(lambda: self.edge_sums(r, x0, reach))
            if self.finish == 0:
                last = self.groups - 1
                if self.part != "inner":
                    pl.when(chosen & (g == 0))(lambda: self.finish_x(r, x0, reach, True, last == 0))
                    if last > 0:
                        pl.when(chosen & (g == last))(lambda: self.finish_x(r, x0, reach, False, True))
                if self.part != "outer" and last > 1:
                    within = (g > 0) & (g < last)
                    pl.when(chosen & within)(lambda: self.finish_x(r, x0, reach, False, False))
        if self.finish == 0:
            if 1 in self.start:
                for n in range(GROUP):
                    work[n] = y_product(r["ky0"], work[n])
        elif 0 in self.start:
            if self.finish == 1:
                for n in range(GROUP):
                    work[n] = finish_y(n)

            def body(rows):
                for q in range(0, GROUP, BLOCK):
                    planes = {}
                    for n in range(q, q + BLOCK):
                        product = work[n, rows] if self.finish == 1 else None
                        planes[n] = self.step(r, x0 + n, n, rows, product)
                    for n in range(q, q + BLOCK):
                        work[n, rows] = x_sum(planes.get, n, 0)

            self.tiles(body)
        else:
            for n in range(GROUP):
                product = finish_y(n) if self.finish in (1, BOTH) else None
                value = self.step(r, x0 + n, n, everything, product)
                if value is not None:
                    work[n] = y_product(r["ky0"], value) if 1 in self.start else value
        if 2 in self.start:
            product = z_product(work[...].reshape(GROUP * ny, nz), r["kz"])
            out[pl.ds(x0, GROUP)] = product.reshape(GROUP, ny, nz)
        if self.send in (1, BOTH):
            names = ("y_even_out", "y_odd_out") if self.send == BOTH else ("even_out", "odd_out")
            for swap, name in enumerate(names):
                r[name][pl.ds(x0, GROUP)] = out[pl.ds(x0, GROUP), edge(1, swap, ny)]

    def complete(self, r, parts, planes):
        if "u_out_in" not in r:
            return
        others = parts["inner" if self.part == "outer" else "outer"]

        def copy(i, carry):
            at = planes(others.start + others.step * i)
            r["u_out"][at] = r["u_out_in"][at]
            return carry

        lax.fori_loop(0, len(others), copy, 0)

    def body(self, r):
        last = self.groups - 1
        parts = {"all": range(last + 1), "inner": range(1, last), "outer": range(0, last + 1, max(last, 1))}
        groups = parts[self.part]
        planes = lambda g: pl.ds(pl.multiple_of(g * GROUP, GROUP), GROUP)

        reads, writes = self.reads(), self.writes()

        def load(n, g):
            source = r[reads[n]]
            source = source.at[self.place(g)]
            return pltpu.make_async_copy(source, r[reads[n] + "_here"].at[planes(g)], r["sems"].at[n, g])

        def slot(g):
            return jnp.minimum(g, 1) if self.part == "outer" else lax.rem(g, SLOTS)

        def save(n, g):
            target = r[writes[n]]
            target = target.at[self.place(g)]
            sem = r["sems"].at[len(reads) + n, g]
            return pltpu.make_async_copy(r[writes[n] + "_here"].at[planes(slot(g))], target, sem)

        for g in groups:
            for n in range(len(reads)):
                load(n, g).start()
        if self.fills:
            fill_z(r["kz"], r["reach"][2])
            if "ky" in r:
                fill_y(r["ky"], r["reach"][1], HALO)
            if "ky0" in r:
                fill_y(r["ky0"], 0, 0)
        nx = self.shape[0]
        for swap, name in enumerate(("even", "odd")):
            if "sides" in r:
                r["sides"][edge(0, swap, 2 * HALO)] = r[name][...]
            if "y_ext" in r:
                rows = pl.ds(swap * HALO, HALO)
                r["y_ext"][HALO : HALO + nx, rows] = r["y_" + name][...]
                for n in range(2):
                    corner = r["corner_" + name][n * HALO : (n + 1) * HALO]
                    r["y_ext"][edge(0, n, nx + 2 * HALO), rows] = corner

        def run(i, carry):
            g = groups.start + groups.step * i
            for n in range(len(reads)):
                load(n, g).wait()
            for n in range(len(writes) if len(groups) > SLOTS else 0):
                pl.when(i >= SLOTS)(lambda: save(n, g - SLOTS).wait())
            self.group(dict(r, slot=slot(g)), g)
            for n in range(len(writes)):
                save(n, g).start()
            return carry

        lax.fori_loop(0, len(groups), run, 0)
        self.complete(r, parts, planes)
        if "even_out" in r and self.send in (0, BOTH):
            for swap, name in enumerate(("even_out", "odd_out")):
                r[name][...] = r["u_out"][edge(0, swap, nx)]
        for g in groups[-SLOTS:]:
            for n in range(len(writes)):
                save(n, g).wait()

    def __call__(self, name, **arrays):
        nx, ny, nz = self.shape
        whole = tuple(n * 2 if line == self.cut else n for line, n in enumerate(self.shape))
        outs = {}
        aliases = {}
        if self.kind == "dual":
            outs["d"] = whole
        if self.kind == "part":
            outs.update(send=(*whole[:2], nz // 2), keep=(*whole[:2], nz // 2), t=whole)
        if self.kind == "grad":
            outs["grad"] = whole
        if self.start or self.kind == "none":
            outs["u_out"] = self.shape
        if self.part != "inner":
            if self.send in (0, BOTH):
                outs["even_out"] = outs["odd_out"] = (HALO, ny, nz)
            if self.send == 1:
                outs["even_out"] = outs["odd_out"] = (nx, HALO, nz)
            if self.send == BOTH:
                outs["y_even_out"] = outs["y_odd_out"] = (nx, HALO, nz)
        if self.fills:
            outs.update(self.matrices())
        for n, key in enumerate(arrays):
            if key.endswith("_in"):
                aliases[n] = list(outs).index(key[:-3])
        scratch = self.scratch()
        names = list(arrays) + list(outs) + list(scratch)
        operands, in_specs = [], []
        stage_reads = self.reads()
        for key, value in arrays.items():
            if key in ("weights", "reach"):
                in_specs.append(pl.BlockSpec(memory_space=pltpu.SMEM))
            elif key in INSIDE and key not in stage_reads:
                value = pltpu.with_memory_space_constraint(value, pltpu.VMEM)
                in_specs.append(pl.BlockSpec(memory_space=pltpu.VMEM))
            else:
                in_specs.append(pl.BlockSpec(memory_space=pl.ANY))
            operands.append(value)
        out_shape, out_specs = [], []
        for key, shape in outs.items():
            space = pltpu.VMEM if key in INSIDE and key not in self.writes() else pltpu.HBM
            out_shape.append(space(shape, BF16 if key in MATRICES else F32))
            out_specs.append(pl.BlockSpec(memory_space=space))
        result = pl.pallas_call(
            lambda *refs: self.body(dict(zip(names, refs))),
            name=name,
            out_shape=out_shape,
            in_specs=in_specs,
            out_specs=out_specs,
            input_output_aliases=aliases,
            scratch_shapes=list(scratch.values()),
            compiler_params=pltpu.CompilerParams(vmem_limit_bytes=(14 if "sems" in scratch else 8) * 2**20),
            cost_estimate=COST,
        )(*operands)
        return dict(zip(outs, result))


def fetch_body(source, after, out, sem):
    copy = pltpu.make_async_copy(source, out, sem.at[0])
    copy.start()
    copy.wait()


def fetch(value, after):
    return pl.pallas_call(
        fetch_body,
        name="fetch",
        out_shape=pltpu.VMEM(value.shape, F32),
        in_specs=[pl.BlockSpec(memory_space=pl.ANY)] * 2,
        out_specs=pl.BlockSpec(memory_space=pltpu.VMEM),
        scratch_shapes=[pltpu.SemaphoreType.DMA((1,))],
        compiler_params=pltpu.CompilerParams(vmem_limit_bytes=6 * 2**20),
        cost_estimate=COST,
    )(value, after)


def add_body(keep, arrived, out, here, sems):
    parts = sems.shape[1]
    step = here.shape[0] // parts
    planes = [pl.ds(n * step, step) for n in range(parts)]
    loads = [pltpu.make_async_copy(arrived.at[p], here.at[p], sems.at[0, n]) for n, p in enumerate(planes)]
    saves = [pltpu.make_async_copy(here.at[p], out.at[p], sems.at[1, n]) for n, p in enumerate(planes)]
    for copy in loads:
        copy.start()
    for n, p in enumerate(planes):
        loads[n].wait()
        here[p] = here[p] + keep[p]
        saves[n].start()
    for copy in saves:
        copy.wait()


def add(keep, arrived):
    return pl.pallas_call(
        add_body,
        name="barycenter",
        out_shape=pltpu.HBM(keep.shape, F32),
        in_specs=[pl.BlockSpec(memory_space=pltpu.VMEM), pl.BlockSpec(memory_space=pl.ANY)],
        out_specs=pl.BlockSpec(memory_space=pltpu.HBM),
        scratch_shapes=[pltpu.VMEM(keep.shape, F32), pltpu.SemaphoreType.DMA((2, 16))],
        compiler_params=pltpu.CompilerParams(vmem_limit_bytes=8 * 2**20),
        cost_estimate=COST,
    )(pltpu.with_memory_space_constraint(keep, pltpu.VMEM), arrived)


def neighbours(sizes, line, even, odd):
    made = []
    for first, value in enumerate((even, odd)):
        pairs = [(i, i + 1) for i in range(first, sizes[line] - 1, 2)]
        made.append(lax.ppermute(value, AXES[line], pairs + [(j, i) for i, j in pairs]))
    return made


def corner_body(even, odd, after, *outs):
    ny = even.shape[1]
    for swap, out in enumerate(outs):
        for n, ref in enumerate((even, odd)):
            out[pl.ds(n * HALO, HALO)] = ref[:, edge(1, swap, ny)]


def corners(even, odd, after):
    inside = pl.BlockSpec(memory_space=pltpu.VMEM)
    shape = (2 * HALO, HALO, even.shape[2])
    return pl.pallas_call(
        corner_body,
        name="corners",
        out_shape=[pltpu.VMEM(shape, F32)] * 2,
        in_specs=[inside] * 2 + [pl.BlockSpec(memory_space=pl.ANY)],
        out_specs=[inside] * 2,
        compiler_params=pltpu.CompilerParams(vmem_limit_bytes=4 * 2**20),
        cost_estimate=COST,
    )(*(pltpu.with_memory_space_constraint(v, pltpu.VMEM) for v in (even, odd)), after)


def exchange(sizes, line, made):
    if line != BOTH:
        return dict(zip(EDGES, neighbours(sizes, line, made["even_out"], made["odd_out"])))
    x = neighbours(sizes, 0, made["even_out"], made["odd_out"])
    y = neighbours(sizes, 1, made["y_even_out"], made["y_odd_out"])
    return dict(zip(EDGES, (*x, *y)))


SWAP = [(0, 1), (1, 0)]


class Case:
    def __init__(self, sizes, line, shape):
        self.sizes = sizes
        self.cut = 0 if line == 0 else None
        self.pieces = (0, 1) if line == 0 else (0,)
        self.shape = shape
        self.groups = shape[0] // GROUP
        self.sent, self.begin = ((1, (0, 2)), (0, (1, 2)), (BOTH, (2,)))[line]

    def run(self, matrices, n, name, kind, arrays, fills=False, **form):
        stage = Stage(self.shape, self.cut, n, kind, fills=fills, **form)
        made = stage(f"{name}_{n}", **arrays, **{key: matrices[key] for key in stage.needs()})
        if fills:
            matrices.update({key: made.pop(key) for key in stage.matrices()})
        return made

    def begin_lines(self, matrices, n, name, kind, arrays, fills):
        form = dict(start=self.begin, send=self.sent)
        if self.sent != 0 or self.groups < 3:
            return self.run(matrices, n, name, kind, arrays, fills=fills, **form)
        made = self.run(matrices, n, name + "_outer", kind, arrays, fills=fills, part="outer", **form)
        arrays = dict(arrays, u_out_in=made["u_out"])
        made.update(self.run(matrices, n, name + "_inner", kind, arrays, part="inner", **form))
        return made

    def end_lines(self, matrices, n, name, kind, arrays, u, halos, **form):
        if self.sent == 1:
            return self.run(matrices, n, name, kind, dict(arrays, u=u, **halos), finish=1, **form)
        x_halos = {key: halos.pop(key) for key in ("even", "odd")}
        if self.sent == 0:
            x_name, x_kind, x_form, given = name, kind, form, dict(arrays, u=u)
        else:
            x_name, x_kind, x_form, given = name + "_x", "none", {}, dict(reach=arrays["reach"], u=u)
        whole, part = {}, "all"
        if self.groups > 2:
            made = self.run(matrices, n, x_name + "_inner", x_kind, given, finish=0, part="inner", **x_form)
            whole, part = {key + "_in": made[key] for key in made}, "outer"
        if self.sent == BOTH:
            made = corners(*x_halos.values(), whole.get("u_out_in", u))
            halos.update(zip(EDGES[4:], neighbours(self.sizes, 1, *made)))
        given = dict(given, **whole, **x_halos)
        made = self.run(matrices, n, f"{x_name}_{part}", x_kind, given, finish=0, part=part, **x_form)
        if self.sent == 0:
            return made
        return self.run(matrices, n, name, kind, dict(arrays, u=made["u_out"], **halos), finish=BOTH, **form)

    def scalings(self, inputs, warm, weights, reach):
        matrices = {}
        form = dict(start=self.begin, send=self.sent)
        given = dict(warm=warm, reach=reach)
        made = {n: self.begin_lines(matrices, n, "scaling", "exp", given, n == 0) for n in self.pieces}
        halos = {n: exchange(self.sizes, self.sent, made[n]) for n in made}
        whole = {}
        for n in self.pieces:
            given = dict(inputs=inputs, reach=reach, **whole)
            made[n] = self.end_lines(matrices, n, "dual", "dual", given, made[n]["u_out"], halos[n], **form)
            whole = dict(d_in=made[n]["d"])
        d = whole["d_in"]
        halos = {n: exchange(self.sizes, self.sent, made[n]) for n in made}
        whole = {}
        for n in self.pieces:
            given = dict(warm=warm, weights=weights, reach=reach, **whole)
            part = self.end_lines(matrices, n, "partial", "part", given, made[n]["u_out"], halos[n])
            whole = {key + "_in": part[key] for key in ("send", "keep", "t")}
        return part["send"], part["keep"], part["t"], d

    def gradient(self, weights, reach, cotangent, far, t, d):
        matrices = {}
        given = dict(t=t, weights=weights, far=far, cot=cotangent, reach=reach)
        made = {n: self.begin_lines(matrices, n, "cotangent", "cot", given, n == 0) for n in self.pieces}
        halos = {n: exchange(self.sizes, self.sent, made[n]) for n in made}
        whole = {}
        for n in self.pieces:
            given = dict(d=d, reach=reach, **whole)
            made[n] = self.end_lines(matrices, n, "gradient", "grad", given, made[n]["u_out"], halos[n])
            whole = dict(grad_in=made[n]["grad"])
        return whole["grad_in"]


def per_device(sizes, log_inputs, warm_potential, bary_weights, band_reach, bary_cotangent):
    shape = log_inputs.shape[1:]
    line = jnp.sum(jnp.where(band_reach == 0, jnp.arange(3, dtype=jnp.int32), 0))
    cases = [Case(sizes, n, shape) for n in range(3)]
    inputs, warm = log_inputs.reshape(shape), warm_potential.reshape(shape)
    far = lax.ppermute(bary_cotangent, "inp", SWAP)
    send, keep, t, d = lax.switch(
        line, [case.scalings for case in cases], inputs, warm, bary_weights, band_reach
    )
    arrived = lax.ppermute(send, "inp", SWAP)
    grad = lax.switch(
        line, [case.gradient for case in cases], bary_weights, band_reach, bary_cotangent, far, t, d
    )
    return (add(fetch(keep, grad), arrived), grad[None])


def solution(mesh):
    sizes = (mesh.shape["pa"], mesh.shape["pb"])
    return jax.shard_map(
        functools.partial(per_device, sizes),
        mesh=mesh,
        in_specs=(
            P("inp", "pa", "pb", None),
            P("inp", "pa", "pb", None),
            P("inp"),
            P(),
            P("pa", "pb", "inp"),
        ),
        out_specs=(P("pa", "pb", "inp"), P("inp", "pa", "pb", None)),
        check_vma=False,
    )
```
